512 devices in a mesh: replica: 16 (over x, y_hi), space: 32 (over z, y_lo, core).
Axes of the slice: x: 4, y: 8 (y_hi: 4, y_lo: 2; y = y_hi * 2 + y_lo), z: 8, core: 2. Of those that a mesh axis runs over, the one named last changes fastest.
Arguments:
- particle_coordinates: float32 [16, 3, 8192], P('replica', None, 'space'), may hold values from 0 to 4
- particle_motions: float32 [16, 3, 8192], P('replica', None, 'space'), may hold values from -6 to 6
- particle_kinds: int32 [16, 8192], P('replica', 'space'), may hold values from 0 to 5
- filled_totals: int32 [16, 8192], P('replica', 'space'), may hold values from 1 to 32, as said below
- adjacent_particles: int32 [16, 32, 8192], P('replica', None, 'space'), may hold values from 0 to 511, as said below
- adjacent_place_kinds: int32 [16, 32, 8192], P('replica', None, 'space'), may hold values from 0 to 5
- border_particle_numbers: int32 [16, 4, 2048], P('replica', None, 'space'), may hold values from 0 to 255, as said below
- reciprocal_kind_inertia: float32 [6], replicated, may hold values from 0.1 to 1
- thermal_levels: float32 [16], P('replica'), may hold values from 250 to 600
- swap_mates: int32 [16], P('replica'), may hold values from 0 to 15, as said below
- bond_intake_coefficients: bfloat16 [256, 28], replicated, may hold values from -1 to 1
- bond_output_coefficients: float32 [256], replicated, may hold values from -0.375 to 0.375
- particle_opening_coefficients: bfloat16 [256, 8], replicated, may hold values from -2 to 2
- particle_middle_coefficients: bfloat16 [256, 256], replicated, may hold values from -0.375 to 0.375
- particle_output_coefficients: float32 [256], replicated, may hold values from -0.375 to 0.375
Outputs:
- positions_out: float32 [16, 3, 8192], P('replica', None, 'space')
- velocities_out: float32 [16, 3, 8192], P('replica', None, 'space')
The draws below stay inside these ranges and needn't reach their ends.
Inputs may be any that keep to these rules, and one draw needn't show every extreme that they name: `filled_totals`: each atom's live slots are its first counts slots. `adjacent_particles`: indices into the domain's own 256 atoms followed by its four ghost sets of 64 in the order of offsets +1, -1, +2, -2; an atom's slots are distinct and never the atom itself. `border_particle_numbers`: for each offset and domain, 64 distinct own atoms of that domain. swap_mates[swap_mates[r]] = r and swap_mates[r] - r is -1, 0 or 1; every swapped pair (r, r + 1) of one draw has r of the same parity, and at least one pair swaps.
All inputs are finite; a program needn't handle non-finite values.
Results may differ from the reference program's by a relative error of at most 0.0003.
Values sent between devices are 32-bit elements; how exact they have to be, the bound alone decides.
No kernel may reach another device: no remote copies, remote signals or barrier semaphores. Data moves between devices by JAX's collectives and lax.ppermute only.
A program may use at most 64 MiB of HBM per device.

```python
import math
import jax
import jax.numpy as jnp
from jax import lax

HID = 256
NB = 8
SPECIES = 6
FEAT = 28
ATOMS_DEV = 256
NEIGH = 32
STEPS = 2
GHOST = 64
DOMAINS = 32
LADDER_RUNGS = 16
ATOMS = 8192


def draw_filled_totals(key, part):
    key = jax.random.fold_in(key, 11)
    dense_key, atom_key = jax.random.split(key)
    density = jax.random.randint(dense_key, (LADDER_RUNGS, DOMAINS, 1), 3 * NEIGH // 4, NEIGH + 1)
    raw_bits = jax.random.randint(atom_key, (LADDER_RUNGS, DOMAINS, ATOMS_DEV), 0, 1 << 20)
    result = density - raw_bits % (density // 4 + 1)
    result = result.at[:, 0, 0].set(NEIGH)
    result = result.at[:, 0, 1].set(1)
    return result.reshape(LADDER_RUNGS, DOMAINS * ATOMS_DEV).astype(jnp.int32)


def draw_adjacent_particles(key, part):
    key = jax.random.fold_in(key, 12)
    own_key, ghost_key, kind_key, side_key = jax.random.split(key, 4)
    span_len = ATOMS_DEV + 4 * GHOST
    own_stride = (ATOMS_DEV - 1) // NEIGH
    ghost_stride = GHOST // NEIGH
    shape = (LADDER_RUNGS, NEIGH, DOMAINS, ATOMS_DEV)
    own_jit = jax.random.randint(own_key, shape, 0, own_stride)
    ghost_jit = jax.random.randint(ghost_key, shape, 0, ghost_stride)
    kind_val = jax.random.randint(kind_key, shape, 0, 25)
    side_val = jax.random.randint(side_key, shape, 0, 2)
    centre = jnp.arange(ATOMS_DEV, dtype=jnp.int32)[None, None, None, :]
    slot_idx = jnp.arange(NEIGH, dtype=jnp.int32)[None, :, None, None]
    own_target = (centre + 1 + slot_idx * own_stride + own_jit) % ATOMS_DEV
    ghost_pos = (centre + slot_idx * ghost_stride + ghost_jit) % GHOST
    which_set = jnp.where(kind_val < 23, side_val, 2 + side_val)
    ghost_target = ATOMS_DEV + which_set * GHOST + ghost_pos
    target = jnp.where(kind_val < 17, own_target, ghost_target)
    slot_line = jnp.arange(NEIGH, dtype=jnp.int32)
    target = target.at[:, :, 0, 0].set((span_len - 1 - slot_line)[None, :])
    target = target.at[:, :, 0, 1].set((slot_line * own_stride)[None, :])
    return target.reshape(LADDER_RUNGS, NEIGH, DOMAINS * ATOMS_DEV).astype(jnp.int32)


def draw_border_particle_numbers(key, part):
    key = jax.random.fold_in(key, 13)
    subkeys = jax.random.split(key, LADDER_RUNGS * 4 * DOMAINS)

    def one_set(sub):
        first_key, second_key = jax.random.split(sub)
        middle = 1 + jax.random.permutation(first_key, ATOMS_DEV - 2)
        chosen = jnp.concatenate([jnp.array([ATOMS_DEV - 1, 0], dtype=jnp.int32), middle[:GHOST - 2].astype(jnp.int32)])
        order = jax.random.permutation(second_key, GHOST)
        return chosen[order]
    orders = jax.vmap(one_set)(subkeys)
    return orders.reshape(LADDER_RUNGS, 4, DOMAINS * GHOST).astype(jnp.int32)


def draw_swap_mates(key, part):
    key = jax.random.fold_in(key, 14)
    parity_key, accept_key = jax.random.split(key)
    parity = jax.random.randint(parity_key, (), 0, 2)
    ladder = jnp.arange(LADDER_RUNGS, dtype=jnp.int32)
    shifted = ladder - parity
    pair_idx = jnp.floor_divide(shifted, 2)
    upper_end = parity + 2 * pair_idx + 1
    accept = jax.random.randint(accept_key, (LADDER_RUNGS,), 0, 2)
    taken = accept[jnp.clip(pair_idx, 0, LADDER_RUNGS - 1)]
    moved = jnp.where(jnp.remainder(shifted, 2) == 0, ladder + 1, ladder - 1)
    mid_low = LADDER_RUNGS // 2 - 1
    mid_high = LADDER_RUNGS // 2
    middle_pair = (ladder == mid_low) | (ladder == mid_high) | (moved == mid_low) | (moved == mid_high)
    usable = (shifted >= 0) & (upper_end < LADDER_RUNGS) & ((taken == 1) | (pair_idx == 0) | middle_pair)
    return jnp.where(usable, moved, ladder).astype(jnp.int32)


def set_ends(values, key, least, largest):
    dims = values.shape
    place = [jax.random.randint(jax.random.fold_in(key, axis), (), 0, dims[axis]) for axis in range(len(dims))]
    values = values.at[tuple(place)].set(least)
    longest = dims.index(max(dims))
    place[longest] = (place[longest] + 1) % dims[longest]
    return values.at[tuple(place)].set(largest)


def level_of(rng, shape, shards, low, top_value):
    level = 1.0
    for position, shards_of in shards:
        draws = jax.random.uniform(jax.random.fold_in(jax.random.fold_in(rng, 6), position), (shards_of,), jnp.float32, low / len(shards), top_value / len(shards))
        level = level * jnp.repeat(jnp.exp(draws), shape[position] // shards_of).reshape((-1,) + (1,) * (len(shape) - 1 - position))
    return level


def gaussian(key, dims, width, limit, cuts=(), kind=jnp.bfloat16):
    loudness = level_of(key, dims, cuts, -0.22, 0.18) if cuts else 1.0
    values = jax.random.normal(key, dims, jnp.float32) * width * loudness
    return jnp.minimum(jnp.maximum(values, -limit), limit).astype(kind)


def setup_inputs(seed: int = 0) -> dict:
    splits = jax.random.split(jax.random.key(seed), 16)
    particle_coordinates = jnp.clip(4.0 * jax.random.uniform(splits[0], (LADDER_RUNGS, 3, ATOMS), jnp.float32) ** level_of(splits[0], (LADDER_RUNGS, 3, ATOMS), ((0, 16), (2, 32)), -0.2, 0.2), 0.0, 4.0)
    particle_motions = gaussian(splits[1], (LADDER_RUNGS, 3, ATOMS), 1.0, 6.0, ((0, 16), (2, 32)), jnp.float32)
    particle_kinds = set_ends(jax.random.randint(splits[2], (LADDER_RUNGS, ATOMS), 0, SPECIES), jax.random.fold_in(splits[2], 1), 0, SPECIES - 1).astype(jnp.int32)
    filled_totals = draw_filled_totals(jax.random.fold_in(splits[15], 71), 0)
    adjacent_particles = draw_adjacent_particles(jax.random.fold_in(splits[15], 71), 0)
    adjacent_place_kinds = set_ends(jax.random.randint(splits[5], (LADDER_RUNGS, NEIGH, ATOMS), 0, SPECIES), jax.random.fold_in(splits[5], 1), 0, SPECIES - 1).astype(jnp.int32)
    border_particle_numbers = draw_border_particle_numbers(jax.random.fold_in(splits[15], 71), 0)
    reciprocal_kind_inertia = jnp.clip(jnp.exp(jax.random.uniform(splits[7], (SPECIES,), jnp.float32, math.log(0.1), math.log(1.0))), 0.1, 1.0)
    thermal_levels = jnp.clip(jnp.exp(math.log(600.0) - 0.87546874 * jax.random.uniform(splits[8], (LADDER_RUNGS,), jnp.float32) ** level_of(splits[8], (LADDER_RUNGS,), ((0, 16),), -0.2, 0.2)), 250.0, 600.0)
    swap_mates = draw_swap_mates(jax.random.fold_in(splits[15], 71), 0)
    bond_intake_coefficients = gaussian(splits[10], (HID, FEAT), FEAT ** -0.5, 1.0)
    bond_output_coefficients = gaussian(splits[11], (HID,), HID ** -0.5, 0.375, (), jnp.float32)
    particle_opening_coefficients = gaussian(splits[12], (HID, NB), NB ** -0.5, 2.0)
    particle_middle_coefficients = gaussian(splits[13], (HID, HID), HID ** -0.5, 0.375)
    particle_output_coefficients = gaussian(splits[14], (HID,), HID ** -0.5, 0.375, (), jnp.float32)
    return {"particle_coordinates": particle_coordinates, "particle_motions": particle_motions, "particle_kinds": particle_kinds, "filled_totals": filled_totals, "adjacent_particles": adjacent_particles, "adjacent_place_kinds": adjacent_place_kinds, "border_particle_numbers": border_particle_numbers, "reciprocal_kind_inertia": reciprocal_kind_inertia, "thermal_levels": thermal_levels, "swap_mates": swap_mates, "bond_intake_coefficients": bond_intake_coefficients, "bond_output_coefficients": bond_output_coefficients, "particle_opening_coefficients": particle_opening_coefficients, "particle_middle_coefficients": particle_middle_coefficients, "particle_output_coefficients": particle_output_coefficients}


OFFSETS = (1, -1, 2, -2)
TIME_STEP = 0.05
CUT_SQ = 9.0

def features(edge_vec, live_mask, centre_hot, neigh_hot, n_basis):
    dist_sq = lax.optimization_barrier(jnp.sum(edge_vec * edge_vec, axis=0))
    inside = 1.0 - dist_sq / CUT_SQ
    cutoff = jnp.where(live_mask & (inside > 0.0), inside * inside, 0.0)
    centres = CUT_SQ * jnp.arange(n_basis).astype(jnp.float32) / (n_basis - 1)
    sharpness = (n_basis / CUT_SQ) ** 2
    radial = jnp.exp(-sharpness * (dist_sq[None] - centres[:, None, None]) ** 2) * cutoff[None]
    environ = lax.optimization_barrier(jnp.sum(radial, axis=1))
    slot_len = edge_vec.shape[1]
    inputs = jnp.concatenate([radial, jnp.broadcast_to(environ[:, None, :], radial.shape), jnp.broadcast_to(centre_hot[:, None, :], (centre_hot.shape[0], slot_len, centre_hot.shape[1])), neigh_hot], axis=0)
    return (inputs, cutoff, environ)

def edge_block(inputs, cutoff, bond_intake_coefficients, bond_output_coefficients):
    rounded = inputs.astype(jnp.bfloat16)
    pre_edge = jnp.dot(bond_intake_coefficients, rounded, preferred_element_type=jnp.float32).astype(jnp.bfloat16)
    pre_edge = lax.optimization_barrier(pre_edge)
    pre_wide = pre_edge.astype(jnp.float32)
    sig_pre = jax.nn.sigmoid(pre_wide)
    output = lax.optimization_barrier(jnp.sum(bond_output_coefficients[:, None] * (pre_wide * sig_pre), axis=0))
    slope_pre = sig_pre * (1.0 + pre_wide * (1.0 - sig_pre))
    g_pre = (cutoff[None, :] * bond_output_coefficients[:, None] * slope_pre).astype(jnp.bfloat16)
    g_in = jnp.dot(bond_intake_coefficients.T, g_pre, preferred_element_type=jnp.float32)
    return (g_in, output)

def atom_block(environ, particle_opening_coefficients, particle_middle_coefficients, particle_output_coefficients):
    env_low = environ.astype(jnp.bfloat16)
    first_pre = jnp.dot(particle_opening_coefficients, env_low, preferred_element_type=jnp.float32)
    sig_first = jax.nn.sigmoid(first_pre)
    hidden_one = (first_pre * sig_first).astype(jnp.bfloat16)
    second = jnp.dot(particle_middle_coefficients, hidden_one, preferred_element_type=jnp.float32)
    sig_second = jax.nn.sigmoid(second)
    g_second = (particle_output_coefficients[:, None] * sig_second * (1.0 + second * (1.0 - sig_second))).astype(jnp.bfloat16)
    g_hidden = jnp.dot(particle_middle_coefficients.T, g_second, preferred_element_type=jnp.float32)
    g_first = (g_hidden * sig_first * (1.0 + first_pre * (1.0 - sig_first))).astype(jnp.bfloat16)
    return jnp.dot(particle_opening_coefficients.T, g_first, preferred_element_type=jnp.float32)

def domain_gradient(domain_coordinates_here, ghost_pos, neighbour_idx, atom_counts, own_species, neigh_spec, weights):
    bond_intake_coefficients, bond_output_coefficients, particle_opening_coefficients, particle_middle_coefficients, particle_output_coefficients = weights
    n_species = 6
    n_basis = particle_opening_coefficients.shape[1]
    all_pos = jnp.concatenate([domain_coordinates_here, ghost_pos], axis=1)
    slot_len, atom_count = neighbour_idx.shape
    edge_vec = all_pos[:, neighbour_idx] - domain_coordinates_here[:, None, :]
    live_mask = jnp.arange(slot_len)[:, None] < atom_counts[None, :]
    kinds = jnp.arange(n_species, dtype=jnp.int32)
    centre_hot = (own_species[None, :] == kinds[:, None]).astype(jnp.float32)
    neigh_hot = (neigh_spec[None] == kinds[:, None, None]).astype(jnp.float32)
    (inputs, cutoff, environ), pullback = jax.vjp(lambda vecs: features(vecs, live_mask, centre_hot, neigh_hot, n_basis), edge_vec)
    feat_len = inputs.shape[0]
    g_in, output = edge_block(inputs.reshape(feat_len, slot_len * atom_count), cutoff.reshape(slot_len * atom_count), bond_intake_coefficients, bond_output_coefficients)
    g_env = atom_block(environ, particle_opening_coefficients, particle_middle_coefficients, particle_output_coefficients)
    g_vec, = pullback((g_in.reshape(feat_len, slot_len, atom_count), output.reshape(slot_len, atom_count), g_env))
    g_all = jnp.zeros_like(all_pos).at[:, neighbour_idx].add(g_vec)
    return g_all.at[:, :atom_count].add(-lax.optimization_barrier(jnp.sum(g_vec, axis=1)))

def reference(particle_coordinates, particle_motions, particle_kinds, filled_totals, adjacent_particles, adjacent_place_kinds, border_particle_numbers, reciprocal_kind_inertia, thermal_levels, swap_mates, bond_intake_coefficients, bond_output_coefficients, particle_opening_coefficients, particle_middle_coefficients, particle_output_coefficients):
    weights = (bond_intake_coefficients, bond_output_coefficients, particle_opening_coefficients, particle_middle_coefficients, particle_output_coefficients)
    domain_len = DOMAINS
    atom_count = ATOMS_DEV
    ghost_len = GHOST

    def replica_run(pieces):
        coords, speeds, own_species, atom_counts, neighbour_idx, neigh_spec, ghost_idx = pieces
        spec_dom = own_species.reshape(domain_len, atom_count)
        count_dom = atom_counts.reshape(domain_len, atom_count)
        neigh_dom = neighbour_idx.reshape(NEIGH, domain_len, atom_count).transpose(1, 0, 2)
        nspec_dom = neigh_spec.reshape(NEIGH, domain_len, atom_count).transpose(1, 0, 2)
        ghost_dom = ghost_idx.reshape(4, domain_len, ghost_len).transpose(1, 0, 2)
        kinds = jnp.arange(reciprocal_kind_inertia.shape[0], dtype=jnp.int32)
        inverse = lax.optimization_barrier(jnp.sum((own_species[None, :] == kinds[:, None]).astype(jnp.float32) * reciprocal_kind_inertia[:, None], axis=0))
        for step_no in range(STEPS):
            domain_pos = coords.reshape(3, domain_len, atom_count).transpose(1, 0, 2)
            outgoing = jax.vmap(lambda pos_one, map_one: pos_one[:, map_one])(domain_pos, ghost_dom)
            received = [jnp.roll(outgoing[:, :, which], OFFSETS[which], axis=0) for which in range(4)]
            ghosts = jnp.concatenate(received, axis=2)

            def one_domain(items):
                return domain_gradient(items[0], items[1], items[2], items[3], items[4], items[5], weights)
            g_every = lax.map(one_domain, (domain_pos, ghosts, neigh_dom, count_dom, spec_dom, nspec_dom))
            g_own = g_every[:, :, :atom_count]
            for which in range(4):
                start = atom_count + which * ghost_len
                returned = jnp.roll(g_every[:, :, start:start + ghost_len], -OFFSETS[which], axis=0)
                g_own = jax.vmap(lambda grad_one, map_one, back_one: grad_one.at[:, map_one].add(back_one))(g_own, ghost_dom[:, which], returned)
            grad = g_own.transpose(1, 0, 2).reshape(3, domain_len * atom_count)
            speeds = speeds - TIME_STEP * grad * inverse[None, :]
            coords = coords + TIME_STEP * speeds
        return (coords, speeds)
    coords_all, speeds_all = lax.map(replica_run, (particle_coordinates, particle_motions, particle_kinds, filled_totals, adjacent_particles, adjacent_place_kinds, border_particle_numbers))
    motion_rescaling = jnp.sqrt(thermal_levels / thermal_levels[swap_mates])
    return (coords_all[swap_mates], speeds_all[swap_mates] * motion_rescaling[:, None, None])
```

```python
import functools

import jax
import jax.numpy as jnp
from jax import lax
from jax.experimental import pallas as pl
from jax.experimental.pallas import tpu as pltpu
from jax.sharding import PartitionSpec as P

STEPS = 2
TIME_STEP = 0.05
CUT_SQ = 9.0
N_BASIS = 8
N_KIND = 6
LANES = 128
SLOTS = 32
GROUPS = SLOTS // 8
HIDDEN = 256
SHARP = (N_BASIS / CUT_SQ) ** 2
CENTRES = [CUT_SQ * c / (N_BASIS - 1) for c in range(N_BASIS)]
F32 = jnp.float32
BF16 = jnp.bfloat16


def nt_dot(a, b):
    return lax.dot_general(a, b, (((1,), (1,)), ((), ())), preferred_element_type=F32)


def tn_dot(a, b):
    return lax.dot_general(a, b, (((0,), (0,)), ((), ())), preferred_element_type=F32)


def nn_dot(a, b):
    return lax.dot_general(a, b, (((1,), (0,)), ((), ())), preferred_element_type=F32)


def as_tile(wide):
    pad = jnp.zeros((2, LANES), wide.dtype)
    return jnp.concatenate([wide[:, :LANES], wide[:, LANES:], pad], axis=0)


def rows_of_two(first, second, pad_with=None):
    shape = (3, LANES)
    pad = jnp.zeros((2, LANES), first.dtype)
    return jnp.concatenate(
        [jnp.broadcast_to(first, shape), jnp.broadcast_to(second, shape), pad], axis=0
    )


def take_lanes(table, lane):
    return jnp.take_along_axis(table, lane, axis=1, mode="promise_in_bounds")


def border_positions(tile, border0, border1):
    index = rows_of_two(border0, border1)
    pad = jnp.zeros((2, LANES), F32)
    low = jnp.concatenate([tile[0:3], tile[0:3], pad], axis=0)
    high = jnp.concatenate([tile[3:6], tile[3:6], pad], axis=0)
    lane = index & (LANES - 1)
    return jnp.where(index < LANES, take_lanes(low, lane), take_lanes(high, lane))


def four_sets(set0, set1, set2, set3):
    row = lax.broadcasted_iota(jnp.int32, (8, LANES), 0)
    col = lax.broadcasted_iota(jnp.int32, (8, LANES), 1)
    left = col < LANES // 2
    return jnp.where(row < 3, jnp.where(left, set0, set1), jnp.where(left, set2, set3))


def split_parts(value, count):
    parts = []
    for _ in range(count):
        part = value.astype(BF16).astype(F32)
        parts.append(part)
        value = value - part
    return parts


def start_kernel(x_ref, v_ref, kind_ref, border_ref, inertia_ref, out_ref):
    x_tile = as_tile(x_ref[0])
    border = border_ref[0]
    border0 = jnp.concatenate([border[0:1], border[1:2]], axis=1)
    border1 = jnp.concatenate([border[2:3], border[3:4]], axis=1)
    kind = kind_ref[...]
    inverse = jnp.zeros(kind.shape, F32)
    for k in range(N_KIND):
        inverse = jnp.where(kind == k, inertia_ref[k], inverse)
    out_ref[0:8] = border_positions(x_tile, border0, border1)
    out_ref[8:14] = x_tile[0:6]
    out_ref[14:15] = inverse[:, :LANES]
    out_ref[15:16] = inverse[:, LANES:]
    out_ref[16:22] = as_tile(v_ref[0])[0:6]
    out_ref[22:23] = border0.astype(F32)
    out_ref[23:24] = border1.astype(F32)


def chosen_columns(slot, count):
    feature = lax.broadcasted_iota(jnp.int32, (28, count), 0)
    col = lax.broadcasted_iota(jnp.int32, (28, count), 1)
    block, which = col // 8, col % 8
    radial = (block < 8) & (which == slot) & (feature == block)
    environ = (block == 8) & (feature == 8 + which)
    centre = (block == 9) & (which < N_KIND) & (feature == 16 + which)
    neigh = (block >= 10) & (which == slot) & (feature == 22 + block - 10)
    return (radial | environ | centre | neigh).astype(F32)


def force_kernel(
    core_ref,
    state_ref,
    near_ref,
    far_ref,
    index_ref,
    place_kind_ref,
    total_ref,
    kind_ref,
    intake_ref,
    edge_out_ref,
    opening_ref,
    middle_ref,
    atom_out_ref,
    out_ref,
    feat_ref,
    gauss_ref,
    geo_ref,
    intake_up,
    intake_down,
    edge_w,
    energy_ref,
    gin_ref,
    scat0_ref,
    scat1_ref,
):
    core = core_ref[0]
    first_core = core == 0
    own = state_ref[core]
    minus2, minus1 = far_ref[0, 0, 0], far_ref[0, 0, 1]
    plus2, plus3 = far_ref[1, 1, 0], far_ref[1, 1, 1]
    near0, near1 = near_ref[0], near_ref[1]

    def pick(a, b):
        return jnp.where(first_core, a, b)

    ghost = four_sets(
        pick(minus1, near0), pick(near1, plus2), pick(minus2, minus1), pick(plus2, plus3)
    )

    intake = intake_ref[...]
    for j in range(8):
        up = (0.5 * chosen_columns(j, 128)).astype(BF16)
        intake_up[j * HIDDEN : (j + 1) * HIDDEN, :] = nn_dot(intake, up).astype(BF16)
        down = chosen_columns(j, 128).astype(BF16)
        intake_down[:, j * HIDDEN : (j + 1) * HIDDEN] = lax.dot_general(
            down, intake, (((0,), (1,)), ((), ())), preferred_element_type=F32
        )[0:80].astype(BF16)
    edge_w[...] = jnp.transpose(jnp.broadcast_to(0.5 * edge_out_ref[...], (LANES, HIDDEN)))

    kind = kind_ref[...]
    kind_rows = lax.broadcasted_iota(jnp.int32, (8, 2 * LANES), 0)
    centre_hot = (kind_rows == kind).astype(F32)
    slot_row = lax.broadcasted_iota(jnp.int32, (8, LANES), 0)
    environ_sum = [[None] * N_BASIS for _ in range(2)]
    for s in range(GROUPS):
        for h in range(2):
            cols = slice(h * LANES, (h + 1) * LANES)
            index = index_ref[0, s * 8 : s * 8 + 8, cols]
            lane = index & (LANES - 1)
            chunk = index // LANES
            dist_sq = None
            for comp in range(3):
                found = None
                for which in range(4):
                    table = own if which < 2 else ghost
                    row = (which % 2) * 3 + comp
                    values = take_lanes(
                        jnp.broadcast_to(table[row : row + 1], (8, LANES)), lane
                    )
                    found = values if which == 0 else jnp.where(chunk == which, values, found)
                vec = found - own[h * 3 + comp : h * 3 + comp + 1]
                geo_ref[comp, s, :, cols] = vec
                dist_sq = vec * vec if comp == 0 else dist_sq + vec * vec
            live = slot_row + s * 8 < total_ref[:, cols]
            inside = 1.0 - dist_sq / CUT_SQ
            used = live & (inside > 0.0)
            cutoff = jnp.where(used, inside * inside, 0.0)
            geo_ref[3, s, :, cols] = dist_sq
            geo_ref[4, s, :, cols] = cutoff
            geo_ref[5, s, :, cols] = jnp.where(used, inside * (-2.0 / CUT_SQ), 0.0)
            for c in range(N_BASIS):
                gap = dist_sq - CENTRES[c]
                gauss = jnp.exp(-SHARP * (gap * gap))
                gauss_ref[s, c * 8 : c * 8 + 8, cols] = gauss
                radial = gauss * cutoff
                sofar = environ_sum[h][c]
                environ_sum[h][c] = radial if sofar is None else sofar + radial
    environ = jnp.concatenate(
        [
            jnp.concatenate(
                [jnp.sum(environ_sum[h][c], axis=0, keepdims=True) for c in range(N_BASIS)], axis=0
            )
            for h in range(2)
        ],
        axis=1,
    )
    for s in range(GROUPS):
        place_kind = place_kind_ref[0, s * 8 : s * 8 + 8, :]
        cutoff = geo_ref[4, s]
        parts = [gauss_ref[s, c * 8 : c * 8 + 8, :] * cutoff for c in range(N_BASIS)]
        parts += [environ, centre_hot]
        parts += [(place_kind == k).astype(F32) for k in range(N_KIND)]
        feat_ref[s] = jnp.concatenate(parts, axis=0).astype(BF16)

    env_low = environ.astype(BF16)
    opening = opening_ref[...]
    middle = middle_ref[...]
    atom_w = jnp.transpose(jnp.broadcast_to(atom_out_ref[...], (LANES, HIDDEN)))
    atom_w = jnp.concatenate([atom_w, atom_w], axis=1)
    first = nn_dot(opening, env_low)
    sig_first = jax.nn.sigmoid(first)
    hidden_one = (first * sig_first).astype(BF16)
    second = nn_dot(middle, hidden_one)
    sig_second = jax.nn.sigmoid(second)
    g_second = (atom_w * sig_second * (1.0 + second * (1.0 - sig_second))).astype(BF16)
    g_hidden = tn_dot(middle, g_second)
    g_first = (g_hidden * sig_first * (1.0 + first * (1.0 - sig_first))).astype(BF16)
    g_env = tn_dot(opening, g_first)

    def group(s, g_env):
        feat = feat_ref[s]
        g_group = None
        for j in range(8):
            pre = nn_dot(intake_up[j * HIDDEN : (j + 1) * HIDDEN, :], feat)
            cut = geo_ref[4, s, j : j + 1, :]
            energy = None
            g_parts = []
            for b in range(HIDDEN // 16):
                rows = slice(b * 16, b * 16 + 16)
                half = pre[rows].astype(BF16).astype(F32)
                w = edge_w[rows, :]
                w = jnp.concatenate([w, w], axis=1)
                th = jnp.tanh(half)
                p = w * (th + 1.0)
                e = half * p
                g = (p + e) - e * th
                energy = e if energy is None else energy + e
                g_parts.append((g * cut).astype(BF16))
            energy_ref[s, j : j + 1, :] = 2.0 * jnp.sum(energy, axis=0, keepdims=True)
            g_pre = jnp.concatenate(g_parts, axis=0)
            part = nn_dot(intake_down[:, j * HIDDEN : (j + 1) * HIDDEN], g_pre)
            g_group = part if g_group is None else g_group + part
        gin_ref[s] = g_group[0:64]
        return g_env + g_group[64:72]

    g_env = lax.fori_loop(0, GROUPS, group, g_env)

    own_sum = [[None] * 3 for _ in range(2)]
    for s in range(GROUPS):
        for h in range(2):
            cols = slice(h * LANES, (h + 1) * LANES)
            dist_sq, cutoff, slope = (geo_ref[k, s, :, cols] for k in (3, 4, 5))
            g_cut = energy_ref[s, :, cols]
            g_gap = None
            for c in range(N_BASIS):
                g_radial = gin_ref[s, c * 8 : c * 8 + 8, cols] + g_env[c : c + 1, cols]
                q = g_radial * gauss_ref[s, c * 8 : c * 8 + 8, cols]
                g_cut = g_cut + q
                moment = q * (dist_sq - CENTRES[c])
                g_gap = moment if g_gap is None else g_gap + moment
            g_dist = (-4.0 * SHARP) * (cutoff * g_gap) + 2.0 * (g_cut * slope)
            chunk = index_ref[0, s * 8 : s * 8 + 8, cols] // LANES
            scat = (scat0_ref, scat1_ref)[h]
            for comp in range(3):
                g_vec = g_dist * geo_ref[comp, s, :, cols]
                sofar = own_sum[h][comp]
                own_sum[h][comp] = g_vec if sofar is None else sofar + g_vec
                for part, value in enumerate(split_parts(g_vec, 2)):
                    for which in range(4):
                        row = s * 8 * 24 + part * 12 + which * 3 + comp
                        scat[pl.ds(row, 8, stride=24), :] = jnp.where(chunk == which, value, 0.0)
    place = lax.broadcasted_iota(jnp.int32, (LANES, 2 * LANES), 0)
    total = None
    for s in range(GROUPS):
        lhs, rhs = [], []
        for j in range(8):
            slot = s * 8 + j
            block = jnp.concatenate(
                [scat0_ref[slot * 24 : slot * 24 + 24, :], scat1_ref[slot * 24 : slot * 24 + 24, :]],
                axis=1,
            )
            lhs.append(block.astype(BF16))
            lane = index_ref[0, slot : slot + 1, :] & (LANES - 1)
            rhs.append((place == lane).astype(F32).astype(BF16))
        part = nt_dot(jnp.concatenate(lhs, axis=1), jnp.concatenate(rhs, axis=1))
        total = part if total is None else total + part
    total = total[0:12] + total[12:24]
    centre = jnp.concatenate(
        [jnp.sum(own_sum[h][comp], axis=0, keepdims=True) for h in range(2) for comp in range(3)],
        axis=0,
    )
    pad = jnp.zeros((2, LANES), F32)
    out_ref[0:8] = jnp.concatenate([total[6:12], pad], axis=0)
    out_ref[8:16] = jnp.concatenate([total[0:6] - centre, pad], axis=0)


def returned_sum(returned, border0, border1):
    row = lax.broadcasted_iota(jnp.int32, (8, LANES), 0)
    place = lax.broadcasted_iota(jnp.int32, (LANES, LANES), 0)
    lhs, rhs = [], []
    for which, border in enumerate((border0, border1)):
        three = returned[which * 3 : which * 3 + 3]
        twice = jnp.concatenate([three, three, jnp.zeros((2, LANES), F32)], axis=0)
        meant = (border // LANES == 1) == (row >= 3)
        kept = jnp.where(meant, twice, 0.0)
        lhs.append(jnp.concatenate(split_parts(kept, 3), axis=0).astype(BF16))
        rhs.append((place == (border & (LANES - 1))).astype(F32).astype(BF16))
    total = nt_dot(jnp.concatenate(lhs, axis=1), jnp.concatenate(rhs, axis=1))
    return total[0:8] + total[8:16] + total[16:24]


def moved(state_ref, near_ref, far_ref):
    minus2, minus1 = far_ref[0, 0, 0], far_ref[0, 0, 1]
    plus2, plus3 = far_ref[1, 1, 0], far_ref[1, 1, 1]
    near0, near1 = near_ref[0, 0:8], near_ref[1, 0:8]
    sets = ((near1, minus1, plus2, minus2), (plus2, near0, plus3, minus1))
    result = []
    for domain in range(2):
        state = state_ref[domain]
        border0 = state[14:15].astype(jnp.int32)
        border1 = state[15:16].astype(jnp.int32)
        inverse = rows_of_two(state[6:7], state[7:8])
        grad = near_ref[domain, 8:16] + returned_sum(four_sets(*sets[domain]), border0, border1)
        speed = state[8:16] - TIME_STEP * grad * inverse
        place = state[0:8] + TIME_STEP * speed
        result.append((place, speed, border0, border1))
    return result


def step_kernel(state_ref, near_ref, far_ref, send_ref, next_ref):
    for domain, (place, speed, border0, border1) in enumerate(moved(state_ref, near_ref, far_ref)):
        send_ref[domain] = border_positions(place, border0, border1)
        next_ref[domain, 0:6] = place[0:6]
        next_ref[domain, 6:8] = state_ref[domain, 6:8]
        next_ref[domain, 8:14] = speed[0:6]
        next_ref[domain, 14:16] = state_ref[domain, 14:16]


def last_kernel(level_ref, state_ref, near_ref, far_ref, next_ref):
    for domain, (place, speed, _, _) in enumerate(moved(state_ref, near_ref, far_ref)):
        next_ref[domain, 0:6] = place[0:6]
        next_ref[domain, 6:8] = jnp.full((2, LANES), level_ref[0], F32)
        next_ref[domain, 8:16] = speed


def swap_kernel(where_ref, level_ref, own_ref, mate_ref, x_ref, v_ref):
    core, swaps, side, position = (where_ref[k] for k in range(4))
    mine = own_ref[core]
    theirs = mate_ref[side, position, core]
    chosen = jnp.where(swaps == 1, theirs, mine)
    scale = jnp.sqrt(level_ref[0] / chosen[6:7])
    scale = jnp.concatenate([scale, scale], axis=1)
    x_ref[0] = jnp.concatenate([chosen[0:3], chosen[3:6]], axis=1)
    v_ref[0] = jnp.concatenate([chosen[8:11], chosen[11:14]], axis=1) * scale


def vmem():
    return pl.BlockSpec(memory_space=pltpu.VMEM)


def smem():
    return pl.BlockSpec(memory_space=pltpu.SMEM)


def tiles(*shape):
    return jax.ShapeDtypeStruct(shape + (LANES,), F32)


def call(kernel, scalars, arrays, out_shape, scratch=(), limit=48 * 2**20):
    out_specs = [vmem() for _ in out_shape] if isinstance(out_shape, list) else vmem()
    return pl.pallas_call(
        kernel,
        out_shape=out_shape,
        in_specs=[smem()] * len(scalars) + [vmem()] * len(arrays),
        out_specs=out_specs,
        scratch_shapes=list(scratch),
        compiler_params=pltpu.CompilerParams(vmem_limit_bytes=limit),
    )(*scalars, *arrays)


def force_scratch():
    return [
        pltpu.VMEM((GROUPS, 128, 2 * LANES), BF16),
        pltpu.VMEM((GROUPS, 64, 2 * LANES), F32),
        pltpu.VMEM((6, GROUPS, 8, 2 * LANES), F32),
        pltpu.VMEM((8 * HIDDEN, 128), BF16),
        pltpu.VMEM((80, 8 * HIDDEN), BF16),
        pltpu.VMEM((HIDDEN, LANES), F32),
        pltpu.VMEM((GROUPS, 8, 2 * LANES), F32),
        pltpu.VMEM((GROUPS, 64, 2 * LANES), F32),
        pltpu.VMEM((SLOTS * 24, LANES), F32),
        pltpu.VMEM((SLOTS * 24, LANES), F32),
    ]


def on_chip(value, domains):
    groups = [[2 * i, 2 * i + 1] for i in range(domains // 2)]
    return lax.all_gather(value, "space", axis_index_groups=groups)


def across_chips(value, domains):
    groups = [[(2 * i - 1) % domains, 2 * i] for i in range(domains // 2)]
    return lax.all_gather(value, "space", axis_index_groups=groups)


def along_ladder(value, rungs, domains):
    groups = []
    for domain in range(domains):
        shift = domain % 2
        for low in range(shift, rungs, 2):
            high = (low + 1) % rungs
            groups.append([low * domains + domain, high * domains + domain])
    return lax.all_gather(value, ("replica", "space"), axis_index_groups=groups)


def on_device(
    particle_coordinates,
    particle_motions,
    particle_kinds,
    filled_totals,
    adjacent_particles,
    adjacent_place_kinds,
    border_particle_numbers,
    reciprocal_kind_inertia,
    thermal_levels,
    swap_mates,
    bond_intake_coefficients,
    bond_output_coefficients,
    particle_opening_coefficients,
    particle_middle_coefficients,
    particle_output_coefficients,
):
    domains, rungs = lax.axis_size("space"), lax.axis_size("replica")
    core = lax.axis_index("space") % 2
    rank = lax.axis_index("replica")
    mate = swap_mates[0]
    odd = rank % 2
    side = jnp.where((mate > rank) == (odd == 0), 0, 1)
    position = jnp.where(side == 0, 1 - odd, odd)
    where_to = jnp.stack([core, (mate != rank).astype(jnp.int32), side, position]).astype(jnp.int32)

    begin = pl.pallas_call(
        start_kernel,
        out_shape=tiles(24),
        in_specs=[vmem()] * 4 + [smem()],
        out_specs=vmem(),
    )(
        particle_coordinates,
        particle_motions,
        particle_kinds,
        border_particle_numbers,
        reciprocal_kind_inertia,
    )
    both = on_chip(begin, domains)
    send, state = both[:, 0:8], both[:, 8:24]
    for step in range(STEPS):
        far = on_chip(across_chips(send, domains), domains)
        partial = call(
            force_kernel,
            (where_to,),
            (
                state,
                send,
                far,
                adjacent_particles,
                adjacent_place_kinds,
                filled_totals,
                particle_kinds,
                bond_intake_coefficients,
                bond_output_coefficients[None],
                particle_opening_coefficients,
                particle_middle_coefficients,
                particle_output_coefficients[None],
            ),
            tiles(16),
            force_scratch(),
        )
        near = on_chip(partial, domains)
        far = on_chip(across_chips(near[:, 0:8], domains), domains)
        if step < STEPS - 1:
            send, state = call(
                step_kernel, (), (state, near, far), [tiles(2, 8), tiles(2, 16)]
            )
        else:
            state = call(last_kernel, (thermal_levels,), (state, near, far), tiles(2, 16))
    mates = on_chip(along_ladder(state, rungs, domains), domains)
    out = jax.ShapeDtypeStruct(particle_coordinates.shape, F32)
    new_x, new_v = call(
        swap_kernel, (where_to, thermal_levels), (state, mates), [out, out]
    )
    return new_x, new_v


def solution(mesh):
    return jax.shard_map(
        on_device,
        mesh=mesh,
        in_specs=(
            P("replica", None, "space"),
            P("replica", None, "space"),
            P("replica", "space"),
            P("replica", "space"),
            P("replica", None, "space"),
            P("replica", None, "space"),
            P("replica", None, "space"),
            P(),
            P("replica"),
            P("replica"),
            P(),
            P(),
            P(),
            P(),
            P(),
        ),
        out_specs=(P("replica", None, "space"), P("replica", None, "space")),
        check_vma=False,
    )
```

```python
import functools

import jax
import jax.numpy as jnp
from jax import lax
from jax.experimental import pallas as pl
from jax.experimental.pallas import tpu as pltpu
from jax.sharding import PartitionSpec as P

STEPS = 2
TIME_STEP = 0.05
CUT_SQ = 9.0
N_BASIS = 8
N_KIND = 6
LANES = 128
SLOTS = 32
GROUPS = SLOTS // 8
HIDDEN = 256
AHEAD = 3
SHARP = (N_BASIS / CUT_SQ) ** 2
CENTRES = [CUT_SQ * c / (N_BASIS - 1) for c in range(N_BASIS)]
F32 = jnp.float32
BF16 = jnp.bfloat16


def nt_dot(a, b):
    return lax.dot_general(a, b, (((1,), (1,)), ((), ())), preferred_element_type=F32)


def tn_dot(a, b):
    return lax.dot_general(a, b, (((0,), (0,)), ((), ())), preferred_element_type=F32)


def nn_dot(a, b):
    return lax.dot_general(a, b, (((1,), (0,)), ((), ())), preferred_element_type=F32)


def tile_of(flat_ref):
    rows = [
        flat_ref[:, (comp * 2 + chunk) * LANES : (comp * 2 + chunk + 1) * LANES]
        for chunk in range(2)
        for comp in range(3)
    ]
    return jnp.concatenate(rows, axis=0)


def put_flat(flat_ref, tile):
    for chunk in range(2):
        for comp in range(3):
            start = (comp * 2 + chunk) * LANES
            row = chunk * 3 + comp
            flat_ref[:, start : start + LANES] = tile[row : row + 1]


def rows_of_two(first, second, pad_with=None):
    shape = (3, LANES)
    pad = jnp.zeros((2, LANES), first.dtype)
    return jnp.concatenate(
        [jnp.broadcast_to(first, shape), jnp.broadcast_to(second, shape), pad], axis=0
    )


def take_lanes(table, lane):
    return jnp.take_along_axis(table, lane, axis=1, mode="promise_in_bounds")


def border_positions(tile, border0, border1):
    index = rows_of_two(border0, border1)
    pad = jnp.zeros((2, LANES), F32)
    low = jnp.concatenate([tile[0:3], tile[0:3], pad], axis=0)
    high = jnp.concatenate([tile[3:6], tile[3:6], pad], axis=0)
    lane = index & (LANES - 1)
    return jnp.where(index < LANES, take_lanes(low, lane), take_lanes(high, lane))


def four_sets(set0, set1, set2, set3):
    row = lax.broadcasted_iota(jnp.int32, (8, LANES), 0)
    col = lax.broadcasted_iota(jnp.int32, (8, LANES), 1)
    left = col < LANES // 2
    return jnp.where(row < 3, jnp.where(left, set0, set1), jnp.where(left, set2, set3))


def split_parts(value, count):
    parts = []
    for _ in range(count):
        part = value.astype(BF16).astype(F32)
        parts.append(part)
        value = value - part
    return parts


def start_kernel(x_ref, v_ref, kind_ref, border_ref, inertia_ref, out_ref):
    x_tile = tile_of(x_ref)
    border = border_ref[0]
    border0 = jnp.concatenate([border[0:1], border[1:2]], axis=1)
    border1 = jnp.concatenate([border[2:3], border[3:4]], axis=1)
    kind = kind_ref[...]
    inverse = jnp.zeros(kind.shape, F32)
    for k in range(N_KIND):
        inverse = jnp.where(kind == k, inertia_ref[k], inverse)
    out_ref[0:8] = border_positions(x_tile, border0, border1)
    out_ref[8:14] = x_tile
    out_ref[14:15] = inverse[:, :LANES]
    out_ref[15:16] = inverse[:, LANES:]
    out_ref[16:22] = tile_of(v_ref)
    out_ref[22:23] = border0.astype(F32)
    out_ref[23:24] = border1.astype(F32)


def fed_columns():
    feature = lax.broadcasted_iota(jnp.int32, (28, LANES), 0)
    col = lax.broadcasted_iota(jnp.int32, (28, LANES), 1)
    block, which = col // 8, col % 8
    radial = (block < 8) & (feature == block)
    environ = (block == 8) & (feature == 8 + which)
    centre = (block == 9) & (which < N_KIND) & (feature == 16 + which)
    neigh = (block >= 10) & (feature == 22 + block - 10)
    return (radial | environ | centre | neigh).astype(F32)


def own_columns(slot, rows):
    col = lax.broadcasted_iota(jnp.int32, (rows, LANES), 1)
    return (col // 8 == 8) | (col // 8 == 9) | (col % 8 == slot)


def two_parts(value):
    high, low = split_parts(value, 2)
    return jnp.concatenate([high, low], axis=0).astype(BF16)


def weight_kernel(
    index_ref, intake_ref, edge_out_ref, opening_ref, middle_ref, atom_out_ref,
    up_ref, down_ref, line_ref, flat_ref, sum_ref, hot_ref, atom_ref, first_ref, second_ref, back_ref,
):
    intake = intake_ref[...]
    fed = fed_columns()
    for j in range(8):
        up = jnp.where(own_columns(j, 28), 0.5 * fed, 0.0).astype(BF16)
        up_ref[j * HIDDEN : (j + 1) * HIDDEN, :] = tn_dot(intake, up).astype(BF16)
    edge_w = edge_out_ref[...]
    weighted = intake.astype(F32) * (0.5 * edge_w)
    down_ref[...] = two_parts(weighted[0:16])
    line = jnp.sum(weighted, axis=1, keepdims=True)
    flat_ref[...] = jnp.broadcast_to(line[0:16], (16, LANES))
    line = jnp.sum(fed * line, axis=0, keepdims=True)
    slot = lax.broadcasted_iota(jnp.int32, (8, LANES), 0)
    line_ref[...] = two_parts(jnp.where(own_columns(slot, 8), line, 0.0))
    wide = jnp.transpose(jnp.broadcast_to(edge_w, (LANES, HIDDEN)))
    sum_ref[...] = jnp.concatenate([wide, wide], axis=1).astype(BF16)
    atom_ref[...] = jnp.transpose(jnp.broadcast_to(0.5 * atom_out_ref[...], (LANES, HIDDEN)))
    first_ref[...] = jnp.transpose((0.5 * opening_ref[...]).astype(F32)).astype(BF16)
    second_ref[...] = 0.5 * middle_ref[...]
    back_ref[...] = jnp.transpose(middle_ref[...].astype(F32)).astype(BF16)
    place = lax.broadcasted_iota(jnp.int32, (LANES, 2 * LANES), 0)

    def group(s, carry):
        for j in range(8):
            lane = index_ref[0, pl.ds(s * 8 + j, 1), :] & (LANES - 1)
            hot_ref[:, pl.ds(pl.multiple_of((s * 8 + j) * 256, 256), 256)] = (place == lane).astype(F32).astype(BF16)
        return carry

    lax.fori_loop(0, GROUPS, group, 0)


def far_tiles(far_ref):
    if len(far_ref.shape) == 5:
        return far_ref[0, 0, 0], far_ref[0, 0, 1], far_ref[1, 1, 0], far_ref[1, 1, 1]
    return far_ref[0, 0], far_ref[0, 1], far_ref[1, 0], far_ref[1, 1]


def force_kernel(
    core_ref,
    state_ref,
    near_ref,
    far_ref,
    index_ref,
    place_kind_ref,
    total_ref,
    kind_ref,
    up_ref,
    down_ref,
    line_ref,
    flat_ref,
    sum_ref,
    hot_ref,
    atom_ref,
    first_ref,
    second_ref,
    back_ref,
    opening_ref,
    out_ref,
    feat_ref,
    gauss_ref,
    geo_ref,
    energy_ref,
    gin0_ref,
    gin1_ref,
    scat0_ref,
    scat1_ref,
):
    core = core_ref[0]
    first_core = core == 0
    own = state_ref[core]
    minus2, minus1, plus2, plus3 = far_tiles(far_ref)
    near0, near1 = near_ref[0], near_ref[1]

    def pick(a, b):
        return jnp.where(first_core, a, b)

    ghost = four_sets(
        pick(minus1, near0), pick(near1, plus2), pick(minus2, minus1), pick(plus2, plus3)
    )

    kind_rows = lax.broadcasted_iota(jnp.int32, (8, 2 * LANES), 0)
    centre_hot = (kind_rows == kind_ref[...]).astype(F32)
    slot_row = lax.broadcasted_iota(jnp.int32, (8, LANES), 0)
    tables = [
        [jnp.broadcast_to(t[r * 3 + c : r * 3 + c + 1], (8, LANES)) for c in range(3)]
        for t in (own, ghost)
        for r in range(2)
    ]

    def geometry(s, sums):
        sums = list(sums)
        slots = pl.ds(pl.multiple_of(s * 8, 8), 8)
        radials = [[], []]
        for h in range(2):
            cols = slice(h * LANES, (h + 1) * LANES)
            index = index_ref[0, slots, cols]
            lane = index & (LANES - 1)
            chunk = index // LANES
            dist_sq = None
            for comp in range(3):
                found = take_lanes(tables[0][comp], lane)
                for which in range(1, 4):
                    found = jnp.where(chunk == which, take_lanes(tables[which][comp], lane), found)
                vec = found - tables[h][comp]
                geo_ref[comp, s, :, cols] = vec
                dist_sq = vec * vec if comp == 0 else dist_sq + vec * vec
            live = slot_row + s * 8 < total_ref[:, cols]
            inside = 1.0 - dist_sq * (1.0 / CUT_SQ)
            used = live & (inside > 0.0)
            cutoff = jnp.where(used, inside * inside, 0.0)
            geo_ref[3, s, :, cols] = dist_sq
            geo_ref[4, s, :, cols] = cutoff
            geo_ref[5, s, :, cols] = jnp.where(used, inside * (-2.0 / CUT_SQ), 0.0)
            for c in range(N_BASIS):
                gap = dist_sq - CENTRES[c]
                gauss = jnp.exp(-SHARP * (gap * gap))
                gauss_ref[s, c * 8 : c * 8 + 8, cols] = gauss
                radial = gauss * cutoff
                radials[h].append(radial)
                sums[h * N_BASIS + c] = sums[h * N_BASIS + c] + radial
        place_kind = place_kind_ref[0, slots, :]
        rows = [jnp.concatenate([a, b], axis=1) for a, b in zip(*radials)]
        feat_ref[s, 0:64] = jnp.concatenate(rows, axis=0).astype(BF16)
        rows = [(place_kind == k).astype(F32) for k in range(N_KIND)]
        feat_ref[s, 80:128] = jnp.concatenate(rows, axis=0).astype(BF16)
        return tuple(sums)

    nothing = jnp.zeros((8, LANES), F32)
    sums = lax.fori_loop(0, GROUPS, geometry, (nothing,) * (2 * N_BASIS))
    rows = [jnp.sum(value, axis=0, keepdims=True) for value in sums]
    environ = jnp.concatenate(
        [jnp.concatenate(rows[:N_BASIS], axis=0), jnp.concatenate(rows[N_BASIS:], axis=0)], axis=1
    )
    shared = jnp.concatenate([environ, centre_hot], axis=0).astype(BF16)
    for s in range(GROUPS):
        feat_ref[s, 64:80] = shared

    atom_w = jnp.concatenate([atom_ref[...], atom_ref[...]], axis=1)
    half = nn_dot(first_ref[...], environ.astype(BF16))
    th = jnp.tanh(half)
    hidden_one = (half + half * th).astype(BF16)
    slope_one = 0.5 * (1.0 + th + half * (1.0 - th * th))
    half = nn_dot(second_ref[...], hidden_one)
    th = jnp.tanh(half)
    g_second = (atom_w * (1.0 + th + half * (1.0 - th * th))).astype(BF16)
    g_hidden = nn_dot(back_ref[...], g_second)
    g_first = (g_hidden * slope_one).astype(BF16)
    g_env = nn_dot(opening_ref[...], g_first)

    flat = jnp.concatenate([flat_ref[...], flat_ref[...]], axis=1)
    slot = lax.broadcasted_iota(jnp.int32, (16, HIDDEN), 0)
    quarter = lax.broadcasted_iota(jnp.int32, (16, HIDDEN), 1) // (HIDDEN // 4)
    members = [(slot == quarter + 4 * k).astype(F32).astype(BF16) for k in range(2)]

    def group(s, g_env):
        feat = feat_ref[s]
        line = nn_dot(line_ref[...], feat)
        energy = line[0:8] + line[8:16]
        folded = []

        def forward(j):
            return nn_dot(up_ref[j * HIDDEN : (j + 1) * HIDDEN, :], feat).astype(BF16)

        ahead = [forward(j) for j in range(AHEAD)]
        for j in range(8):
            half = ahead.pop(0)
            if j + AHEAD < 8:
                ahead.append(forward(j + AHEAD))
            th = jnp.tanh(half)
            rest = sum_ref[...] * (half * th)
            rest = rest[: HIDDEN // 2] + rest[HIDDEN // 2 :]
            folded.append(rest[: HIDDEN // 4] + rest[HIDDEN // 4 :])
            slope = th + half * (jnp.asarray(1.0, BF16) - th * th)
            g_in = nn_dot(down_ref[...], slope)
            cut = geo_ref[4, s, j : j + 1, :]
            g_in = (g_in[0:16] + g_in[16:32] + flat) * cut
            rows = pl.ds(s * 64 + j, 8, stride=8)
            gin0_ref[rows, :] = g_in[0:8, :LANES]
            gin1_ref[rows, :] = g_in[0:8, LANES:]
            g_env = g_env + g_in[8:16]
        for k in range(2):
            rest = jnp.concatenate(folded[k * 4 : k * 4 + 4], axis=0)
            energy = energy + nn_dot(members[k], rest)[0:8]
        energy_ref[s] = energy
        return g_env

    g_env = lax.fori_loop(0, GROUPS, group, g_env)

    def backward(s, sums):
        sums = list(sums)
        slots = slice(s * 8, s * 8 + 8)
        for h in range(2):
            cols = slice(h * LANES, (h + 1) * LANES)
            dist_sq, cutoff, slope = (geo_ref[k, s, :, cols] for k in (3, 4, 5))
            g_cut = energy_ref[s, :, cols]
            g_gap = None
            gin = (gin0_ref, gin1_ref)[h]
            for c in range(N_BASIS):
                rows = slice(s * 64 + c * 8, s * 64 + c * 8 + 8)
                g_radial = gin[rows, :] + g_env[c : c + 1, cols]
                q = g_radial * gauss_ref[s, c * 8 : c * 8 + 8, cols]
                g_cut = g_cut + q
                moment = q * (dist_sq - CENTRES[c])
                g_gap = moment if g_gap is None else g_gap + moment
            g_dist = (-4.0 * SHARP) * (cutoff * g_gap) + 2.0 * (g_cut * slope)
            chunk = index_ref[0, slots, cols] // LANES
            scat = (scat0_ref, scat1_ref)[h]
            for comp in range(3):
                g_vec = g_dist * geo_ref[comp, s, :, cols]
                sums[h * 3 + comp] = sums[h * 3 + comp] + g_vec
                for part, value in enumerate(split_parts(g_vec, 2)):
                    for which in range(4):
                        row = s * 8 * 24 + part * 12 + which * 3 + comp
                        scat[pl.ds(row, 8, stride=24), :] = jnp.where(chunk == which, value, 0.0)
        return tuple(sums)

    sums = (nothing,) * 6
    for s in range(GROUPS):
        sums = backward(s, sums)

    lhs = []
    for slot in range(SLOTS):
        rows = slice(slot * 24, slot * 24 + 24)
        lhs.append(jnp.concatenate([scat0_ref[rows, :], scat1_ref[rows, :]], axis=1).astype(BF16))
    total = nt_dot(jnp.concatenate(lhs, axis=1), hot_ref[...])
    total = total[0:12] + total[12:24]
    centre = jnp.concatenate([jnp.sum(value, axis=0, keepdims=True) for value in sums], axis=0)
    pad = jnp.zeros((2, LANES), F32)
    out_ref[0:8] = jnp.concatenate([total[6:12], pad], axis=0)
    out_ref[8:16] = jnp.concatenate([total[0:6] - centre, pad], axis=0)


def returned_sum(returned, border0, border1):
    row = lax.broadcasted_iota(jnp.int32, (8, LANES), 0)
    place = lax.broadcasted_iota(jnp.int32, (LANES, LANES), 0)
    lhs, rhs = [], []
    for which, border in enumerate((border0, border1)):
        three = returned[which * 3 : which * 3 + 3]
        twice = jnp.concatenate([three, three, jnp.zeros((2, LANES), F32)], axis=0)
        meant = (border // LANES == 1) == (row >= 3)
        kept = jnp.where(meant, twice, 0.0)
        lhs.append(jnp.concatenate(split_parts(kept, 3), axis=0).astype(BF16))
        rhs.append((place == (border & (LANES - 1))).astype(F32).astype(BF16))
    total = nt_dot(jnp.concatenate(lhs, axis=1), jnp.concatenate(rhs, axis=1))
    return total[0:8] + total[8:16] + total[16:24]


def moved(state_ref, near_ref, far_ref):
    minus2, minus1, plus2, plus3 = far_tiles(far_ref)
    near0, near1 = near_ref[0, 0:8], near_ref[1, 0:8]
    sets = ((near1, minus1, plus2, minus2), (plus2, near0, plus3, minus1))
    result = []
    for domain in range(2):
        state = state_ref[domain]
        border0 = state[14:15].astype(jnp.int32)
        border1 = state[15:16].astype(jnp.int32)
        inverse = rows_of_two(state[6:7], state[7:8])
        grad = near_ref[domain, 8:16] + returned_sum(four_sets(*sets[domain]), border0, border1)
        speed = state[8:16] - TIME_STEP * grad * inverse
        place = state[0:8] + TIME_STEP * speed
        result.append((place, speed, border0, border1))
    return result


def step_kernel(state_ref, near_ref, far_ref, send_ref, next_ref):
    for domain, (place, speed, border0, border1) in enumerate(moved(state_ref, near_ref, far_ref)):
        send_ref[domain] = border_positions(place, border0, border1)
        next_ref[domain, 0:6] = place[0:6]
        next_ref[domain, 6:8] = state_ref[domain, 6:8]
        next_ref[domain, 8:14] = speed[0:6]
        next_ref[domain, 14:16] = state_ref[domain, 14:16]


def last_kernel(level_ref, state_ref, near_ref, far_ref, next_ref):
    for domain, (place, speed, _, _) in enumerate(moved(state_ref, near_ref, far_ref)):
        next_ref[domain, 0:6] = place[0:6]
        next_ref[domain, 6:8] = jnp.full((2, LANES), level_ref[0], F32)
        next_ref[domain, 8:16] = speed


def swap_kernel(where_ref, level_ref, own_ref, mate_ref, x_ref, v_ref):
    core, swaps, side, position = (where_ref[k] for k in range(4))
    mine = own_ref[core]
    theirs = mate_ref[side, position, core]
    chosen = jnp.where(swaps == 1, theirs, mine)
    scale = jnp.sqrt(level_ref[0] / chosen[6:7])
    put_flat(x_ref, chosen[0:6])
    put_flat(v_ref, chosen[8:14] * scale)


def vmem():
    return pl.BlockSpec(memory_space=pltpu.VMEM)


def smem():
    return pl.BlockSpec(memory_space=pltpu.SMEM)


def tiles(*shape):
    return jax.ShapeDtypeStruct(shape + (LANES,), F32)


def call(kernel, scalars, arrays, out_shape, scratch=(), flops=10**6, limit=24 * 2**20):
    out_specs = [vmem() for _ in out_shape] if isinstance(out_shape, list) else vmem()
    return pl.pallas_call(
        kernel,
        out_shape=out_shape,
        in_specs=[smem()] * len(scalars) + [vmem()] * len(arrays),
        out_specs=out_specs,
        scratch_shapes=list(scratch),
        cost_estimate=pl.CostEstimate(flops=flops, bytes_accessed=10**6, transcendentals=0),
        compiler_params=pltpu.CompilerParams(vmem_limit_bytes=limit),
    )(*scalars, *arrays)


def weight_shapes():
    return [
        jax.ShapeDtypeStruct((8 * HIDDEN, LANES), BF16),
        jax.ShapeDtypeStruct((32, HIDDEN), BF16),
        jax.ShapeDtypeStruct((16, LANES), BF16),
        tiles(16),
        jax.ShapeDtypeStruct((HIDDEN, 2 * LANES), BF16),
        jax.ShapeDtypeStruct((LANES, SLOTS * 2 * LANES), BF16),
        tiles(HIDDEN),
        jax.ShapeDtypeStruct((HIDDEN, N_BASIS), BF16),
        jax.ShapeDtypeStruct((HIDDEN, HIDDEN), BF16),
        jax.ShapeDtypeStruct((HIDDEN, HIDDEN), BF16),
    ]


def force_scratch():
    return [
        pltpu.VMEM((GROUPS, 128, 2 * LANES), BF16),
        pltpu.VMEM((GROUPS, 64, 2 * LANES), F32),
        pltpu.VMEM((6, GROUPS, 8, 2 * LANES), F32),
        pltpu.VMEM((GROUPS, 8, 2 * LANES), F32),
        pltpu.VMEM((GROUPS * 64, LANES), F32),
        pltpu.VMEM((GROUPS * 64, LANES), F32),
        pltpu.VMEM((SLOTS * 24, LANES), F32),
        pltpu.VMEM((SLOTS * 24, LANES), F32),
    ]


def on_chip(value, domains):
    groups = [[2 * i, 2 * i + 1] for i in range(domains // 2)]
    return lax.all_gather(value, "space", axis_index_groups=groups)


def across_chips(value, domains):
    groups = [[(2 * i - 1) % domains, 2 * i] for i in range(domains // 2)]
    return lax.all_gather(value, "space", axis_index_groups=groups)


def partner_across(value, domains):
    pairs = []
    for i in range(domains // 2):
        odd, even = (2 * i - 1) % domains, 2 * i
        pairs += [(odd, even), (even, odd)]
    return lax.ppermute(value, "space", pairs)


def along_ladder(value, rungs, domains):
    groups = []
    for domain in range(domains):
        shift = domain % 2
        for low in range(shift, rungs, 2):
            high = (low + 1) % rungs
            groups.append([low * domains + domain, high * domains + domain])
    return lax.all_gather(value, ("replica", "space"), axis_index_groups=groups)


def on_device(
    particle_coordinates,
    particle_motions,
    particle_kinds,
    filled_totals,
    adjacent_particles,
    adjacent_place_kinds,
    border_particle_numbers,
    reciprocal_kind_inertia,
    thermal_levels,
    swap_mates,
    bond_intake_coefficients,
    bond_output_coefficients,
    particle_opening_coefficients,
    particle_middle_coefficients,
    particle_output_coefficients,
):
    domains, rungs = lax.axis_size("space"), lax.axis_size("replica")
    core = lax.axis_index("space") % 2
    rank = lax.axis_index("replica")
    mate = swap_mates[0]
    odd = rank % 2
    side = jnp.where((mate > rank) == (odd == 0), 0, 1)
    position = jnp.where(side == 0, 1 - odd, odd)
    where_to = jnp.stack([core, (mate != rank).astype(jnp.int32), side, position]).astype(jnp.int32)

    begin = pl.pallas_call(
        start_kernel,
        out_shape=tiles(24),
        in_specs=[vmem()] * 4 + [smem()],
        out_specs=vmem(),
        compiler_params=pltpu.CompilerParams(vmem_limit_bytes=16 * 2**20),
    )(
        particle_coordinates.reshape(1, -1),
        particle_motions.reshape(1, -1),
        particle_kinds,
        border_particle_numbers,
        reciprocal_kind_inertia,
    )
    weights = call(
        weight_kernel,
        (),
        (
            adjacent_particles,
            bond_intake_coefficients.T,
            bond_output_coefficients[None],
            particle_opening_coefficients.T,
            particle_middle_coefficients,
            particle_output_coefficients[None],
        ),
        weight_shapes(),
        flops=10**9,
    )
    both = on_chip(begin, domains)
    send, state = both[:, 0:8], both[:, 8:24]
    for step in range(STEPS):
        if step == 0:
            far = on_chip(partner_across(send, domains), domains)
        else:
            far = on_chip(across_chips(send, domains), domains)
        partial = call(
            force_kernel,
            (where_to,),
            (
                state,
                send,
                far,
                adjacent_particles,
                adjacent_place_kinds,
                filled_totals,
                particle_kinds,
                *weights,
                particle_opening_coefficients.T,
            ),
            tiles(16),
            force_scratch(),
        )
        near = on_chip(partial, domains)
        far = on_chip(across_chips(near[:, 0:8], domains), domains)
        if step < STEPS - 1:
            send, state = call(step_kernel, (), (state, near, far), [tiles(2, 8), tiles(2, 16)])
        else:
            state = call(last_kernel, (thermal_levels,), (state, near, far), tiles(2, 16))
    mates = on_chip(along_ladder(state, rungs, domains), domains)
    shape = particle_coordinates.shape
    out = jax.ShapeDtypeStruct((1, particle_coordinates.size), F32)
    new_x, new_v = call(swap_kernel, (where_to, thermal_levels), (state, mates), [out, out])
    return new_x.reshape(shape), new_v.reshape(shape)


def solution(mesh):
    return jax.shard_map(
        on_device,
        mesh=mesh,
        in_specs=(
            P("replica", None, "space"),
            P("replica", None, "space"),
            P("replica", "space"),
            P("replica", "space"),
            P("replica", None, "space"),
            P("replica", None, "space"),
            P("replica", None, "space"),
            P(),
            P("replica"),
            P("replica"),
            P(),
            P(),
            P(),
            P(),
            P(),
        ),
        out_specs=(P("replica", None, "space"), P("replica", None, "space")),
        check_vma=False,
    )
```

```python
import functools

import jax
import jax.numpy as jnp
from jax import lax
from jax.experimental import pallas as pl
from jax.experimental.pallas import tpu as pltpu
from jax.sharding import PartitionSpec as P

STEPS = 2
TIME_STEP = 0.05
CUT_SQ = 9.0
N_BASIS = 8
N_KIND = 6
LANES = 128
SLOTS = 32
GROUPS = SLOTS // 8
HIDDEN = 256
AHEAD = 3
SHARP = (N_BASIS / CUT_SQ) ** 2
CENTRES = [CUT_SQ * c / (N_BASIS - 1) for c in range(N_BASIS)]
F32 = jnp.float32
BF16 = jnp.bfloat16


def nt_dot(a, b):
    return lax.dot_general(a, b, (((1,), (1,)), ((), ())), preferred_element_type=F32)


def tn_dot(a, b):
    return lax.dot_general(a, b, (((0,), (0,)), ((), ())), preferred_element_type=F32)


def nn_dot(a, b):
    return lax.dot_general(a, b, (((1,), (0,)), ((), ())), preferred_element_type=F32)


def put_flat(flat_ref, tile):
    for chunk in range(2):
        for comp in range(3):
            start = (comp * 2 + chunk) * LANES
            row = chunk * 3 + comp
            flat_ref[:, start : start + LANES] = tile[row : row + 1]


def rows_of_two(first, second, pad_with=None):
    shape = (3, LANES)
    pad = jnp.zeros((2, LANES), first.dtype)
    return jnp.concatenate(
        [jnp.broadcast_to(first, shape), jnp.broadcast_to(second, shape), pad], axis=0
    )


def take_lanes(table, lane):
    return jnp.take_along_axis(table, lane, axis=1, mode="promise_in_bounds")


def border_positions(tile, border0, border1):
    index = rows_of_two(border0, border1)
    pad = jnp.zeros((2, LANES), F32)
    low = jnp.concatenate([tile[0:3], tile[0:3], pad], axis=0)
    high = jnp.concatenate([tile[3:6], tile[3:6], pad], axis=0)
    lane = index & (LANES - 1)
    return jnp.where(index < LANES, take_lanes(low, lane), take_lanes(high, lane))


def four_sets(set0, set1, set2, set3):
    row = lax.broadcasted_iota(jnp.int32, (8, LANES), 0)
    col = lax.broadcasted_iota(jnp.int32, (8, LANES), 1)
    left = col < LANES // 2
    return jnp.where(row < 3, jnp.where(left, set0, set1), jnp.where(left, set2, set3))


def split_parts(value, count):
    parts = []
    for _ in range(count):
        part = value.astype(BF16).astype(F32)
        parts.append(part)
        value = value - part
    return parts


def bring(sources, targets, sems):
    copies = [
        pltpu.make_async_copy(source, target, sems.at[k])
        for k, (source, target) in enumerate(zip(sources, targets))
    ]
    for copy in copies:
        copy.start()
    for copy in copies:
        copy.wait()


def start_kernel(given_ref, out_ref):
    def tile(first):
        rows = [first + comp * 2 + chunk for chunk in range(2) for comp in range(3)]
        return jnp.concatenate([given_ref[row : row + 1] for row in rows], axis=0)

    place = tile(0)
    border = given_ref[14:16]
    kind = given_ref[12:14]
    inverse = jnp.zeros(kind.shape, F32)
    for k in range(N_KIND):
        inverse = jnp.where(kind == k, given_ref[16:17, k : k + 1], inverse)
    index = border.astype(jnp.int32)
    out_ref[0:8] = border_positions(place, index[0:1], index[1:2])
    out_ref[8:14] = place
    out_ref[14:16] = inverse
    out_ref[16:22] = tile(6)
    out_ref[22:24] = border


def fed_columns():
    feature = lax.broadcasted_iota(jnp.int32, (28, LANES), 0)
    col = lax.broadcasted_iota(jnp.int32, (28, LANES), 1)
    block, which = col // 8, col % 8
    radial = (block < 8) & (feature == block)
    environ = (block == 8) & (feature == 8 + which)
    centre = (block == 9) & (which < N_KIND) & (feature == 16 + which)
    neigh = (block >= 10) & (feature == 22 + block - 10)
    return (radial | environ | centre | neigh).astype(F32)


def own_columns(slot, rows):
    col = lax.broadcasted_iota(jnp.int32, (rows, LANES), 1)
    return (col // 8 == 8) | (col // 8 == 9) | (col % 8 == slot)


def two_parts(value):
    high, low = split_parts(value, 2)
    return jnp.concatenate([high, low], axis=0).astype(BF16)


def weight_kernel(
    index_ref, given_ref,
    up_ref, down_ref, line_ref, flat_ref, sum_ref, hot_ref, atom_ref, first_ref, second_ref, back_ref,
):
    middle = given_ref[0:HIDDEN]
    opening = given_ref[HIDDEN : HIDDEN + 8]
    edge_w = given_ref[HIDDEN + 8 : HIDDEN + 9]
    atom_w = given_ref[HIDDEN + 9 : HIDDEN + 10]
    intake = given_ref[HIDDEN + 16 : HIDDEN + 44].astype(BF16)
    fed = fed_columns()
    for j in range(8):
        up = jnp.where(own_columns(j, 28), 0.5 * fed, 0.0).astype(BF16)
        up_ref[j * HIDDEN : (j + 1) * HIDDEN, :] = tn_dot(intake, up).astype(BF16)
    weighted = intake.astype(F32) * (0.5 * edge_w)
    down_ref[...] = two_parts(weighted[0:16])
    line = jnp.sum(weighted, axis=1, keepdims=True)
    flat_ref[...] = jnp.broadcast_to(line[0:16], (16, LANES))
    line = jnp.sum(fed * line, axis=0, keepdims=True)
    slot = lax.broadcasted_iota(jnp.int32, (8, LANES), 0)
    line_ref[...] = two_parts(jnp.where(own_columns(slot, 8), line, 0.0))
    wide = jnp.transpose(jnp.broadcast_to(edge_w, (LANES, HIDDEN)))
    sum_ref[...] = jnp.concatenate([wide, wide], axis=1).astype(BF16)
    atom_ref[...] = jnp.transpose(jnp.broadcast_to(0.5 * atom_w, (LANES, HIDDEN)))
    first_ref[...] = jnp.transpose(0.5 * opening).astype(BF16)
    second_ref[...] = (0.5 * middle).astype(BF16)
    back_ref[...] = jnp.transpose(middle).astype(BF16)
    place = lax.broadcasted_iota(jnp.int32, (LANES, 2 * LANES), 0)

    def group(s, carry):
        for j in range(8):
            lane = index_ref[0, pl.ds(s * 8 + j, 1), :] & (LANES - 1)
            hot_ref[:, pl.ds(pl.multiple_of((s * 8 + j) * 256, 256), 256)] = (place == lane).astype(F32).astype(BF16)
        return carry

    lax.fori_loop(0, GROUPS, group, 0)


def far_tiles(far_ref):
    if len(far_ref.shape) == 5:
        return far_ref[0, 0, 0], far_ref[0, 0, 1], far_ref[1, 1, 0], far_ref[1, 1, 1]
    return far_ref[0, 0], far_ref[0, 1], far_ref[1, 0], far_ref[1, 1]


def force_kernel(
    core_ref,
    state_ref,
    near_ref,
    far_ref,
    index_ref,
    place_kind_ref,
    total_ref,
    kind_ref,
    up_ref,
    down_ref,
    line_ref,
    flat_ref,
    sum_ref,
    hot_ref,
    atom_ref,
    first_ref,
    second_ref,
    back_ref,
    opening_ref,
    out_ref,
    feat_ref,
    gauss_ref,
    geo_ref,
    energy_ref,
    gin0_ref,
    gin1_ref,
    scat0_ref,
    scat1_ref,
):
    core = core_ref[0]
    first_core = core == 0
    own = state_ref[core]
    minus2, minus1, plus2, plus3 = far_tiles(far_ref)
    near0, near1 = near_ref[0], near_ref[1]

    def pick(a, b):
        return jnp.where(first_core, a, b)

    ghost = four_sets(
        pick(minus1, near0), pick(near1, plus2), pick(minus2, minus1), pick(plus2, plus3)
    )

    kind_rows = lax.broadcasted_iota(jnp.int32, (8, 2 * LANES), 0)
    centre_hot = (kind_rows == kind_ref[...]).astype(F32)
    slot_row = lax.broadcasted_iota(jnp.int32, (8, LANES), 0)
    tables = [
        [jnp.broadcast_to(t[r * 3 + c : r * 3 + c + 1], (8, LANES)) for c in range(3)]
        for t in (own, ghost)
        for r in range(2)
    ]

    def geometry(s, sums):
        sums = list(sums)
        slots = pl.ds(pl.multiple_of(s * 8, 8), 8)
        radials = [[], []]
        for h in range(2):
            cols = slice(h * LANES, (h + 1) * LANES)
            index = index_ref[0, slots, cols]
            lane = index & (LANES - 1)
            chunk = index // LANES
            dist_sq = None
            for comp in range(3):
                found = take_lanes(tables[0][comp], lane)
                for which in range(1, 4):
                    found = jnp.where(chunk == which, take_lanes(tables[which][comp], lane), found)
                vec = found - tables[h][comp]
                geo_ref[comp, s, :, cols] = vec
                dist_sq = vec * vec if comp == 0 else dist_sq + vec * vec
            live = slot_row + s * 8 < total_ref[:, cols]
            inside = 1.0 - dist_sq * (1.0 / CUT_SQ)
            used = live & (inside > 0.0)
            cutoff = jnp.where(used, inside * inside, 0.0)
            geo_ref[3, s, :, cols] = dist_sq
            geo_ref[4, s, :, cols] = cutoff
            geo_ref[5, s, :, cols] = jnp.where(used, inside * (-2.0 / CUT_SQ), 0.0)
            for c in range(N_BASIS):
                gap = dist_sq - CENTRES[c]
                gauss = jnp.exp(-SHARP * (gap * gap))
                gauss_ref[s, c * 8 : c * 8 + 8, cols] = gauss
                radial = gauss * cutoff
                radials[h].append(radial)
                sums[h * N_BASIS + c] = sums[h * N_BASIS + c] + radial
        place_kind = place_kind_ref[0, slots, :]
        rows = [jnp.concatenate([a, b], axis=1) for a, b in zip(*radials)]
        feat_ref[s, 0:64] = jnp.concatenate(rows, axis=0).astype(BF16)
        rows = [(place_kind == k).astype(F32) for k in range(N_KIND)]
        feat_ref[s, 80:128] = jnp.concatenate(rows, axis=0).astype(BF16)
        return tuple(sums)

    nothing = jnp.zeros((8, LANES), F32)
    sums = lax.fori_loop(0, GROUPS, geometry, (nothing,) * (2 * N_BASIS))
    rows = [jnp.sum(value, axis=0, keepdims=True) for value in sums]
    environ = jnp.concatenate(
        [jnp.concatenate(rows[:N_BASIS], axis=0), jnp.concatenate(rows[N_BASIS:], axis=0)], axis=1
    )
    shared = jnp.concatenate([environ, centre_hot], axis=0).astype(BF16)
    for s in range(GROUPS):
        feat_ref[s, 64:80] = shared

    atom_w = jnp.concatenate([atom_ref[...], atom_ref[...]], axis=1)
    half = nn_dot(first_ref[...], environ.astype(BF16))
    th = jnp.tanh(half)
    hidden_one = (half + half * th).astype(BF16)
    slope_one = 0.5 * (1.0 + th + half * (1.0 - th * th))
    half = nn_dot(second_ref[...], hidden_one)
    th = jnp.tanh(half)
    g_second = (atom_w * (1.0 + th + half * (1.0 - th * th))).astype(BF16)
    g_hidden = nn_dot(back_ref[...], g_second)
    g_first = (g_hidden * slope_one).astype(BF16)
    g_env = nn_dot(opening_ref[...], g_first)

    flat = jnp.concatenate([flat_ref[...], flat_ref[...]], axis=1)
    slot = lax.broadcasted_iota(jnp.int32, (16, HIDDEN), 0)
    quarter = lax.broadcasted_iota(jnp.int32, (16, HIDDEN), 1) // (HIDDEN // 4)
    members = [(slot == quarter + 4 * k).astype(F32).astype(BF16) for k in range(2)]

    def group(s, g_env):
        feat = feat_ref[s]
        line = nn_dot(line_ref[...], feat)
        energy = line[0:8] + line[8:16]
        folded = []

        def forward(j):
            return nn_dot(up_ref[j * HIDDEN : (j + 1) * HIDDEN, :], feat).astype(BF16)

        ahead = [forward(j) for j in range(AHEAD)]
        for j in range(8):
            half = ahead.pop(0)
            if j + AHEAD < 8:
                ahead.append(forward(j + AHEAD))
            th = jnp.tanh(half)
            rest = sum_ref[...] * (half * th)
            rest = rest[: HIDDEN // 2] + rest[HIDDEN // 2 :]
            folded.append(rest[: HIDDEN // 4] + rest[HIDDEN // 4 :])
            slope = th + half * (jnp.asarray(1.0, BF16) - th * th)
            g_in = nn_dot(down_ref[...], slope)
            cut = geo_ref[4, s, j : j + 1, :]
            g_in = (g_in[0:16] + g_in[16:32] + flat) * cut
            rows = pl.ds(s * 64 + j, 8, stride=8)
            gin0_ref[rows, :] = g_in[0:8, :LANES]
            gin1_ref[rows, :] = g_in[0:8, LANES:]
            g_env = g_env + g_in[8:16]
        for k in range(2):
            rest = jnp.concatenate(folded[k * 4 : k * 4 + 4], axis=0)
            energy = energy + nn_dot(members[k], rest)[0:8]
        energy_ref[s] = energy
        return g_env

    g_env = lax.fori_loop(0, GROUPS, group, g_env)

    def backward(s, sums):
        sums = list(sums)
        slots = slice(s * 8, s * 8 + 8)
        for h in range(2):
            cols = slice(h * LANES, (h + 1) * LANES)
            dist_sq, cutoff, slope = (geo_ref[k, s, :, cols] for k in (3, 4, 5))
            g_cut = energy_ref[s, :, cols]
            g_gap = None
            gin = (gin0_ref, gin1_ref)[h]
            for c in range(N_BASIS):
                rows = slice(s * 64 + c * 8, s * 64 + c * 8 + 8)
                g_radial = gin[rows, :] + g_env[c : c + 1, cols]
                q = g_radial * gauss_ref[s, c * 8 : c * 8 + 8, cols]
                g_cut = g_cut + q
                moment = q * (dist_sq - CENTRES[c])
                g_gap = moment if g_gap is None else g_gap + moment
            g_dist = (-4.0 * SHARP) * (cutoff * g_gap) + 2.0 * (g_cut * slope)
            chunk = index_ref[0, slots, cols] // LANES
            scat = (scat0_ref, scat1_ref)[h]
            for comp in range(3):
                g_vec = g_dist * geo_ref[comp, s, :, cols]
                sums[h * 3 + comp] = sums[h * 3 + comp] + g_vec
                for part, value in enumerate(split_parts(g_vec, 2)):
                    for which in range(4):
                        row = s * 8 * 24 + part * 12 + which * 3 + comp
                        scat[pl.ds(row, 8, stride=24), :] = jnp.where(chunk == which, value, 0.0)
        return tuple(sums)

    sums = (nothing,) * 6
    for s in range(GROUPS):
        sums = backward(s, sums)

    lhs = []
    for slot in range(SLOTS):
        rows = slice(slot * 24, slot * 24 + 24)
        lhs.append(jnp.concatenate([scat0_ref[rows, :], scat1_ref[rows, :]], axis=1).astype(BF16))
    total = nt_dot(jnp.concatenate(lhs, axis=1), hot_ref[...])
    total = total[0:12] + total[12:24]
    centre = jnp.concatenate([jnp.sum(value, axis=0, keepdims=True) for value in sums], axis=0)
    pad = jnp.zeros((2, LANES), F32)
    out_ref[0:8] = jnp.concatenate([total[6:12], pad], axis=0)
    out_ref[8:16] = jnp.concatenate([total[0:6] - centre, pad], axis=0)


def returned_sum(returned, border0, border1):
    row = lax.broadcasted_iota(jnp.int32, (8, LANES), 0)
    place = lax.broadcasted_iota(jnp.int32, (LANES, LANES), 0)
    lhs, rhs = [], []
    for which, border in enumerate((border0, border1)):
        three = returned[which * 3 : which * 3 + 3]
        twice = jnp.concatenate([three, three, jnp.zeros((2, LANES), F32)], axis=0)
        meant = (border // LANES == 1) == (row >= 3)
        kept = jnp.where(meant, twice, 0.0)
        lhs.append(jnp.concatenate(split_parts(kept, 3), axis=0).astype(BF16))
        rhs.append((place == (border & (LANES - 1))).astype(F32).astype(BF16))
    total = nt_dot(jnp.concatenate(lhs, axis=1), jnp.concatenate(rhs, axis=1))
    return total[0:8] + total[8:16] + total[16:24]


def moved(state_ref, near_ref, far_ref):
    minus2, minus1, plus2, plus3 = far_tiles(far_ref)
    near0, near1 = near_ref[0, 0:8], near_ref[1, 0:8]
    sets = ((near1, minus1, plus2, minus2), (plus2, near0, plus3, minus1))
    result = []
    for domain in range(2):
        state = state_ref[domain]
        border0 = state[14:15].astype(jnp.int32)
        border1 = state[15:16].astype(jnp.int32)
        inverse = rows_of_two(state[6:7], state[7:8])
        grad = near_ref[domain, 8:16] + returned_sum(four_sets(*sets[domain]), border0, border1)
        speed = state[8:16] - TIME_STEP * grad * inverse
        place = state[0:8] + TIME_STEP * speed
        result.append((place, speed, border0, border1))
    return result


def step_kernel(state_ref, near_ref, far_ref, send_ref, next_ref):
    for domain, (place, speed, border0, border1) in enumerate(moved(state_ref, near_ref, far_ref)):
        send_ref[domain] = border_positions(place, border0, border1)
        next_ref[domain, 0:6] = place[0:6]
        next_ref[domain, 6:8] = state_ref[domain, 6:8]
        next_ref[domain, 8:14] = speed[0:6]
        next_ref[domain, 14:16] = state_ref[domain, 14:16]


def last_kernel(level_ref, state_ref, near_ref, far_ref, next_ref):
    for domain, (place, speed, _, _) in enumerate(moved(state_ref, near_ref, far_ref)):
        next_ref[domain, 0:6] = place[0:6]
        next_ref[domain, 6:8] = jnp.full((2, LANES), level_ref[0], F32)
        next_ref[domain, 8:16] = speed


def swap_kernel(where_ref, level_ref, own_ref, mate_ref, x_out, v_out, x_ref, v_ref, sems):
    core, swaps, side, position = (where_ref[k] for k in range(4))
    mine = own_ref[core]
    theirs = mate_ref[side, position, core]
    chosen = jnp.where(swaps == 1, theirs, mine)
    scale = jnp.sqrt(level_ref[0] / chosen[6:7])
    put_flat(x_ref, chosen[0:6])
    put_flat(v_ref, chosen[8:14] * scale)
    bring((x_ref, v_ref), (x_out, v_out), sems)


def vmem():
    return pl.BlockSpec(memory_space=pltpu.VMEM)


def smem():
    return pl.BlockSpec(memory_space=pltpu.SMEM)


def tiles(*shape):
    return jax.ShapeDtypeStruct(shape + (LANES,), F32)


def call(kernel, scalars, arrays, out_shape, scratch=(), flops=10**6, outputs=None):
    outputs = outputs or vmem
    out_specs = [outputs() for _ in out_shape] if isinstance(out_shape, list) else outputs()
    return pl.pallas_call(
        kernel,
        out_shape=out_shape,
        in_specs=[smem()] * len(scalars) + [vmem()] * len(arrays),
        out_specs=out_specs,
        scratch_shapes=list(scratch),
        cost_estimate=pl.CostEstimate(flops=flops, bytes_accessed=10**6, transcendentals=0),
        compiler_params=pltpu.CompilerParams(vmem_limit_bytes=24 * 2**20),
    )(*scalars, *arrays)


def anywhere():
    return pl.BlockSpec(memory_space=pltpu.HBM)


def landing(arrays):
    return [pltpu.VMEM(a.shape, a.dtype) for a in arrays] + [pltpu.SemaphoreType.DMA((len(arrays),))]


def weight_shapes():
    return [
        jax.ShapeDtypeStruct((8 * HIDDEN, LANES), BF16),
        jax.ShapeDtypeStruct((32, HIDDEN), BF16),
        jax.ShapeDtypeStruct((16, LANES), BF16),
        tiles(16),
        jax.ShapeDtypeStruct((HIDDEN, 2 * LANES), BF16),
        jax.ShapeDtypeStruct((LANES, SLOTS * 2 * LANES), BF16),
        tiles(HIDDEN),
        jax.ShapeDtypeStruct((HIDDEN, N_BASIS), BF16),
        jax.ShapeDtypeStruct((HIDDEN, HIDDEN), BF16),
        jax.ShapeDtypeStruct((HIDDEN, HIDDEN), BF16),
    ]


def force_scratch():
    return [
        pltpu.VMEM((GROUPS, 128, 2 * LANES), BF16),
        pltpu.VMEM((GROUPS, 64, 2 * LANES), F32),
        pltpu.VMEM((6, GROUPS, 8, 2 * LANES), F32),
        pltpu.VMEM((GROUPS, 8, 2 * LANES), F32),
        pltpu.VMEM((GROUPS * 64, LANES), F32),
        pltpu.VMEM((GROUPS * 64, LANES), F32),
        pltpu.VMEM((SLOTS * 24, LANES), F32),
        pltpu.VMEM((SLOTS * 24, LANES), F32),
    ]


def on_chip(value, domains):
    groups = [[2 * i, 2 * i + 1] for i in range(domains // 2)]
    return lax.all_gather(value, "space", axis_index_groups=groups)


def across_chips(value, domains):
    groups = [[(2 * i - 1) % domains, 2 * i] for i in range(domains // 2)]
    return lax.all_gather(value, "space", axis_index_groups=groups)


def partner_across(value, domains):
    pairs = []
    for i in range(domains // 2):
        odd, even = (2 * i - 1) % domains, 2 * i
        pairs += [(odd, even), (even, odd)]
    return lax.ppermute(value, "space", pairs)


def along_ladder(value, rungs, domains):
    groups = []
    for domain in range(domains):
        shift = domain % 2
        for low in range(shift, rungs, 2):
            high = (low + 1) % rungs
            groups.append([low * domains + domain, high * domains + domain])
    return lax.all_gather(value, ("replica", "space"), axis_index_groups=groups)


def on_device(
    particle_coordinates,
    particle_motions,
    particle_kinds,
    filled_totals,
    adjacent_particles,
    adjacent_place_kinds,
    border_particle_numbers,
    reciprocal_kind_inertia,
    thermal_levels,
    swap_mates,
    bond_intake_coefficients,
    bond_output_coefficients,
    particle_opening_coefficients,
    particle_middle_coefficients,
    particle_output_coefficients,
):
    domains, rungs = lax.axis_size("space"), lax.axis_size("replica")
    core = lax.axis_index("space") % 2
    rank = lax.axis_index("replica")
    mate = swap_mates[0]
    odd = rank % 2
    side = jnp.where((mate > rank) == (odd == 0), 0, 1)
    position = jnp.where(side == 0, 1 - odd, odd)
    where_to = jnp.stack([core, (mate != rank).astype(jnp.int32), side, position]).astype(jnp.int32)

    rows = [particle_coordinates, particle_motions, particle_kinds, border_particle_numbers]
    rows = [value.reshape(-1, LANES).astype(F32) for value in rows]
    rows += [jnp.pad(reciprocal_kind_inertia[None], ((0, 7), (0, LANES - N_KIND)))]
    begin = call(start_kernel, (), (jnp.concatenate(rows, axis=0),), tiles(24))
    rows = [
        particle_middle_coefficients,
        particle_opening_coefficients.T,
        bond_output_coefficients[None],
        particle_output_coefficients[None],
        jnp.zeros((6, HIDDEN), F32),
        bond_intake_coefficients.T,
    ]
    rows = jnp.concatenate([value.astype(F32) for value in rows], axis=0)
    weights = call(weight_kernel, (), (adjacent_particles, rows), weight_shapes(), (), 10**9)
    both = on_chip(begin, domains)
    send, state = both[:, 0:8], both[:, 8:24]
    for step in range(STEPS):
        if step == 0:
            far = on_chip(partner_across(send, domains), domains)
        else:
            far = on_chip(across_chips(send, domains), domains)
        partial = call(
            force_kernel,
            (where_to,),
            (
                state,
                send,
                far,
                adjacent_particles,
                adjacent_place_kinds,
                filled_totals,
                particle_kinds,
                *weights,
                particle_opening_coefficients.T,
            ),
            tiles(16),
            force_scratch(),
        )
        near = on_chip(partial, domains)
        far = on_chip(across_chips(near[:, 0:8], domains), domains)
        if step < STEPS - 1:
            send, state = call(step_kernel, (), (state, near, far), [tiles(2, 8), tiles(2, 16)])
        else:
            state = call(last_kernel, (thermal_levels,), (state, near, far), tiles(2, 16))
    mates = on_chip(along_ladder(state, rungs, domains), domains)
    shape = particle_coordinates.shape
    out = jax.ShapeDtypeStruct((1, particle_coordinates.size), F32)
    scratch = landing((out, out))
    new_x, new_v = call(
        swap_kernel, (where_to, thermal_levels), (state, mates), [out, out], scratch, outputs=anywhere
    )
    return new_x.reshape(shape), new_v.reshape(shape)


def solution(mesh):
    return jax.shard_map(
        on_device,
        mesh=mesh,
        in_specs=(
            P("replica", None, "space"),
            P("replica", None, "space"),
            P("replica", "space"),
            P("replica", "space"),
            P("replica", None, "space"),
            P("replica", None, "space"),
            P("replica", None, "space"),
            P(),
            P("replica"),
            P("replica"),
            P(),
            P(),
            P(),
            P(),
            P(),
        ),
        out_specs=(P("replica", None, "space"), P("replica", None, "space")),
        check_vma=False,
    )
```

```python
import functools

import jax
import jax.numpy as jnp
from jax import lax
from jax.experimental import pallas as pl
from jax.experimental.pallas import tpu as pltpu
from jax.sharding import PartitionSpec as P

STEPS = 2
TIME_STEP = 0.05
CUT_SQ = 9.0
N_BASIS = 8
N_KIND = 6
LANES = 128
SLOTS = 32
GROUPS = SLOTS // 8
HIDDEN = 256
AHEAD = 4
SHARP = (N_BASIS / CUT_SQ) ** 2
CENTRES = [CUT_SQ * c / (N_BASIS - 1) for c in range(N_BASIS)]
F32 = jnp.float32
BF16 = jnp.bfloat16


def nt_dot(a, b):
    return lax.dot_general(a, b, (((1,), (1,)), ((), ())), preferred_element_type=F32)


def tn_dot(a, b):
    return lax.dot_general(a, b, (((0,), (0,)), ((), ())), preferred_element_type=F32)


def nn_dot(a, b):
    return lax.dot_general(a, b, (((1,), (0,)), ((), ())), preferred_element_type=F32)


def tile_of(flat_ref):
    rows = [
        flat_ref[:, (comp * 2 + chunk) * LANES : (comp * 2 + chunk + 1) * LANES]
        for chunk in range(2)
        for comp in range(3)
    ]
    return jnp.concatenate(rows, axis=0)


def put_flat(flat_ref, tile):
    for chunk in range(2):
        for comp in range(3):
            start = (comp * 2 + chunk) * LANES
            row = chunk * 3 + comp
            flat_ref[:, start : start + LANES] = tile[row : row + 1]


def rows_of_two(first, second, pad_with=None):
    shape = (3, LANES)
    pad = jnp.zeros((2, LANES), first.dtype)
    return jnp.concatenate(
        [jnp.broadcast_to(first, shape), jnp.broadcast_to(second, shape), pad], axis=0
    )


def take_lanes(table, lane):
    return jnp.take_along_axis(table, lane, axis=1, mode="promise_in_bounds")


def border_positions(tile, border0, border1):
    index = rows_of_two(border0, border1)
    pad = jnp.zeros((2, LANES), F32)
    low = jnp.concatenate([tile[0:3], tile[0:3], pad], axis=0)
    high = jnp.concatenate([tile[3:6], tile[3:6], pad], axis=0)
    lane = index & (LANES - 1)
    return jnp.where(index < LANES, take_lanes(low, lane), take_lanes(high, lane))


def four_sets(set0, set1, set2, set3):
    row = lax.broadcasted_iota(jnp.int32, (8, LANES), 0)
    col = lax.broadcasted_iota(jnp.int32, (8, LANES), 1)
    left = col < LANES // 2
    return jnp.where(row < 3, jnp.where(left, set0, set1), jnp.where(left, set2, set3))


def split_parts(value, count):
    parts = []
    for _ in range(count):
        part = value.astype(BF16).astype(F32)
        parts.append(part)
        value = value - part
    return parts


def bring(sources, targets, sems):
    copies = [
        pltpu.make_async_copy(source, target, sems.at[k])
        for k, (source, target) in enumerate(zip(sources, targets))
    ]
    for copy in copies:
        copy.start()
    for copy in copies:
        copy.wait()


def fed_columns():
    feature = lax.broadcasted_iota(jnp.int32, (28, LANES), 0)
    col = lax.broadcasted_iota(jnp.int32, (28, LANES), 1)
    block, which = col // 8, col % 8
    radial = (block < 8) & (feature == block)
    environ = (block == 8) & (feature == 8 + which)
    centre = (block == 9) & (which < N_KIND) & (feature == 16 + which)
    neigh = (block >= 10) & (feature == 22 + block - 10)
    return (radial | environ | centre | neigh).astype(F32)


def own_columns(slot, rows):
    col = lax.broadcasted_iota(jnp.int32, (rows, LANES), 1)
    return (col // 8 == 8) | (col // 8 == 9) | (col % 8 == slot)


def two_parts(value):
    high, low = split_parts(value, 2)
    return jnp.concatenate([high, low], axis=0).astype(BF16)


def begin_kernel(*refs):
    inputs, refs = refs[:13], refs[13:]
    (out_ref, up_ref, down_ref, line_ref, flat_ref, sum_ref, hot_ref, atom_ref, first_ref,
     second_ref, back_ref, index_ref, place_ref, total_ref, kind_ref, opening_ref), refs = (
        refs[:16], refs[16:]
    )
    x_ref, v_ref, border_ref, inertia_ref, intake_ref, edge_out_ref, middle_ref, atom_out_ref = (
        refs[:8]
    )
    landed = (
        x_ref, v_ref, kind_ref, border_ref, inertia_ref, index_ref, place_ref, total_ref,
        intake_ref, edge_out_ref, opening_ref, middle_ref, atom_out_ref,
    )
    bring(inputs, landed, refs[8])

    x_tile = tile_of(x_ref)
    border = border_ref[0]
    border0 = jnp.concatenate([border[0:1], border[1:2]], axis=1)
    border1 = jnp.concatenate([border[2:3], border[3:4]], axis=1)
    kind = kind_ref[...]
    inverse = jnp.zeros(kind.shape, F32)
    for k in range(N_KIND):
        inverse = jnp.where(kind == k, inertia_ref[k], inverse)
    out_ref[0:8] = border_positions(x_tile, border0, border1)
    out_ref[8:14] = x_tile
    out_ref[14:15] = inverse[:, :LANES]
    out_ref[15:16] = inverse[:, LANES:]
    out_ref[16:22] = tile_of(v_ref)
    out_ref[22:23] = border0.astype(F32)
    out_ref[23:24] = border1.astype(F32)

    place = lax.broadcasted_iota(jnp.int32, (LANES, 2 * LANES), 0).astype(F32).astype(BF16)
    one, none = jnp.asarray(1.0, BF16), jnp.asarray(0.0, BF16)

    def group(s, carry):
        for j in range(8):
            lane = (index_ref[0, pl.ds(s * 8 + j, 1), :] & (LANES - 1)).astype(F32)
            lane = jnp.broadcast_to(lane, (16, 2 * LANES)).astype(BF16)
            lane = jnp.concatenate([lane] * (LANES // 16), axis=0)
            cols = pl.ds(pl.multiple_of((s * 8 + j) * 2 * LANES, 2 * LANES), 2 * LANES)
            hot_ref[:, cols] = jnp.where(place == lane, one, none)
        return carry

    lax.fori_loop(0, GROUPS, group, 0)
    intake = intake_ref[...]
    fed = fed_columns()
    for j in range(8):
        up = jnp.where(own_columns(j, 28), 0.5 * fed, 0.0).astype(BF16)
        up_ref[j * HIDDEN : (j + 1) * HIDDEN, :] = tn_dot(intake, up).astype(BF16)
    edge_w = edge_out_ref[...]
    weighted = intake.astype(F32) * (0.5 * edge_w)
    down_ref[...] = two_parts(weighted[0:16])
    line = jnp.sum(weighted, axis=1, keepdims=True)
    flat_ref[...] = jnp.broadcast_to(line[0:16], (16, LANES))
    line = jnp.sum(fed * line, axis=0, keepdims=True)
    slot = lax.broadcasted_iota(jnp.int32, (8, LANES), 0)
    line_ref[...] = two_parts(jnp.where(own_columns(slot, 8), line, 0.0))
    wide = jnp.transpose(jnp.broadcast_to(edge_w, (LANES, HIDDEN)))
    sum_ref[...] = jnp.concatenate([wide, wide], axis=1).astype(BF16)
    atom_ref[...] = jnp.transpose(jnp.broadcast_to(0.5 * atom_out_ref[...], (LANES, HIDDEN)))
    first_ref[...] = jnp.transpose((0.5 * opening_ref[...]).astype(F32)).astype(BF16)
    second_ref[...] = 0.5 * middle_ref[...]
    back_ref[...] = jnp.transpose(middle_ref[...].astype(F32)).astype(BF16)


def far_tiles(far_ref):
    return far_ref[0, 0, 0], far_ref[0, 0, 1], far_ref[1, 1, 0], far_ref[1, 1, 1]


def force_kernel(
    where_ref,
    state_ref,
    near_ref,
    far_ref,
    up_ref,
    down_ref,
    line_ref,
    flat_ref,
    sum_ref,
    hot_ref,
    atom_ref,
    first_ref,
    second_ref,
    back_ref,
    index_ref,
    place_kind_ref,
    total_ref,
    kind_ref,
    opening_ref,
    out_ref,
    feat_ref,
    gauss_ref,
    geo_ref,
    energy_ref,
    gin0_ref,
    gin1_ref,
    scat0_ref,
    scat1_ref,
):
    first_core = where_ref[0:1] == 0
    own = jnp.where(first_core, state_ref[0], state_ref[1])
    minus2, minus1, plus2, plus3 = far_tiles(far_ref)
    near0, near1 = near_ref[0], near_ref[1]

    def pick(a, b):
        return jnp.where(first_core, a, b)

    ghost = four_sets(
        pick(minus1, near0), pick(near1, plus2), pick(minus2, minus1), pick(plus2, plus3)
    )

    kind_rows = lax.broadcasted_iota(jnp.int32, (8, 2 * LANES), 0)
    centre_hot = (kind_rows == kind_ref[...]).astype(F32)
    slot_row = lax.broadcasted_iota(jnp.int32, (8, LANES), 0)
    tables = [
        [jnp.broadcast_to(t[r * 3 + c : r * 3 + c + 1], (8, LANES)) for c in range(3)]
        for t in (own, ghost)
        for r in range(2)
    ]

    def geometry(s, sums):
        sums = list(sums)
        slots = pl.ds(pl.multiple_of(s * 8, 8), 8)
        radials = [[], []]
        for h in range(2):
            cols = slice(h * LANES, (h + 1) * LANES)
            index = index_ref[0, slots, cols]
            lane = index & (LANES - 1)
            chunk = index // LANES
            dist_sq = None
            for comp in range(3):
                found = take_lanes(tables[0][comp], lane)
                for which in range(1, 4):
                    found = jnp.where(chunk == which, take_lanes(tables[which][comp], lane), found)
                vec = found - tables[h][comp]
                geo_ref[comp, s, :, cols] = vec
                dist_sq = vec * vec if comp == 0 else dist_sq + vec * vec
            live = slot_row + s * 8 < total_ref[:, cols]
            inside = 1.0 - dist_sq * (1.0 / CUT_SQ)
            used = live & (inside > 0.0)
            cutoff = jnp.where(used, inside * inside, 0.0)
            geo_ref[3, s, :, cols] = dist_sq
            geo_ref[4, s, :, cols] = cutoff
            geo_ref[5, s, :, cols] = jnp.where(used, inside * (-2.0 / CUT_SQ), 0.0)
            for c in range(N_BASIS):
                gap = dist_sq - CENTRES[c]
                gauss = jnp.exp(-SHARP * (gap * gap))
                gauss_ref[s, c * 8 : c * 8 + 8, cols] = gauss
                radial = gauss * cutoff
                radials[h].append(radial)
                sums[h * N_BASIS + c] = sums[h * N_BASIS + c] + radial
        place_kind = place_kind_ref[0, slots, :]
        rows = [jnp.concatenate([a, b], axis=1) for a, b in zip(*radials)]
        feat_ref[s, 0:64] = jnp.concatenate(rows, axis=0).astype(BF16)
        rows = [(place_kind == k).astype(F32) for k in range(N_KIND)]
        feat_ref[s, 80:128] = jnp.concatenate(rows, axis=0).astype(BF16)
        return tuple(sums)

    nothing = jnp.zeros((8, LANES), F32)
    sums = lax.fori_loop(0, GROUPS, geometry, (nothing,) * (2 * N_BASIS))
    rows = [jnp.sum(value, axis=0, keepdims=True) for value in sums]
    environ = jnp.concatenate(
        [jnp.concatenate(rows[:N_BASIS], axis=0), jnp.concatenate(rows[N_BASIS:], axis=0)], axis=1
    )
    shared = jnp.concatenate([environ, centre_hot], axis=0).astype(BF16)
    for s in range(GROUPS):
        feat_ref[s, 64:80] = shared

    atom_w = jnp.concatenate([atom_ref[...], atom_ref[...]], axis=1)
    half = nn_dot(first_ref[...], environ.astype(BF16))
    th = jnp.tanh(half)
    hidden_one = (half + half * th).astype(BF16)
    slope_one = 0.5 * (1.0 + th + half * (1.0 - th * th))
    half = nn_dot(second_ref[...], hidden_one)
    th = jnp.tanh(half)
    g_second = (atom_w * (1.0 + th + half * (1.0 - th * th))).astype(BF16)
    g_hidden = nn_dot(back_ref[...], g_second)
    g_first = (g_hidden * slope_one).astype(BF16)
    g_env = nn_dot(opening_ref[...], g_first)

    flat = jnp.concatenate([flat_ref[...], flat_ref[...]], axis=1)
    slot = lax.broadcasted_iota(jnp.int32, (16, HIDDEN), 0)
    quarter = lax.broadcasted_iota(jnp.int32, (16, HIDDEN), 1) // (HIDDEN // 4)
    members = [(slot == quarter + 4 * k).astype(F32).astype(BF16) for k in range(2)]

    def group(s, g_env):
        feat = feat_ref[s]
        line = nn_dot(line_ref[...], feat)
        energy = line[0:8] + line[8:16]
        folded = []

        def forward(k):
            many = nn_dot(up_ref[k * AHEAD * HIDDEN : (k + 1) * AHEAD * HIDDEN, :], feat)
            return [many[i * HIDDEN : (i + 1) * HIDDEN].astype(BF16) for i in range(AHEAD)]

        ahead = forward(0)
        for j in range(8):
            half = ahead.pop(0)
            if j % AHEAD == 0 and j + AHEAD < 8:
                ahead += forward(j // AHEAD + 1)
            th = jnp.tanh(half)
            rest = sum_ref[...] * (half * th)
            rest = rest[: HIDDEN // 2] + rest[HIDDEN // 2 :]
            folded.append(rest[: HIDDEN // 4] + rest[HIDDEN // 4 :])
            slope = th + half * (jnp.asarray(1.0, BF16) - th * th)
            g_in = nn_dot(down_ref[...], slope)
            cut = geo_ref[4, s, j : j + 1, :]
            g_in = (g_in[0:16] + g_in[16:32] + flat) * cut
            rows = pl.ds(s * 64 + j, 8, stride=8)
            gin0_ref[rows, :] = g_in[0:8, :LANES]
            gin1_ref[rows, :] = g_in[0:8, LANES:]
            g_env = g_env + g_in[8:16]
        for k in range(2):
            rest = jnp.concatenate(folded[k * 4 : k * 4 + 4], axis=0)
            energy = energy + nn_dot(members[k], rest)[0:8]
        energy_ref[s] = energy
        return g_env

    g_env = lax.fori_loop(1, GROUPS, group, group(0, g_env))

    def backward(s, sums):
        sums = list(sums)
        slots = slice(s * 8, s * 8 + 8)
        for h in range(2):
            cols = slice(h * LANES, (h + 1) * LANES)
            dist_sq, cutoff, slope = (geo_ref[k, s, :, cols] for k in (3, 4, 5))
            g_cut = energy_ref[s, :, cols]
            g_gap = None
            gin = (gin0_ref, gin1_ref)[h]
            for c in range(N_BASIS):
                rows = slice(s * 64 + c * 8, s * 64 + c * 8 + 8)
                g_radial = gin[rows, :] + g_env[c : c + 1, cols]
                q = g_radial * gauss_ref[s, c * 8 : c * 8 + 8, cols]
                g_cut = g_cut + q
                moment = q * (dist_sq - CENTRES[c])
                g_gap = moment if g_gap is None else g_gap + moment
            g_dist = (-4.0 * SHARP) * (cutoff * g_gap) + 2.0 * (g_cut * slope)
            chunk = index_ref[0, slots, cols] // LANES
            scat = (scat0_ref, scat1_ref)[h]
            for comp in range(3):
                g_vec = g_dist * geo_ref[comp, s, :, cols]
                sums[h * 3 + comp] = sums[h * 3 + comp] + g_vec
                for part, value in enumerate(split_parts(g_vec, 2)):
                    for which in range(4):
                        row = s * 8 * 24 + part * 12 + which * 3 + comp
                        scat[pl.ds(row, 8, stride=24), :] = jnp.where(chunk == which, value, 0.0)
        return tuple(sums)

    sums = (nothing,) * 6
    for s in range(GROUPS):
        sums = backward(s, sums)

    lhs = []
    for slot in range(SLOTS):
        rows = slice(slot * 24, slot * 24 + 24)
        lhs.append(jnp.concatenate([scat0_ref[rows, :], scat1_ref[rows, :]], axis=1).astype(BF16))
    total = nt_dot(jnp.concatenate(lhs, axis=1), hot_ref[...])
    total = total[0:12] + total[12:24]
    centre = jnp.concatenate([jnp.sum(value, axis=0, keepdims=True) for value in sums], axis=0)
    pad = jnp.zeros((2, LANES), F32)
    out_ref[0:8] = jnp.concatenate([total[6:12], pad], axis=0)
    out_ref[8:16] = jnp.concatenate([total[0:6] - centre, pad], axis=0)


def returned_sum(returned, border0, border1):
    row = lax.broadcasted_iota(jnp.int32, (8, LANES), 0)
    place = lax.broadcasted_iota(jnp.int32, (LANES, LANES), 0)
    lhs, rhs = [], []
    for which, border in enumerate((border0, border1)):
        three = returned[which * 3 : which * 3 + 3]
        twice = jnp.concatenate([three, three, jnp.zeros((2, LANES), F32)], axis=0)
        meant = (border // LANES == 1) == (row >= 3)
        kept = jnp.where(meant, twice, 0.0)
        lhs.append(jnp.concatenate(split_parts(kept, 3), axis=0).astype(BF16))
        rhs.append((place == (border & (LANES - 1))).astype(F32).astype(BF16))
    total = nt_dot(jnp.concatenate(lhs, axis=1), jnp.concatenate(rhs, axis=1))
    return total[0:8] + total[8:16] + total[16:24]


def moved(state_ref, near_ref, far_ref):
    minus2, minus1, plus2, plus3 = far_tiles(far_ref)
    near0, near1 = near_ref[0, 0:8], near_ref[1, 0:8]
    sets = ((near1, minus1, plus2, minus2), (plus2, near0, plus3, minus1))
    result = []
    for domain in range(2):
        state = state_ref[domain]
        border0 = state[14:15].astype(jnp.int32)
        border1 = state[15:16].astype(jnp.int32)
        inverse = rows_of_two(state[6:7], state[7:8])
        grad = near_ref[domain, 8:16] + returned_sum(four_sets(*sets[domain]), border0, border1)
        speed = state[8:16] - TIME_STEP * grad * inverse
        place = state[0:8] + TIME_STEP * speed
        result.append((place, speed, border0, border1))
    return result


def step_kernel(state_ref, near_ref, far_ref, send_ref, next_ref):
    for domain, (place, speed, border0, border1) in enumerate(moved(state_ref, near_ref, far_ref)):
        send_ref[domain] = border_positions(place, border0, border1)
        next_ref[domain, 0:6] = place[0:6]
        next_ref[domain, 6:8] = state_ref[domain, 6:8]
        next_ref[domain, 8:14] = speed[0:6]
        next_ref[domain, 14:16] = state_ref[domain, 14:16]


def last_kernel(where_ref, state_ref, near_ref, far_ref, next_ref):
    for domain, (place, speed, _, _) in enumerate(moved(state_ref, near_ref, far_ref)):
        next_ref[domain, 0:6] = place[0:6]
        next_ref[domain, 6:8] = jnp.broadcast_to(where_ref[4:5], (2, LANES))
        next_ref[domain, 8:16] = speed


def swap_kernel(where_ref, own_ref, mate_ref, x_out, v_out, x_ref, v_ref, sems):
    core, swaps, side, position = (where_ref[k : k + 1] == 0 for k in range(4))

    def of_core(pair):
        return jnp.where(core, pair[0], pair[1])

    def of_side(s):
        return of_core(jnp.where(position, mate_ref[s, 0], mate_ref[s, 1]))

    mine = of_core(own_ref)
    chosen = jnp.where(swaps, mine, jnp.where(side, of_side(0), of_side(1)))
    scale = jnp.sqrt(mine[6:7] / chosen[6:7])
    put_flat(x_ref, chosen[0:6])
    put_flat(v_ref, chosen[8:14] * scale)
    bring((x_ref, v_ref), (x_out, v_out), sems)


def vmem():
    return pl.BlockSpec(memory_space=pltpu.VMEM)


def smem():
    return pl.BlockSpec(memory_space=pltpu.SMEM)


def tiles(*shape):
    return jax.ShapeDtypeStruct(shape + (LANES,), F32)


def call(kernel, scalars, arrays, out_shape, scratch=(), flops=10**6, inputs=None, outputs=None,
         limit=24 * 2**20):
    outputs = outputs or vmem
    out_specs = [outputs() for _ in out_shape] if isinstance(out_shape, list) else outputs()
    return pl.pallas_call(
        kernel,
        out_shape=out_shape,
        in_specs=[smem()] * len(scalars) + [(inputs or vmem)()] * len(arrays),
        out_specs=out_specs,
        scratch_shapes=list(scratch),
        cost_estimate=pl.CostEstimate(flops=flops, bytes_accessed=10**6, transcendentals=0),
        compiler_params=pltpu.CompilerParams(vmem_limit_bytes=limit),
    )(*scalars, *arrays)


def anywhere():
    return pl.BlockSpec(memory_space=pltpu.HBM)


def landing(arrays):
    return [pltpu.VMEM(a.shape, a.dtype) for a in arrays] + [pltpu.SemaphoreType.DMA((len(arrays),))]


def weight_shapes():
    return [
        jax.ShapeDtypeStruct((8 * HIDDEN, LANES), BF16),
        jax.ShapeDtypeStruct((32, HIDDEN), BF16),
        jax.ShapeDtypeStruct((16, LANES), BF16),
        tiles(16),
        jax.ShapeDtypeStruct((HIDDEN, 2 * LANES), BF16),
        jax.ShapeDtypeStruct((LANES, SLOTS * 2 * LANES), BF16),
        tiles(HIDDEN),
        jax.ShapeDtypeStruct((HIDDEN, N_BASIS), BF16),
        jax.ShapeDtypeStruct((HIDDEN, HIDDEN), BF16),
        jax.ShapeDtypeStruct((HIDDEN, HIDDEN), BF16),
    ]


def begin_shapes(arrays):
    through = [jax.ShapeDtypeStruct(arrays[k].shape, arrays[k].dtype) for k in (5, 6, 7, 2, 10)]
    space = landing([arrays[k] for k in (0, 1, 3, 4, 8, 9, 11, 12)])
    space[3] = pltpu.SMEM(arrays[4].shape, F32)
    space[-1] = pltpu.SemaphoreType.DMA((len(arrays),))
    made = [tiles(24)] + weight_shapes() + through
    return made, space


def force_scratch():
    return [
        pltpu.VMEM((GROUPS, 128, 2 * LANES), BF16),
        pltpu.VMEM((GROUPS, 64, 2 * LANES), F32),
        pltpu.VMEM((6, GROUPS, 8, 2 * LANES), F32),
        pltpu.VMEM((GROUPS, 8, 2 * LANES), F32),
        pltpu.VMEM((GROUPS * 64, LANES), F32),
        pltpu.VMEM((GROUPS * 64, LANES), F32),
        pltpu.VMEM((SLOTS * 24, LANES), F32),
        pltpu.VMEM((SLOTS * 24, LANES), F32),
    ]


def on_chip(value, domains):
    groups = [[2 * i, 2 * i + 1] for i in range(domains // 2)]
    return lax.all_gather(value, "space", axis_index_groups=groups)


def across_chips(value, domains):
    groups = [[(2 * i - 1) % domains, 2 * i] for i in range(domains // 2)]
    return lax.all_gather(value, "space", axis_index_groups=groups)


def along_ladder(value, rungs, domains):
    groups = []
    for domain in range(domains):
        shift = domain % 2
        for low in range(shift, rungs - shift, 2):
            groups.append([low * domains + domain, (low + 1) * domains + domain])
        if shift and domain // 2 % 2 == 0:
            for end in (0, rungs - 1):
                groups.append([end * domains + domain, end * domains + domain + 2])
    return lax.all_gather(value, ("replica", "space"), axis_index_groups=groups)


def on_device(
    particle_coordinates,
    particle_motions,
    particle_kinds,
    filled_totals,
    adjacent_particles,
    adjacent_place_kinds,
    border_particle_numbers,
    reciprocal_kind_inertia,
    thermal_levels,
    swap_mates,
    bond_intake_coefficients,
    bond_output_coefficients,
    particle_opening_coefficients,
    particle_middle_coefficients,
    particle_output_coefficients,
):
    domains, rungs = lax.axis_size("space"), lax.axis_size("replica")
    core = lax.axis_index("space") % 2
    rank = lax.axis_index("replica")
    mate = swap_mates[0]
    odd = rank % 2
    side = jnp.where((mate > rank) == (odd == 0), 0, 1)
    position = jnp.where(side == 0, 1 - odd, odd)
    where_to = [value.astype(F32) for value in (core, mate != rank, side, position)]
    where_to = jnp.stack(where_to + [thermal_levels[0]])
    where_to = jnp.broadcast_to(where_to[:, None], (5, LANES))

    arrays = (
        particle_coordinates.reshape(1, -1),
        particle_motions.reshape(1, -1),
        particle_kinds,
        border_particle_numbers,
        reciprocal_kind_inertia,
        adjacent_particles,
        adjacent_place_kinds,
        filled_totals,
        bond_intake_coefficients.T,
        bond_output_coefficients[None],
        particle_opening_coefficients.T,
        particle_middle_coefficients,
        particle_output_coefficients[None],
    )
    arrays = tuple(pltpu.with_memory_space_constraint(a, pltpu.HBM) for a in arrays)
    made, space = begin_shapes(arrays)
    begin, *fixed = call(begin_kernel, (), arrays, made, space, inputs=anywhere)
    both = on_chip(begin, domains)
    send, state = both[:, 0:8], both[:, 8:24]
    for step in range(STEPS):
        far = on_chip(across_chips(send, domains), domains)
        partial = call(
            force_kernel,
            (),
            (
                where_to,
                state,
                send,
                far,
                *fixed,
            ),
            tiles(16),
            force_scratch(),
        )
        near = on_chip(partial, domains)
        far = on_chip(across_chips(near[:, 0:8], domains), domains)
        if step < STEPS - 1:
            send, state = call(step_kernel, (), (state, near, far), [tiles(2, 8), tiles(2, 16)])
        else:
            state = call(last_kernel, (), (where_to, state, near, far), tiles(2, 16))
    mates = on_chip(along_ladder(state, rungs, domains), domains)
    shape = particle_coordinates.shape
    out = jax.ShapeDtypeStruct((1, particle_coordinates.size), F32)
    scratch = landing((out, out))
    new_x, new_v = call(
        swap_kernel, (), (where_to, state, mates), [out, out], scratch, outputs=anywhere
    )
    return new_x.reshape(shape), new_v.reshape(shape)


def solution(mesh):
    return jax.shard_map(
        on_device,
        mesh=mesh,
        in_specs=(
            P("replica", None, "space"),
            P("replica", None, "space"),
            P("replica", "space"),
            P("replica", "space"),
            P("replica", None, "space"),
            P("replica", None, "space"),
            P("replica", None, "space"),
            P(),
            P("replica"),
            P("replica"),
            P(),
            P(),
            P(),
            P(),
            P(),
        ),
        out_specs=(P("replica", None, "space"), P("replica", None, "space")),
        check_vma=False,
    )
```

```python
import functools

import jax
import jax.numpy as jnp
from jax import lax
from jax.experimental import pallas as pl
from jax.experimental.pallas import tpu as pltpu
from jax.sharding import PartitionSpec as P

STEPS = 2
TIME_STEP = 0.05
CUT_SQ = 9.0
N_BASIS = 8
N_KIND = 6
LANES = 128
SLOTS = 32
GROUPS = SLOTS // 8
HIDDEN = 256
AHEAD = 4
SHARP = (N_BASIS / CUT_SQ) ** 2
CENTRES = [CUT_SQ * c / (N_BASIS - 1) for c in range(N_BASIS)]
F32 = jnp.float32
BF16 = jnp.bfloat16


def nt_dot(a, b):
    return lax.dot_general(a, b, (((1,), (1,)), ((), ())), preferred_element_type=F32)


def tn_dot(a, b):
    return lax.dot_general(a, b, (((0,), (0,)), ((), ())), preferred_element_type=F32)


def nn_dot(a, b):
    return lax.dot_general(a, b, (((1,), (0,)), ((), ())), preferred_element_type=F32)


def tile_of(flat_ref):
    rows = [
        flat_ref[:, (comp * 2 + chunk) * LANES : (comp * 2 + chunk + 1) * LANES]
        for chunk in range(2)
        for comp in range(3)
    ]
    return jnp.concatenate(rows, axis=0)


def put_flat(flat_ref, tile):
    for chunk in range(2):
        for comp in range(3):
            start = (comp * 2 + chunk) * LANES
            row = chunk * 3 + comp
            flat_ref[:, start : start + LANES] = tile[row : row + 1]


def rows_of_two(first, second, pad_with=None):
    shape = (3, LANES)
    pad = jnp.zeros((2, LANES), first.dtype)
    return jnp.concatenate(
        [jnp.broadcast_to(first, shape), jnp.broadcast_to(second, shape), pad], axis=0
    )


def take_lanes(table, lane):
    return jnp.take_along_axis(table, lane, axis=1, mode="promise_in_bounds")


def border_positions(tile, border0, border1):
    index = rows_of_two(border0, border1)
    pad = jnp.zeros((2, LANES), F32)
    low = jnp.concatenate([tile[0:3], tile[0:3], pad], axis=0)
    high = jnp.concatenate([tile[3:6], tile[3:6], pad], axis=0)
    lane = index & (LANES - 1)
    return jnp.where(index < LANES, take_lanes(low, lane), take_lanes(high, lane))


def four_sets(set0, set1, set2, set3):
    row = lax.broadcasted_iota(jnp.int32, (8, LANES), 0)
    col = lax.broadcasted_iota(jnp.int32, (8, LANES), 1)
    left = col < LANES // 2
    return jnp.where(row < 3, jnp.where(left, set0, set1), jnp.where(left, set2, set3))


def split_parts(value, count):
    parts = []
    for _ in range(count):
        part = value.astype(BF16).astype(F32)
        parts.append(part)
        value = value - part
    return parts


def bring(sources, targets, sems):
    copies = [
        pltpu.make_async_copy(source, target, sems.at[k])
        for k, (source, target) in enumerate(zip(sources, targets))
    ]
    for copy in copies:
        copy.start()
    for copy in copies:
        copy.wait()


def fed_columns():
    feature = lax.broadcasted_iota(jnp.int32, (28, LANES), 0)
    col = lax.broadcasted_iota(jnp.int32, (28, LANES), 1)
    block, which = col // 8, col % 8
    radial = (block < 8) & (feature == block)
    environ = (block == 8) & (feature == 8 + which)
    centre = (block == 9) & (which < N_KIND) & (feature == 16 + which)
    neigh = (block >= 10) & (feature == 22 + block - 10)
    return (radial | environ | centre | neigh).astype(F32)


def own_columns(slot, rows):
    col = lax.broadcasted_iota(jnp.int32, (rows, LANES), 1)
    return ((col // 8 == 8) | (col // 8 == 9) | (col % 8 == slot)).astype(F32)


def two_parts(value):
    high, low = split_parts(value, 2)
    return jnp.concatenate([high, low], axis=0).astype(BF16)


def begin_kernel(*refs):
    inputs, refs = refs[:13], refs[13:]
    (out_ref, up_ref, down_ref, line_ref, flat_ref, sum_ref, hot_ref, atom_ref, first_ref,
     second_ref, back_ref, index_ref, place_ref, total_ref, kind_ref, opening_ref), refs = (
        refs[:16], refs[16:]
    )
    x_ref, v_ref, border_ref, inertia_ref, intake_ref, edge_out_ref, middle_ref, atom_out_ref = (
        refs[:8]
    )
    landed = (
        x_ref, v_ref, kind_ref, border_ref, inertia_ref, index_ref, place_ref, total_ref,
        intake_ref, edge_out_ref, opening_ref, middle_ref, atom_out_ref,
    )
    bring(inputs, landed, refs[8])

    x_tile = tile_of(x_ref)
    border = border_ref[0]
    border0 = jnp.concatenate([border[0:1], border[1:2]], axis=1)
    border1 = jnp.concatenate([border[2:3], border[3:4]], axis=1)
    kind = kind_ref[...]
    inverse = jnp.zeros(kind.shape, F32)
    for k in range(N_KIND):
        inverse = jnp.where(kind == k, inertia_ref[k], inverse)
    out_ref[0:8] = border_positions(x_tile, border0, border1)
    out_ref[8:14] = x_tile
    out_ref[14:15] = inverse[:, :LANES]
    out_ref[15:16] = inverse[:, LANES:]
    out_ref[16:22] = tile_of(v_ref)
    out_ref[22:23] = border0.astype(F32)
    out_ref[23:24] = border1.astype(F32)

    place = lax.broadcasted_iota(jnp.int32, (LANES, 2 * LANES), 0).astype(F32).astype(BF16)
    one, none = jnp.asarray(1.0, BF16), jnp.asarray(0.0, BF16)

    def group(s, carry):
        for j in range(8):
            lane = (index_ref[0, pl.ds(s * 8 + j, 1), :] & (LANES - 1)).astype(F32)
            lane = jnp.broadcast_to(lane, (16, 2 * LANES)).astype(BF16)
            lane = jnp.concatenate([lane] * (LANES // 16), axis=0)
            cols = pl.ds(pl.multiple_of((s * 8 + j) * 2 * LANES, 2 * LANES), 2 * LANES)
            hot_ref[:, cols] = jnp.where(place == lane, one, none)
        return carry

    lax.fori_loop(0, GROUPS, group, 0)
    intake = intake_ref[...]
    fed = fed_columns()
    for j in range(8):
        up = (0.5 * fed * own_columns(j, 1)).astype(BF16)
        up_ref[j * HIDDEN : (j + 1) * HIDDEN, :] = tn_dot(intake, up).astype(BF16)
    edge_w = edge_out_ref[...]
    weighted = intake.astype(F32) * (0.5 * edge_w)
    down_ref[...] = two_parts(weighted[0:16])
    line = jnp.sum(weighted, axis=1, keepdims=True)
    flat_ref[...] = jnp.broadcast_to(line[0:16], (16, LANES))
    line = jnp.sum(fed * line, axis=0, keepdims=True)
    slot = lax.broadcasted_iota(jnp.int32, (8, LANES), 0)
    line_ref[...] = two_parts(own_columns(slot, 8) * line)
    sum_ref[...] = jnp.transpose(jnp.broadcast_to(edge_w, (LANES, HIDDEN)))
    atom_ref[...] = jnp.transpose(jnp.broadcast_to(0.5 * atom_out_ref[...], (LANES, HIDDEN)))
    first_ref[...] = jnp.transpose((0.5 * opening_ref[...]).astype(F32)).astype(BF16)
    second_ref[...] = 0.5 * middle_ref[...]
    back_ref[...] = jnp.transpose(middle_ref[...].astype(F32)).astype(BF16)


def far_tiles(far_ref):
    return far_ref[0, 0, 0], far_ref[0, 0, 1], far_ref[1, 1, 0], far_ref[1, 1, 1]


def force_kernel(
    where_ref,
    state_ref,
    near_ref,
    far_ref,
    up_ref,
    down_ref,
    line_ref,
    flat_ref,
    sum_ref,
    hot_ref,
    atom_ref,
    first_ref,
    second_ref,
    back_ref,
    index_ref,
    place_kind_ref,
    total_ref,
    kind_ref,
    opening_ref,
    out_ref,
    feat_ref,
    gauss_ref,
    geo_ref,
    energy_ref,
    gin0_ref,
    gin1_ref,
    *scratch,
):
    scat, ahead_ref = (scratch[:GROUPS], scratch[GROUPS : 2 * GROUPS]), scratch[2 * GROUPS]
    first_core = where_ref[0:1] == 0
    own = jnp.where(first_core, state_ref[0], state_ref[1])
    minus2, minus1, plus2, plus3 = far_tiles(far_ref)
    near0, near1 = near_ref[0], near_ref[1]

    def pick(a, b):
        return jnp.where(first_core, a, b)

    ghost = four_sets(
        pick(minus1, near0), pick(near1, plus2), pick(minus2, minus1), pick(plus2, plus3)
    )

    kind_rows = lax.broadcasted_iota(jnp.int32, (8, 2 * LANES), 0)
    centre_hot = (kind_rows == kind_ref[...]).astype(F32)
    slot_row = lax.broadcasted_iota(jnp.int32, (8, LANES), 0)
    tables = [
        [jnp.broadcast_to(t[r * 3 + c : r * 3 + c + 1], (8, LANES)) for c in range(3)]
        for t in (own, ghost)
        for r in range(2)
    ]

    def geometry(s, sums):
        sums = list(sums)
        slots = pl.ds(pl.multiple_of(s * 8, 8), 8)
        radials = [[], []]
        for h in range(2):
            cols = slice(h * LANES, (h + 1) * LANES)
            index = index_ref[0, slots, cols]
            lane = index & (LANES - 1)
            chunk = index // LANES
            dist_sq = None
            for comp in range(3):
                found = take_lanes(tables[0][comp], lane)
                for which in range(1, 4):
                    found = jnp.where(chunk == which, take_lanes(tables[which][comp], lane), found)
                vec = found - tables[h][comp]
                geo_ref[comp, s, :, cols] = vec
                dist_sq = vec * vec if comp == 0 else dist_sq + vec * vec
            live = slot_row + s * 8 < total_ref[:, cols]
            inside = 1.0 - dist_sq * (1.0 / CUT_SQ)
            used = live & (inside > 0.0)
            cutoff = jnp.where(used, inside * inside, 0.0)
            geo_ref[3, s, :, cols] = dist_sq
            geo_ref[4, s, :, cols] = cutoff
            geo_ref[5, s, :, cols] = jnp.where(used, inside * (-2.0 / CUT_SQ), 0.0)
            for c in range(N_BASIS):
                gap = dist_sq - CENTRES[c]
                gauss = jnp.exp(-SHARP * (gap * gap))
                gauss_ref[s, c * 8 : c * 8 + 8, cols] = gauss
                radial = gauss * cutoff
                radials[h].append(radial)
                sums[h * N_BASIS + c] = sums[h * N_BASIS + c] + radial
        place_kind = place_kind_ref[0, slots, :]
        rows = [jnp.concatenate([a, b], axis=1) for a, b in zip(*radials)]
        feat_ref[s, 0:64] = jnp.concatenate(rows, axis=0).astype(BF16)
        rows = [(place_kind == k).astype(F32) for k in range(N_KIND)]
        feat_ref[s, 80:128] = jnp.concatenate(rows, axis=0).astype(BF16)
        return tuple(sums)

    nothing = jnp.zeros((8, LANES), F32)
    sums = lax.fori_loop(0, GROUPS, geometry, (nothing,) * (2 * N_BASIS))
    rows = [jnp.sum(value, axis=0, keepdims=True) for value in sums]
    environ = jnp.concatenate(
        [jnp.concatenate(rows[:N_BASIS], axis=0), jnp.concatenate(rows[N_BASIS:], axis=0)], axis=1
    )
    shared = jnp.concatenate([environ, centre_hot], axis=0).astype(BF16)
    for s in range(GROUPS):
        feat_ref[s, 64:80] = shared

    atom_w = jnp.concatenate([atom_ref[...], atom_ref[...]], axis=1)
    half = nn_dot(first_ref[...], environ.astype(BF16))
    th = jnp.tanh(half)
    hidden_one = (half + half * th).astype(BF16)
    slope_one = 0.5 * (1.0 + th + half * (1.0 - th * th))
    half = nn_dot(second_ref[...], hidden_one)
    th = jnp.tanh(half)
    g_second = (atom_w * (1.0 + th + half * (1.0 - th * th))).astype(BF16)
    g_hidden = nn_dot(back_ref[...], g_second)
    g_first = (g_hidden * slope_one).astype(BF16)
    g_env = nn_dot(opening_ref[...], g_first)

    flat = jnp.concatenate([flat_ref[...], flat_ref[...]], axis=1)
    slot = lax.broadcasted_iota(jnp.int32, (16, HIDDEN), 0)
    quarter = lax.broadcasted_iota(jnp.int32, (16, HIDDEN), 1) // (HIDDEN // 4)
    members = [(slot == quarter + 4 * k).astype(F32).astype(BF16) for k in range(2)]

    def first_forward(s):
        ahead_ref[...] = nn_dot(up_ref[: AHEAD * HIDDEN, :], feat_ref[s])

    def group(s, g_env):
        feat = feat_ref[s]
        line = nn_dot(line_ref[...], feat)
        energy = line[0:8] + line[8:16]
        folded = []
        edge_w = sum_ref[...].astype(BF16)
        edge_w = jnp.concatenate([edge_w, edge_w], axis=1)

        def forward(k):
            many = nn_dot(up_ref[k * AHEAD * HIDDEN : (k + 1) * AHEAD * HIDDEN, :], feat)
            return [many[i * HIDDEN : (i + 1) * HIDDEN].astype(BF16) for i in range(AHEAD)]

        ahead = [ahead_ref[i * HIDDEN : (i + 1) * HIDDEN].astype(BF16) for i in range(AHEAD)]
        ahead += forward(1)
        for j in range(8):
            half = ahead.pop(0)
            if j == AHEAD:
                first_forward(jnp.minimum(s + 1, GROUPS - 1))
            th = jnp.tanh(half)
            rest = edge_w * (half * th)
            rest = rest[: HIDDEN // 2] + rest[HIDDEN // 2 :]
            folded.append(rest[: HIDDEN // 4] + rest[HIDDEN // 4 :])
            slope = th + half * (jnp.asarray(1.0, BF16) - th * th)
            g_in = nn_dot(down_ref[...], slope)
            cut = geo_ref[4, s, j : j + 1, :]
            g_in = (g_in[0:16] + g_in[16:32] + flat) * cut
            rows = pl.ds(s * 64 + j, 8, stride=8)
            gin0_ref[rows, :] = g_in[0:8, :LANES]
            gin1_ref[rows, :] = g_in[0:8, LANES:]
            g_env = g_env + g_in[8:16]
        for k in range(2):
            rest = jnp.concatenate(folded[k * 4 : k * 4 + 4], axis=0)
            energy = energy + nn_dot(members[k], rest)[0:8]
        energy_ref[s] = energy
        return g_env

    first_forward(0)
    g_env = lax.fori_loop(1, GROUPS, group, group(0, g_env))

    def backward(s, sums):
        sums = list(sums)
        slots = slice(s * 8, s * 8 + 8)
        for h in range(2):
            cols = slice(h * LANES, (h + 1) * LANES)
            dist_sq, cutoff, slope = (geo_ref[k, s, :, cols] for k in (3, 4, 5))
            g_cut = energy_ref[s, :, cols]
            g_gap = None
            gin = (gin0_ref, gin1_ref)[h]
            for c in range(N_BASIS):
                rows = slice(s * 64 + c * 8, s * 64 + c * 8 + 8)
                g_radial = gin[rows, :] + g_env[c : c + 1, cols]
                q = g_radial * gauss_ref[s, c * 8 : c * 8 + 8, cols]
                g_cut = g_cut + q
                moment = q * (dist_sq - CENTRES[c])
                g_gap = moment if g_gap is None else g_gap + moment
            g_dist = (-4.0 * SHARP) * (cutoff * g_gap) + 2.0 * (g_cut * slope)
            chunk = index_ref[0, slots, cols] // LANES
            target = scat[h][s]
            for comp in range(3):
                g_vec = g_dist * geo_ref[comp, s, :, cols]
                sums[h * 3 + comp] = sums[h * 3 + comp] + g_vec
                for part, value in enumerate(split_parts(g_vec, 2)):
                    for which in range(4):
                        row = part * 12 + which * 3 + comp
                        target[pl.ds(row, 8, stride=24), :] = jnp.where(chunk == which, value, 0.0)
        return tuple(sums)

    def scatter(s):
        lhs = []
        for j in range(8):
            rows = slice(j * 24, j * 24 + 24)
            lhs.append(jnp.concatenate([half[s][rows, :] for half in scat], axis=1).astype(BF16))
        return nt_dot(jnp.concatenate(lhs, axis=1), hot_ref[:, s * 16 * LANES : (s + 1) * 16 * LANES])

    sums, total = (nothing,) * 6, None
    for s in range(GROUPS):
        sums = backward(s, sums)
        part = scatter(s)
        total = part if total is None else total + part
    total = total[0:12] + total[12:24]
    centre = jnp.concatenate([jnp.sum(value, axis=0, keepdims=True) for value in sums], axis=0)
    pad = jnp.zeros((2, LANES), F32)
    out_ref[0:8] = jnp.concatenate([total[6:12], pad], axis=0)
    out_ref[8:16] = jnp.concatenate([total[0:6] - centre, pad], axis=0)


def returned_sum(returned, border0, border1):
    row = lax.broadcasted_iota(jnp.int32, (8, LANES), 0)
    place = lax.broadcasted_iota(jnp.int32, (LANES, LANES), 0)
    lhs, rhs = [], []
    for which, border in enumerate((border0, border1)):
        three = returned[which * 3 : which * 3 + 3]
        twice = jnp.concatenate([three, three, jnp.zeros((2, LANES), F32)], axis=0)
        meant = (border // LANES == 1) == (row >= 3)
        kept = jnp.where(meant, twice, 0.0)
        lhs.append(jnp.concatenate(split_parts(kept, 3), axis=0).astype(BF16))
        rhs.append((place == (border & (LANES - 1))).astype(F32).astype(BF16))
    total = nt_dot(jnp.concatenate(lhs, axis=1), jnp.concatenate(rhs, axis=1))
    return total[0:8] + total[8:16] + total[16:24]


def moved(state_ref, near_ref, far_ref):
    minus2, minus1, plus2, plus3 = far_tiles(far_ref)
    near0, near1 = near_ref[0, 0:8], near_ref[1, 0:8]
    sets = ((near1, minus1, plus2, minus2), (plus2, near0, plus3, minus1))
    result = []
    for domain in range(2):
        state = state_ref[domain]
        border0 = state[14:15].astype(jnp.int32)
        border1 = state[15:16].astype(jnp.int32)
        inverse = rows_of_two(state[6:7], state[7:8])
        grad = near_ref[domain, 8:16] + returned_sum(four_sets(*sets[domain]), border0, border1)
        speed = state[8:16] - TIME_STEP * grad * inverse
        place = state[0:8] + TIME_STEP * speed
        result.append((place, speed, border0, border1))
    return result


def step_kernel(state_ref, near_ref, far_ref, send_ref, next_ref):
    for domain, (place, speed, border0, border1) in enumerate(moved(state_ref, near_ref, far_ref)):
        send_ref[domain] = border_positions(place, border0, border1)
        next_ref[domain, 0:6] = place[0:6]
        next_ref[domain, 6:8] = state_ref[domain, 6:8]
        next_ref[domain, 8:14] = speed[0:6]
        next_ref[domain, 14:16] = state_ref[domain, 14:16]


def last_kernel(where_ref, state_ref, near_ref, far_ref, next_ref):
    for domain, (place, speed, _, _) in enumerate(moved(state_ref, near_ref, far_ref)):
        next_ref[domain, 0:6] = place[0:6]
        next_ref[domain, 6:8] = jnp.broadcast_to(where_ref[4:5], (2, LANES))
        next_ref[domain, 8:16] = speed


def swap_kernel(where_ref, own_ref, mate_ref, x_out, v_out, x_ref, v_ref, sems):
    core, swaps, side, position = (where_ref[k : k + 1] == 0 for k in range(4))

    def of_core(pair):
        return jnp.where(core, pair[0], pair[1])

    def of_side(s):
        return of_core(jnp.where(position, mate_ref[s, 0], mate_ref[s, 1]))

    mine = of_core(own_ref)
    chosen = jnp.where(swaps, mine, jnp.where(side, of_side(0), of_side(1)))
    scale = jnp.sqrt(mine[6:7] / chosen[6:7])
    put_flat(x_ref, chosen[0:6])
    put_flat(v_ref, chosen[8:14] * scale)
    bring((x_ref, v_ref), (x_out, v_out), sems)


def vmem():
    return pl.BlockSpec(memory_space=pltpu.VMEM)


def smem():
    return pl.BlockSpec(memory_space=pltpu.SMEM)


def tiles(*shape):
    return jax.ShapeDtypeStruct(shape + (LANES,), F32)


def call(kernel, scalars, arrays, out_shape, scratch=(), flops=10**6, inputs=None, outputs=None,
         limit=24 * 2**20):
    outputs = outputs or vmem
    out_specs = [outputs() for _ in out_shape] if isinstance(out_shape, list) else outputs()
    return pl.pallas_call(
        kernel,
        out_shape=out_shape,
        in_specs=[smem()] * len(scalars) + [(inputs or vmem)()] * len(arrays),
        out_specs=out_specs,
        scratch_shapes=list(scratch),
        cost_estimate=pl.CostEstimate(flops=flops, bytes_accessed=10**6, transcendentals=0),
        compiler_params=pltpu.CompilerParams(vmem_limit_bytes=limit),
    )(*scalars, *arrays)


def anywhere():
    return pl.BlockSpec(memory_space=pltpu.HBM)


def landing(arrays):
    return [pltpu.VMEM(a.shape, a.dtype) for a in arrays] + [pltpu.SemaphoreType.DMA((len(arrays),))]


def weight_shapes():
    return [
        jax.ShapeDtypeStruct((8 * HIDDEN, LANES), BF16),
        jax.ShapeDtypeStruct((32, HIDDEN), BF16),
        jax.ShapeDtypeStruct((16, LANES), BF16),
        tiles(16),
        tiles(HIDDEN),
        jax.ShapeDtypeStruct((LANES, SLOTS * 2 * LANES), BF16),
        tiles(HIDDEN),
        jax.ShapeDtypeStruct((HIDDEN, N_BASIS), BF16),
        jax.ShapeDtypeStruct((HIDDEN, HIDDEN), BF16),
        jax.ShapeDtypeStruct((HIDDEN, HIDDEN), BF16),
    ]


def begin_shapes(arrays):
    through = [jax.ShapeDtypeStruct(arrays[k].shape, arrays[k].dtype) for k in (5, 6, 7, 2, 10)]
    space = landing([arrays[k] for k in (0, 1, 3, 4, 8, 9, 11, 12)])
    space[3] = pltpu.SMEM(arrays[4].shape, F32)
    space[-1] = pltpu.SemaphoreType.DMA((len(arrays),))
    made = [tiles(24)] + weight_shapes() + through
    return made, space


def force_scratch():
    return [
        pltpu.VMEM((GROUPS, 128, 2 * LANES), BF16),
        pltpu.VMEM((GROUPS, 64, 2 * LANES), F32),
        pltpu.VMEM((6, GROUPS, 8, 2 * LANES), F32),
        pltpu.VMEM((GROUPS, 8, 2 * LANES), F32),
        pltpu.VMEM((GROUPS * 64, LANES), F32),
        pltpu.VMEM((GROUPS * 64, LANES), F32),
    ] + [pltpu.VMEM((8 * 24, LANES), F32)] * (2 * GROUPS) + [pltpu.VMEM((AHEAD * HIDDEN, 2 * LANES), F32)]


def on_chip(value, domains):
    groups = [[2 * i, 2 * i + 1] for i in range(domains // 2)]
    return lax.all_gather(value, "space", axis_index_groups=groups)


def across_chips(value, domains):
    groups = [[(2 * i - 1) % domains, 2 * i] for i in range(domains // 2)]
    return lax.all_gather(value, "space", axis_index_groups=groups)


def along_ladder(value, rungs, domains):
    groups = []
    for domain in range(domains):
        shift = domain % 2
        for low in range(shift, rungs - shift, 2):
            groups.append([low * domains + domain, (low + 1) * domains + domain])
        if shift and domain // 2 % 2 == 0:
            for end in (0, rungs - 1):
                groups.append([end * domains + domain, end * domains + domain + 2])
    return lax.all_gather(value, ("replica", "space"), axis_index_groups=groups)


def on_device(
    particle_coordinates,
    particle_motions,
    particle_kinds,
    filled_totals,
    adjacent_particles,
    adjacent_place_kinds,
    border_particle_numbers,
    reciprocal_kind_inertia,
    thermal_levels,
    swap_mates,
    bond_intake_coefficients,
    bond_output_coefficients,
    particle_opening_coefficients,
    particle_middle_coefficients,
    particle_output_coefficients,
):
    domains, rungs = lax.axis_size("space"), lax.axis_size("replica")
    core = lax.axis_index("space") % 2
    rank = lax.axis_index("replica")
    mate = swap_mates[0]
    odd = rank % 2
    side = jnp.where((mate > rank) == (odd == 0), 0, 1)
    position = jnp.where(side == 0, 1 - odd, odd)
    where_to = [value.astype(F32) for value in (core, mate != rank, side, position)]
    where_to = jnp.stack(where_to + [thermal_levels[0]])
    where_to = jnp.broadcast_to(where_to[:, None], (5, LANES))

    arrays = (
        particle_coordinates.reshape(1, -1),
        particle_motions.reshape(1, -1),
        particle_kinds,
        border_particle_numbers,
        reciprocal_kind_inertia,
        adjacent_particles,
        adjacent_place_kinds,
        filled_totals,
        bond_intake_coefficients.T,
        bond_output_coefficients[None],
        particle_opening_coefficients.T,
        particle_middle_coefficients,
        particle_output_coefficients[None],
    )
    arrays = tuple(pltpu.with_memory_space_constraint(a, pltpu.HBM) for a in arrays)
    made, space = begin_shapes(arrays)
    begin, *fixed = call(begin_kernel, (), arrays, made, space, inputs=anywhere)
    both = on_chip(begin, domains)
    send, state = both[:, 0:8], both[:, 8:24]
    for step in range(STEPS):
        far = on_chip(across_chips(send, domains), domains)
        partial = call(
            force_kernel,
            (),
            (
                where_to,
                state,
                send,
                far,
                *fixed,
            ),
            tiles(16),
            force_scratch(),
        )
        near = on_chip(partial, domains)
        far = on_chip(across_chips(near[:, 0:8], domains), domains)
        if step < STEPS - 1:
            send, state = call(step_kernel, (), (state, near, far), [tiles(2, 8), tiles(2, 16)])
        else:
            state = call(last_kernel, (), (where_to, state, near, far), tiles(2, 16))
    mates = on_chip(along_ladder(state, rungs, domains), domains)
    shape = particle_coordinates.shape
    out = jax.ShapeDtypeStruct((1, particle_coordinates.size), F32)
    scratch = landing((out, out))
    new_x, new_v = call(
        swap_kernel, (), (where_to, state, mates), [out, out], scratch, outputs=anywhere
    )
    return new_x.reshape(shape), new_v.reshape(shape)


def solution(mesh):
    return jax.shard_map(
        on_device,
        mesh=mesh,
        in_specs=(
            P("replica", None, "space"),
            P("replica", None, "space"),
            P("replica", "space"),
            P("replica", "space"),
            P("replica", None, "space"),
            P("replica", None, "space"),
            P("replica", None, "space"),
            P(),
            P("replica"),
            P("replica"),
            P(),
            P(),
            P(),
            P(),
            P(),
        ),
        out_specs=(P("replica", None, "space"), P("replica", None, "space")),
        check_vma=False,
    )
```

```python
import functools

import jax
import jax.numpy as jnp
from jax import lax
from jax.experimental import pallas as pl
from jax.experimental.pallas import tpu as pltpu
from jax.sharding import PartitionSpec as P

STEPS = 2
TIME_STEP = 0.05
CUT_SQ = 9.0
N_BASIS = 8
N_KIND = 6
LANES = 128
SLOTS = 32
GROUPS = SLOTS // 8
HIDDEN = 256
AHEAD = 4
SHARP = (N_BASIS / CUT_SQ) ** 2
CENTRES = [CUT_SQ * c / (N_BASIS - 1) for c in range(N_BASIS)]
F32 = jnp.float32
BF16 = jnp.bfloat16


def nt_dot(a, b):
    return lax.dot_general(a, b, (((1,), (1,)), ((), ())), preferred_element_type=F32)


def tn_dot(a, b):
    return lax.dot_general(a, b, (((0,), (0,)), ((), ())), preferred_element_type=F32)


def nn_dot(a, b):
    return lax.dot_general(a, b, (((1,), (0,)), ((), ())), preferred_element_type=F32)


def tile_of(flat_ref):
    rows = [
        flat_ref[:, (comp * 2 + chunk) * LANES : (comp * 2 + chunk + 1) * LANES]
        for chunk in range(2)
        for comp in range(3)
    ]
    return jnp.concatenate(rows, axis=0)


def put_flat(flat_ref, tile):
    for chunk in range(2):
        for comp in range(3):
            start = (comp * 2 + chunk) * LANES
            row = chunk * 3 + comp
            flat_ref[:, start : start + LANES] = tile[row : row + 1]


def rows_of_two(first, second, pad_with=None):
    shape = (3, LANES)
    pad = jnp.zeros((2, LANES), first.dtype)
    return jnp.concatenate(
        [jnp.broadcast_to(first, shape), jnp.broadcast_to(second, shape), pad], axis=0
    )


def take_lanes(table, lane):
    return jnp.take_along_axis(table, lane, axis=1, mode="promise_in_bounds")


def border_positions(tile, border0, border1):
    index = rows_of_two(border0, border1)
    pad = jnp.zeros((2, LANES), F32)
    low = jnp.concatenate([tile[0:3], tile[0:3], pad], axis=0)
    high = jnp.concatenate([tile[3:6], tile[3:6], pad], axis=0)
    lane = index & (LANES - 1)
    return jnp.where(index < LANES, take_lanes(low, lane), take_lanes(high, lane))


def four_sets(set0, set1, set2, set3):
    row = lax.broadcasted_iota(jnp.int32, (8, LANES), 0)
    col = lax.broadcasted_iota(jnp.int32, (8, LANES), 1)
    left = col < LANES // 2
    return jnp.where(row < 3, jnp.where(left, set0, set1), jnp.where(left, set2, set3))


def split_parts(value, count):
    parts = []
    for _ in range(count):
        part = value.astype(BF16).astype(F32)
        parts.append(part)
        value = value - part
    return parts


def bring(sources, targets, sems):
    copies = [
        pltpu.make_async_copy(source, target, sems.at[k])
        for k, (source, target) in enumerate(zip(sources, targets))
    ]
    for copy in copies:
        copy.start()
    for copy in copies:
        copy.wait()


def fed_columns():
    feature = lax.broadcasted_iota(jnp.int32, (28, LANES), 0)
    col = lax.broadcasted_iota(jnp.int32, (28, LANES), 1)
    block, which = col // 8, col % 8
    radial = (block < 8) & (feature == block)
    environ = (block == 8) & (feature == 8 + which)
    centre = (block == 9) & (which < N_KIND) & (feature == 16 + which)
    neigh = (block >= 10) & (feature == 22 + block - 10)
    return (radial | environ | centre | neigh).astype(F32)


def own_columns(slot, rows):
    col = lax.broadcasted_iota(jnp.int32, (rows, LANES), 1)
    return ((col // 8 == 8) | (col // 8 == 9) | (col % 8 == slot)).astype(F32)


def two_parts(value):
    high, low = split_parts(value, 2)
    return jnp.concatenate([high, low], axis=0).astype(BF16)


def start_kernel(x_in, v_in, kind_in, border_in, inertia_in, out_ref, *scratch):
    x_ref, v_ref, kind_ref, border_ref, inertia_ref, sems = scratch
    bring((x_in, v_in, kind_in, border_in, inertia_in), scratch[:-1], sems)
    x_tile = tile_of(x_ref)
    border = border_ref[0]
    border0 = jnp.concatenate([border[0:1], border[1:2]], axis=1)
    border1 = jnp.concatenate([border[2:3], border[3:4]], axis=1)
    kind = kind_ref[...]
    inverse = jnp.zeros(kind.shape, F32)
    for k in range(N_KIND):
        inverse = jnp.where(kind == k, inertia_ref[k], inverse)
    out_ref[0:8] = border_positions(x_tile, border0, border1)
    out_ref[8:14] = x_tile
    out_ref[14:15] = inverse[:, :LANES]
    out_ref[15:16] = inverse[:, LANES:]
    out_ref[16:22] = tile_of(v_ref)
    out_ref[22:23] = border0.astype(F32)
    out_ref[23:24] = border1.astype(F32)


def weight_kernel(*refs):
    inputs, refs = refs[:9], refs[9:]
    (up_ref, down_ref, line_ref, flat_ref, sum_ref, hot_ref, atom_ref, first_ref,
     second_ref, back_ref, index_ref, place_ref, total_ref, kind_ref, opening_ref), refs = (
        refs[:15], refs[15:]
    )
    intake_ref, edge_out_ref, middle_ref, atom_out_ref, sems = refs
    landed = (
        index_ref, place_ref, total_ref, kind_ref, opening_ref, intake_ref, edge_out_ref,
        middle_ref, atom_out_ref,
    )
    bring(inputs, landed, sems)
    place = lax.broadcasted_iota(jnp.int32, (LANES, 2 * LANES), 0).astype(F32).astype(BF16)
    one, none = jnp.asarray(1.0, BF16), jnp.asarray(0.0, BF16)

    def group(s, carry):
        for j in range(8):
            lane = (index_ref[0, pl.ds(s * 8 + j, 1), :] & (LANES - 1)).astype(F32)
            lane = jnp.broadcast_to(lane, (16, 2 * LANES)).astype(BF16)
            lane = jnp.concatenate([lane] * (LANES // 16), axis=0)
            cols = pl.ds(pl.multiple_of((s * 8 + j) * 2 * LANES, 2 * LANES), 2 * LANES)
            hot_ref[:, cols] = jnp.where(place == lane, one, none)
        return carry

    lax.fori_loop(0, GROUPS, group, 0)
    intake = intake_ref[...]
    fed = fed_columns()
    for j in range(8):
        up = (0.5 * fed * own_columns(j, 1)).astype(BF16)
        up_ref[j * HIDDEN : (j + 1) * HIDDEN, :] = tn_dot(intake, up).astype(BF16)
    edge_w = edge_out_ref[...]
    weighted = intake.astype(F32) * (0.5 * edge_w)
    down_ref[...] = two_parts(weighted[0:16])
    line = jnp.sum(weighted, axis=1, keepdims=True)
    flat_ref[...] = jnp.broadcast_to(line[0:16], (16, LANES))
    line = jnp.sum(fed * line, axis=0, keepdims=True)
    slot = lax.broadcasted_iota(jnp.int32, (8, LANES), 0)
    line_ref[...] = two_parts(own_columns(slot, 8) * line)
    sum_ref[...] = jnp.transpose(jnp.broadcast_to(edge_w, (LANES, HIDDEN)))
    atom_ref[...] = jnp.transpose(jnp.broadcast_to(0.5 * atom_out_ref[...], (LANES, HIDDEN)))
    first_ref[...] = jnp.transpose((0.5 * opening_ref[...]).astype(F32)).astype(BF16)
    second_ref[...] = 0.5 * middle_ref[...]
    back_ref[...] = jnp.transpose(middle_ref[...].astype(F32)).astype(BF16)


def far_tiles(far_ref):
    if len(far_ref.shape) == 4:
        return far_ref[0, 0], far_ref[0, 1], far_ref[1, 0], far_ref[1, 1]
    return far_ref[0, 0, 0], far_ref[0, 0, 1], far_ref[1, 1, 0], far_ref[1, 1, 1]


def force_kernel(
    where_ref,
    state_ref,
    near_ref,
    far_ref,
    up_ref,
    down_ref,
    line_ref,
    flat_ref,
    sum_ref,
    hot_ref,
    atom_ref,
    first_ref,
    second_ref,
    back_ref,
    index_ref,
    place_kind_ref,
    total_ref,
    kind_ref,
    opening_ref,
    out_ref,
    feat_ref,
    gauss_ref,
    geo_ref,
    energy_ref,
    gin0_ref,
    gin1_ref,
    *scratch,
):
    scat, ahead_ref = (scratch[:GROUPS], scratch[GROUPS : 2 * GROUPS]), scratch[2 * GROUPS]
    first_core = where_ref[0:1] == 0
    own = jnp.where(first_core, state_ref[0], state_ref[1])
    minus2, minus1, plus2, plus3 = far_tiles(far_ref)
    near0, near1 = near_ref[0], near_ref[1]

    def pick(a, b):
        return jnp.where(first_core, a, b)

    ghost = four_sets(
        pick(minus1, near0), pick(near1, plus2), pick(minus2, minus1), pick(plus2, plus3)
    )

    kind_rows = lax.broadcasted_iota(jnp.int32, (8, 2 * LANES), 0)
    centre_hot = (kind_rows == kind_ref[...]).astype(F32)
    slot_row = lax.broadcasted_iota(jnp.int32, (8, LANES), 0)
    tables = [
        [jnp.broadcast_to(t[r * 3 + c : r * 3 + c + 1], (8, LANES)) for c in range(3)]
        for t in (own, ghost)
        for r in range(2)
    ]

    def geometry(s, sums):
        sums = list(sums)
        slots = pl.ds(pl.multiple_of(s * 8, 8), 8)
        radials = [[], []]
        for h in range(2):
            cols = slice(h * LANES, (h + 1) * LANES)
            index = index_ref[0, slots, cols]
            lane = index & (LANES - 1)
            chunk = index // LANES
            dist_sq = None
            for comp in range(3):
                found = take_lanes(tables[0][comp], lane)
                for which in range(1, 4):
                    found = jnp.where(chunk == which, take_lanes(tables[which][comp], lane), found)
                vec = found - tables[h][comp]
                geo_ref[comp, s, :, cols] = vec
                dist_sq = vec * vec if comp == 0 else dist_sq + vec * vec
            live = slot_row + s * 8 < total_ref[:, cols]
            inside = 1.0 - dist_sq * (1.0 / CUT_SQ)
            used = live & (inside > 0.0)
            cutoff = jnp.where(used, inside * inside, 0.0)
            geo_ref[3, s, :, cols] = dist_sq
            geo_ref[4, s, :, cols] = cutoff
            geo_ref[5, s, :, cols] = jnp.where(used, inside * (-2.0 / CUT_SQ), 0.0)
            for c in range(N_BASIS):
                gap = dist_sq - CENTRES[c]
                gauss = jnp.exp(-SHARP * (gap * gap))
                gauss_ref[s, c * 8 : c * 8 + 8, cols] = gauss
                radial = gauss * cutoff
                radials[h].append(radial)
                sums[h * N_BASIS + c] = sums[h * N_BASIS + c] + radial
        place_kind = place_kind_ref[0, slots, :]
        rows = [jnp.concatenate([a, b], axis=1) for a, b in zip(*radials)]
        feat_ref[s, 0:64] = jnp.concatenate(rows, axis=0).astype(BF16)
        rows = [(place_kind == k).astype(F32) for k in range(N_KIND)]
        feat_ref[s, 80:128] = jnp.concatenate(rows, axis=0).astype(BF16)
        return tuple(sums)

    nothing = jnp.zeros((8, LANES), F32)
    sums = lax.fori_loop(0, GROUPS, geometry, (nothing,) * (2 * N_BASIS))
    rows = [jnp.sum(value, axis=0, keepdims=True) for value in sums]
    environ = jnp.concatenate(
        [jnp.concatenate(rows[:N_BASIS], axis=0), jnp.concatenate(rows[N_BASIS:], axis=0)], axis=1
    )
    shared = jnp.concatenate([environ, centre_hot], axis=0).astype(BF16)
    for s in range(GROUPS):
        feat_ref[s, 64:80] = shared

    atom_w = jnp.concatenate([atom_ref[...], atom_ref[...]], axis=1)
    half = nn_dot(first_ref[...], environ.astype(BF16))
    th = jnp.tanh(half)
    hidden_one = (half + half * th).astype(BF16)
    slope_one = 0.5 * (1.0 + th + half * (1.0 - th * th))
    half = nn_dot(second_ref[...], hidden_one)
    th = jnp.tanh(half)
    g_second = (atom_w * (1.0 + th + half * (1.0 - th * th))).astype(BF16)
    g_hidden = nn_dot(back_ref[...], g_second)
    g_first = (g_hidden * slope_one).astype(BF16)
    g_env = nn_dot(opening_ref[...], g_first)

    flat = jnp.concatenate([flat_ref[...], flat_ref[...]], axis=1)
    slot = lax.broadcasted_iota(jnp.int32, (16, HIDDEN), 0)
    quarter = lax.broadcasted_iota(jnp.int32, (16, HIDDEN), 1) // (HIDDEN // 4)
    members = [(slot == quarter + 4 * k).astype(F32).astype(BF16) for k in range(2)]

    def first_forward(s):
        ahead_ref[...] = nn_dot(up_ref[: AHEAD * HIDDEN, :], feat_ref[s])

    def group(s, g_env):
        feat = feat_ref[s]
        line = nn_dot(line_ref[...], feat)
        energy = line[0:8] + line[8:16]
        folded = []
        edge_w = sum_ref[...].astype(BF16)
        edge_w = jnp.concatenate([edge_w, edge_w], axis=1)

        def forward(k):
            many = nn_dot(up_ref[k * AHEAD * HIDDEN : (k + 1) * AHEAD * HIDDEN, :], feat)
            return [many[i * HIDDEN : (i + 1) * HIDDEN].astype(BF16) for i in range(AHEAD)]

        ahead = [ahead_ref[i * HIDDEN : (i + 1) * HIDDEN].astype(BF16) for i in range(AHEAD)]
        ahead += forward(1)
        for j in range(8):
            half = ahead.pop(0)
            if j == AHEAD:
                first_forward(jnp.minimum(s + 1, GROUPS - 1))
            th = jnp.tanh(half)
            rest = edge_w * (half * th)
            rest = rest[: HIDDEN // 2] + rest[HIDDEN // 2 :]
            folded.append(rest[: HIDDEN // 4] + rest[HIDDEN // 4 :])
            slope = th + half * (jnp.asarray(1.0, BF16) - th * th)
            g_in = nn_dot(down_ref[...], slope)
            cut = geo_ref[4, s, j : j + 1, :]
            g_in = (g_in[0:16] + g_in[16:32] + flat) * cut
            rows = pl.ds(s * 64 + j, 8, stride=8)
            gin0_ref[rows, :] = g_in[0:8, :LANES]
            gin1_ref[rows, :] = g_in[0:8, LANES:]
            g_env = g_env + g_in[8:16]
        for k in range(2):
            rest = jnp.concatenate(folded[k * 4 : k * 4 + 4], axis=0)
            energy = energy + nn_dot(members[k], rest)[0:8]
        energy_ref[s] = energy
        return g_env

    first_forward(0)
    g_env = lax.fori_loop(1, GROUPS, group, group(0, g_env))

    def backward(s, sums):
        sums = list(sums)
        slots = slice(s * 8, s * 8 + 8)
        for h in range(2):
            cols = slice(h * LANES, (h + 1) * LANES)
            dist_sq, cutoff, slope = (geo_ref[k, s, :, cols] for k in (3, 4, 5))
            g_cut = energy_ref[s, :, cols]
            g_gap = None
            gin = (gin0_ref, gin1_ref)[h]
            for c in range(N_BASIS):
                rows = slice(s * 64 + c * 8, s * 64 + c * 8 + 8)
                g_radial = gin[rows, :] + g_env[c : c + 1, cols]
                q = g_radial * gauss_ref[s, c * 8 : c * 8 + 8, cols]
                g_cut = g_cut + q
                moment = q * (dist_sq - CENTRES[c])
                g_gap = moment if g_gap is None else g_gap + moment
            g_dist = (-4.0 * SHARP) * (cutoff * g_gap) + 2.0 * (g_cut * slope)
            chunk = index_ref[0, slots, cols] // LANES
            target = scat[h][s]
            for comp in range(3):
                g_vec = g_dist * geo_ref[comp, s, :, cols]
                sums[h * 3 + comp] = sums[h * 3 + comp] + g_vec
                for part, value in enumerate(split_parts(g_vec, 2)):
                    for which in range(4):
                        row = part * 12 + which * 3 + comp
                        target[pl.ds(row, 8, stride=24), :] = jnp.where(chunk == which, value, 0.0)
        return tuple(sums)

    def scatter(s):
        lhs = []
        for j in range(8):
            rows = slice(j * 24, j * 24 + 24)
            lhs.append(jnp.concatenate([half[s][rows, :] for half in scat], axis=1).astype(BF16))
        return nt_dot(jnp.concatenate(lhs, axis=1), hot_ref[:, s * 16 * LANES : (s + 1) * 16 * LANES])

    sums, total = (nothing,) * 6, None
    for s in range(GROUPS):
        sums = backward(s, sums)
        part = scatter(s)
        total = part if total is None else total + part
    total = total[0:12] + total[12:24]
    centre = jnp.concatenate([jnp.sum(value, axis=0, keepdims=True) for value in sums], axis=0)
    pad = jnp.zeros((2, LANES), F32)
    out_ref[0:8] = jnp.concatenate([total[6:12], pad], axis=0)
    out_ref[8:16] = jnp.concatenate([total[0:6] - centre, pad], axis=0)


def returned_sum(returned, border0, border1):
    row = lax.broadcasted_iota(jnp.int32, (8, LANES), 0)
    place = lax.broadcasted_iota(jnp.int32, (LANES, LANES), 0)
    lhs, rhs = [], []
    for which, border in enumerate((border0, border1)):
        three = returned[which * 3 : which * 3 + 3]
        twice = jnp.concatenate([three, three, jnp.zeros((2, LANES), F32)], axis=0)
        meant = (border // LANES == 1) == (row >= 3)
        kept = jnp.where(meant, twice, 0.0)
        lhs.append(jnp.concatenate(split_parts(kept, 3), axis=0).astype(BF16))
        rhs.append((place == (border & (LANES - 1))).astype(F32).astype(BF16))
    total = nt_dot(jnp.concatenate(lhs, axis=1), jnp.concatenate(rhs, axis=1))
    return total[0:8] + total[8:16] + total[16:24]


def moved(state_ref, near_ref, far_ref):
    minus2, minus1, plus2, plus3 = far_tiles(far_ref)
    near0, near1 = near_ref[0, 0:8], near_ref[1, 0:8]
    sets = ((near1, minus1, plus2, minus2), (plus2, near0, plus3, minus1))
    result = []
    for domain in range(2):
        state = state_ref[domain]
        border0 = state[14:15].astype(jnp.int32)
        border1 = state[15:16].astype(jnp.int32)
        inverse = rows_of_two(state[6:7], state[7:8])
        grad = near_ref[domain, 8:16] + returned_sum(four_sets(*sets[domain]), border0, border1)
        speed = state[8:16] - TIME_STEP * grad * inverse
        place = state[0:8] + TIME_STEP * speed
        result.append((place, speed, border0, border1))
    return result


def step_kernel(state_ref, near_ref, far_ref, send_ref, next_ref):
    for domain, (place, speed, border0, border1) in enumerate(moved(state_ref, near_ref, far_ref)):
        send_ref[domain] = border_positions(place, border0, border1)
        next_ref[domain, 0:6] = place[0:6]
        next_ref[domain, 6:8] = state_ref[domain, 6:8]
        next_ref[domain, 8:14] = speed[0:6]
        next_ref[domain, 14:16] = state_ref[domain, 14:16]


def last_kernel(where_ref, state_ref, near_ref, far_ref, next_ref):
    for domain, (place, speed, _, _) in enumerate(moved(state_ref, near_ref, far_ref)):
        next_ref[domain, 0:6] = place[0:6]
        next_ref[domain, 6:8] = jnp.broadcast_to(where_ref[4:5], (2, LANES))
        next_ref[domain, 8:16] = speed


def swap_kernel(where_ref, own_ref, mate_ref, x_out, v_out, x_ref, v_ref, sems):
    core, swaps, side, position = (where_ref[k : k + 1] == 0 for k in range(4))

    def of_core(pair):
        return jnp.where(core, pair[0], pair[1])

    def of_side(s):
        return of_core(jnp.where(position, mate_ref[s, 0], mate_ref[s, 1]))

    mine = of_core(own_ref)
    chosen = jnp.where(swaps, mine, jnp.where(side, of_side(0), of_side(1)))
    scale = jnp.sqrt(mine[6:7] / chosen[6:7])
    put_flat(x_ref, chosen[0:6])
    put_flat(v_ref, chosen[8:14] * scale)
    bring((x_ref, v_ref), (x_out, v_out), sems)


def vmem():
    return pl.BlockSpec(memory_space=pltpu.VMEM)


def smem():
    return pl.BlockSpec(memory_space=pltpu.SMEM)


def tiles(*shape):
    return jax.ShapeDtypeStruct(shape + (LANES,), F32)


def call(kernel, scalars, arrays, out_shape, scratch=(), flops=10**6, inputs=None, outputs=None,
         limit=24 * 2**20):
    outputs = outputs or vmem
    out_specs = [outputs() for _ in out_shape] if isinstance(out_shape, list) else outputs()
    return pl.pallas_call(
        kernel,
        out_shape=out_shape,
        in_specs=[smem()] * len(scalars) + [(inputs or vmem)()] * len(arrays),
        out_specs=out_specs,
        scratch_shapes=list(scratch),
        cost_estimate=pl.CostEstimate(flops=flops, bytes_accessed=10**6, transcendentals=0),
        compiler_params=pltpu.CompilerParams(vmem_limit_bytes=limit),
    )(*scalars, *arrays)


def anywhere():
    return pl.BlockSpec(memory_space=pltpu.HBM)


def pinned(*arrays):
    return tuple(pltpu.with_memory_space_constraint(a, pltpu.HBM) for a in arrays)


def landing(arrays):
    return [pltpu.VMEM(a.shape, a.dtype) for a in arrays] + [pltpu.SemaphoreType.DMA((len(arrays),))]


def weight_shapes():
    return [
        jax.ShapeDtypeStruct((8 * HIDDEN, LANES), BF16),
        jax.ShapeDtypeStruct((32, HIDDEN), BF16),
        jax.ShapeDtypeStruct((16, LANES), BF16),
        tiles(16),
        tiles(HIDDEN),
        jax.ShapeDtypeStruct((LANES, SLOTS * 2 * LANES), BF16),
        tiles(HIDDEN),
        jax.ShapeDtypeStruct((HIDDEN, N_BASIS), BF16),
        jax.ShapeDtypeStruct((HIDDEN, HIDDEN), BF16),
        jax.ShapeDtypeStruct((HIDDEN, HIDDEN), BF16),
    ]


def weight_parts(arrays):
    through = [jax.ShapeDtypeStruct(a.shape, a.dtype) for a in arrays[:5]]
    space = landing(arrays[5:])
    space[-1] = pltpu.SemaphoreType.DMA((len(arrays),))
    return weight_shapes() + through, space


def force_scratch():
    return [
        pltpu.VMEM((GROUPS, 128, 2 * LANES), BF16),
        pltpu.VMEM((GROUPS, 64, 2 * LANES), F32),
        pltpu.VMEM((6, GROUPS, 8, 2 * LANES), F32),
        pltpu.VMEM((GROUPS, 8, 2 * LANES), F32),
        pltpu.VMEM((GROUPS * 64, LANES), F32),
        pltpu.VMEM((GROUPS * 64, LANES), F32),
    ] + [pltpu.VMEM((8 * 24, LANES), F32)] * (2 * GROUPS) + [pltpu.VMEM((AHEAD * HIDDEN, 2 * LANES), F32)]


def on_chip(value, domains):
    groups = [[2 * i, 2 * i + 1] for i in range(domains // 2)]
    return lax.all_gather(value, "space", axis_index_groups=groups)


def across_chips(value, domains):
    groups = [[(2 * i - 1) % domains, 2 * i] for i in range(domains // 2)]
    return lax.all_gather(value, "space", axis_index_groups=groups)


def partner_across(value, domains):
    pairs = []
    for i in range(domains // 2):
        odd, even = (2 * i - 1) % domains, 2 * i
        pairs += [(odd, even), (even, odd)]
    return lax.ppermute(value, "space", pairs)


def along_ladder(value, rungs, domains):
    groups = []
    for domain in range(domains):
        shift = domain % 2
        for low in range(shift, rungs - shift, 2):
            groups.append([low * domains + domain, (low + 1) * domains + domain])
        if shift and domain // 2 % 2 == 0:
            for end in (0, rungs - 1):
                groups.append([end * domains + domain, end * domains + domain + 2])
    return lax.all_gather(value, ("replica", "space"), axis_index_groups=groups)


def on_device(
    particle_coordinates,
    particle_motions,
    particle_kinds,
    filled_totals,
    adjacent_particles,
    adjacent_place_kinds,
    border_particle_numbers,
    reciprocal_kind_inertia,
    thermal_levels,
    swap_mates,
    bond_intake_coefficients,
    bond_output_coefficients,
    particle_opening_coefficients,
    particle_middle_coefficients,
    particle_output_coefficients,
):
    domains, rungs = lax.axis_size("space"), lax.axis_size("replica")
    core = lax.axis_index("space") % 2
    rank = lax.axis_index("replica")
    mate = swap_mates[0]
    odd = rank % 2
    side = jnp.where((mate > rank) == (odd == 0), 0, 1)
    position = jnp.where(side == 0, 1 - odd, odd)
    where_to = [value.astype(F32) for value in (core, mate != rank, side, position)]
    where_to = jnp.stack(where_to + [thermal_levels[0]])
    where_to = jnp.broadcast_to(where_to[:, None], (5, LANES))

    arrays = pinned(
        particle_coordinates.reshape(1, -1),
        particle_motions.reshape(1, -1),
        particle_kinds,
        border_particle_numbers,
        reciprocal_kind_inertia,
    )
    space = landing(arrays)
    space[4] = pltpu.SMEM(reciprocal_kind_inertia.shape, F32)
    begin = call(start_kernel, (), arrays, tiles(24), space, inputs=anywhere)
    arrays = pinned(
        adjacent_particles,
        adjacent_place_kinds,
        filled_totals,
        particle_kinds,
        particle_opening_coefficients.T,
        bond_intake_coefficients.T,
        bond_output_coefficients[None],
        particle_middle_coefficients,
        particle_output_coefficients[None],
    )
    made, space = weight_parts(arrays)
    fixed = call(weight_kernel, (), arrays, made, space, 10**9, inputs=anywhere)
    both = on_chip(begin, domains)
    send, state = both[:, 0:8], both[:, 8:24]
    for step in range(STEPS):
        across = partner_across if step == 0 else across_chips
        far = on_chip(across(send, domains), domains)
        partial = call(
            force_kernel,
            (),
            (
                where_to,
                state,
                send,
                far,
                *fixed,
            ),
            tiles(16),
            force_scratch(),
        )
        near = on_chip(partial, domains)
        far = on_chip(across_chips(near[:, 0:8], domains), domains)
        if step < STEPS - 1:
            send, state = call(step_kernel, (), (state, near, far), [tiles(2, 8), tiles(2, 16)])
        else:
            state = call(last_kernel, (), (where_to, state, near, far), tiles(2, 16))
    mates = on_chip(along_ladder(state, rungs, domains), domains)
    shape = particle_coordinates.shape
    out = jax.ShapeDtypeStruct((1, particle_coordinates.size), F32)
    scratch = landing((out, out))
    new_x, new_v = call(
        swap_kernel, (), (where_to, state, mates), [out, out], scratch, outputs=anywhere
    )
    return new_x.reshape(shape), new_v.reshape(shape)


def solution(mesh):
    return jax.shard_map(
        on_device,
        mesh=mesh,
        in_specs=(
            P("replica", None, "space"),
            P("replica", None, "space"),
            P("replica", "space"),
            P("replica", "space"),
            P("replica", None, "space"),
            P("replica", None, "space"),
            P("replica", None, "space"),
            P(),
            P("replica"),
            P("replica"),
            P(),
            P(),
            P(),
            P(),
            P(),
        ),
        out_specs=(P("replica", None, "space"), P("replica", None, "space")),
        check_vma=False,
    )
```

```python
import functools

import jax
import jax.numpy as jnp
from jax import lax
from jax.experimental import pallas as pl
from jax.experimental.pallas import tpu as pltpu
from jax.sharding import PartitionSpec as P

STEPS = 2
TIME_STEP = 0.05
CUT_SQ = 9.0
N_BASIS = 8
N_KIND = 6
LANES = 128
SLOTS = 32
GROUPS = SLOTS // 8
HIDDEN = 256
AHEAD = 4
SENT, STATE = slice(0, 8), slice(8, 24)
GHOSTS, OWN = slice(0, 8), slice(8, 16)
SHARP = (N_BASIS / CUT_SQ) ** 2
CENTRES = [CUT_SQ * c / (N_BASIS - 1) for c in range(N_BASIS)]
F32 = jnp.float32
BF16 = jnp.bfloat16


def nt_dot(a, b):
    return lax.dot_general(a, b, (((1,), (1,)), ((), ())), preferred_element_type=F32)


def tn_dot(a, b):
    return lax.dot_general(a, b, (((0,), (0,)), ((), ())), preferred_element_type=F32)


def nn_dot(a, b):
    return lax.dot_general(a, b, (((1,), (0,)), ((), ())), preferred_element_type=F32)


def tile_of(flat_ref):
    rows = [
        flat_ref[:, (comp * 2 + chunk) * LANES : (comp * 2 + chunk + 1) * LANES]
        for chunk in range(2)
        for comp in range(3)
    ]
    return jnp.concatenate(rows, axis=0)


def put_flat(flat_ref, tile):
    for chunk in range(2):
        for comp in range(3):
            start = (comp * 2 + chunk) * LANES
            row = chunk * 3 + comp
            flat_ref[:, start : start + LANES] = tile[row : row + 1]


def rows_of_two(first, second, pad_with=None):
    shape = (3, LANES)
    pad = jnp.zeros((2, LANES), first.dtype)
    return jnp.concatenate(
        [jnp.broadcast_to(first, shape), jnp.broadcast_to(second, shape), pad], axis=0
    )


def take_lanes(table, lane):
    return jnp.take_along_axis(table, lane, axis=1, mode="promise_in_bounds")


def border_positions(tile, border0, border1):
    index = rows_of_two(border0, border1)
    pad = jnp.zeros((2, LANES), F32)
    low = jnp.concatenate([tile[0:3], tile[0:3], pad], axis=0)
    high = jnp.concatenate([tile[3:6], tile[3:6], pad], axis=0)
    lane = index & (LANES - 1)
    return jnp.where(index < LANES, take_lanes(low, lane), take_lanes(high, lane))


def four_sets(set0, set1, set2, set3):
    row = lax.broadcasted_iota(jnp.int32, (8, LANES), 0)
    col = lax.broadcasted_iota(jnp.int32, (8, LANES), 1)
    left = col < LANES // 2
    return jnp.where(row < 3, jnp.where(left, set0, set1), jnp.where(left, set2, set3))


def split_parts(value, count):
    parts = []
    for _ in range(count):
        part = value.astype(BF16).astype(F32)
        parts.append(part)
        value = value - part
    return parts


def bring(sources, targets, sems):
    copies = [
        pltpu.make_async_copy(source, target, sems.at[k])
        for k, (source, target) in enumerate(zip(sources, targets))
    ]
    for copy in copies:
        copy.start()
    for copy in copies:
        copy.wait()


def fed_columns():
    feature = lax.broadcasted_iota(jnp.int32, (28, LANES), 0)
    col = lax.broadcasted_iota(jnp.int32, (28, LANES), 1)
    block, which = col // 8, col % 8
    radial = (block < 8) & (feature == block)
    environ = (block == 8) & (feature == 8 + which)
    centre = (block == 9) & (which < N_KIND) & (feature == 16 + which)
    neigh = (block >= 10) & (feature == 22 + block - 10)
    return (radial | environ | centre | neigh).astype(F32)


def own_columns(slot, rows):
    col = lax.broadcasted_iota(jnp.int32, (rows, LANES), 1)
    return ((col // 8 == 8) | (col // 8 == 9) | (col % 8 == slot)).astype(F32)


def two_parts(value):
    high, low = split_parts(value, 2)
    return jnp.concatenate([high, low], axis=0).astype(BF16)


def begin_kernel(*refs):
    inputs, refs = refs[:13], refs[13:]
    (out_ref, up_ref, down_ref, line_ref, flat_ref, sum_ref, hot_ref, atom_ref, first_ref,
     second_ref, back_ref, index_ref, place_ref, total_ref, kind_ref, opening_ref), refs = (
        refs[:16], refs[16:]
    )
    x_ref, v_ref, border_ref, inertia_ref, intake_ref, edge_out_ref, middle_ref, atom_out_ref = (
        refs[:8]
    )
    landed = (
        x_ref, v_ref, kind_ref, border_ref, inertia_ref, index_ref, place_ref, total_ref,
        intake_ref, edge_out_ref, opening_ref, middle_ref, atom_out_ref,
    )
    bring(inputs, landed, refs[8])

    x_tile = tile_of(x_ref)
    border = border_ref[0]
    border0 = jnp.concatenate([border[0:1], border[1:2]], axis=1)
    border1 = jnp.concatenate([border[2:3], border[3:4]], axis=1)
    kind = kind_ref[...]
    inverse = jnp.zeros(kind.shape, F32)
    for k in range(N_KIND):
        inverse = jnp.where(kind == k, inertia_ref[k], inverse)
    out_ref[0:8] = border_positions(x_tile, border0, border1)
    out_ref[8:14] = x_tile
    out_ref[14:15] = inverse[:, :LANES]
    out_ref[15:16] = inverse[:, LANES:]
    out_ref[16:22] = tile_of(v_ref)
    out_ref[22:23] = border0.astype(F32)
    out_ref[23:24] = border1.astype(F32)

    place = lax.broadcasted_iota(jnp.int32, (LANES, 2 * LANES), 0).astype(F32).astype(BF16)
    one, none = jnp.asarray(1.0, BF16), jnp.asarray(0.0, BF16)

    def group(s, carry):
        for j in range(8):
            lane = (index_ref[0, pl.ds(s * 8 + j, 1), :] & (LANES - 1)).astype(F32)
            lane = jnp.broadcast_to(lane, (16, 2 * LANES)).astype(BF16)
            lane = jnp.concatenate([lane] * (LANES // 16), axis=0)
            cols = pl.ds(pl.multiple_of((s * 8 + j) * 2 * LANES, 2 * LANES), 2 * LANES)
            hot_ref[:, cols] = jnp.where(place == lane, one, none)
        return carry

    lax.fori_loop(0, GROUPS, group, 0)
    intake = intake_ref[...]
    fed = fed_columns()
    for j in range(8):
        up = (0.5 * fed * own_columns(j, 1)).astype(BF16)
        up_ref[j * HIDDEN : (j + 1) * HIDDEN, :] = tn_dot(intake, up).astype(BF16)
    edge_w = edge_out_ref[...]
    weighted = intake.astype(F32) * (0.5 * edge_w)
    down_ref[...] = two_parts(weighted[0:16])
    line = jnp.sum(weighted, axis=1, keepdims=True)
    flat_ref[...] = jnp.broadcast_to(line[0:16], (16, LANES))
    line = jnp.sum(fed * line, axis=0, keepdims=True)
    slot = lax.broadcasted_iota(jnp.int32, (8, LANES), 0)
    line_ref[...] = two_parts(own_columns(slot, 8) * line)
    sum_ref[...] = jnp.transpose(jnp.broadcast_to(edge_w, (LANES, HIDDEN)))
    atom_ref[...] = jnp.transpose(jnp.broadcast_to(0.5 * atom_out_ref[...], (LANES, HIDDEN)))
    first_ref[...] = jnp.transpose((0.5 * opening_ref[...]).astype(F32)).astype(BF16)
    second_ref[...] = 0.5 * middle_ref[...]
    back_ref[...] = jnp.transpose(middle_ref[...].astype(F32)).astype(BF16)


def around(far_ref, rows):
    if len(far_ref.shape) == 3:
        return [far_ref[k, rows] for k in range(4)]
    return [far_ref[0, 0, 0, rows], far_ref[0, 0, 1, rows], far_ref[1, 1, 0, rows], far_ref[1, 1, 1, rows]]


def force_kernel(
    where_ref,
    home_ref,
    far_ref,
    up_ref,
    down_ref,
    line_ref,
    flat_ref,
    sum_ref,
    hot_ref,
    atom_ref,
    first_ref,
    second_ref,
    back_ref,
    index_ref,
    place_kind_ref,
    total_ref,
    kind_ref,
    opening_ref,
    out_ref,
    feat_ref,
    gauss_ref,
    geo_ref,
    energy_ref,
    gin0_ref,
    gin1_ref,
    *scratch,
):
    scat, ahead_ref = (scratch[:GROUPS], scratch[GROUPS : 2 * GROUPS]), scratch[2 * GROUPS]
    first_core = where_ref[0:1] == 0
    own = jnp.where(first_core, home_ref[0, STATE], home_ref[1, STATE])
    minus2, minus1, plus2, plus3 = around(far_ref, SENT)
    near0, near1 = home_ref[0, SENT], home_ref[1, SENT]

    def pick(a, b):
        return jnp.where(first_core, a, b)

    ghost = four_sets(
        pick(minus1, near0), pick(near1, plus2), pick(minus2, minus1), pick(plus2, plus3)
    )

    kind_rows = lax.broadcasted_iota(jnp.int32, (8, 2 * LANES), 0)
    centre_hot = (kind_rows == kind_ref[...]).astype(F32)
    slot_row = lax.broadcasted_iota(jnp.int32, (8, LANES), 0)
    tables = [
        [jnp.broadcast_to(t[r * 3 + c : r * 3 + c + 1], (8, LANES)) for c in range(3)]
        for t in (own, ghost)
        for r in range(2)
    ]

    def geometry(s, sums):
        sums = list(sums)
        slots = pl.ds(pl.multiple_of(s * 8, 8), 8)
        radials = [[], []]
        for h in range(2):
            cols = slice(h * LANES, (h + 1) * LANES)
            index = index_ref[0, slots, cols]
            lane = index & (LANES - 1)
            chunk = index // LANES
            dist_sq = None
            for comp in range(3):
                found = take_lanes(tables[0][comp], lane)
                for which in range(1, 4):
                    found = jnp.where(chunk == which, take_lanes(tables[which][comp], lane), found)
                vec = found - tables[h][comp]
                geo_ref[comp, s, :, cols] = vec
                dist_sq = vec * vec if comp == 0 else dist_sq + vec * vec
            live = slot_row + s * 8 < total_ref[:, cols]
            inside = 1.0 - dist_sq * (1.0 / CUT_SQ)
            used = live & (inside > 0.0)
            cutoff = jnp.where(used, inside * inside, 0.0)
            geo_ref[3, s, :, cols] = dist_sq
            geo_ref[4, s, :, cols] = cutoff
            geo_ref[5, s, :, cols] = jnp.where(used, inside * (-2.0 / CUT_SQ), 0.0)
            for c in range(N_BASIS):
                gap = dist_sq - CENTRES[c]
                gauss = jnp.exp(-SHARP * (gap * gap))
                gauss_ref[s, c * 8 : c * 8 + 8, cols] = gauss
                radial = gauss * cutoff
                radials[h].append(radial)
                sums[h * N_BASIS + c] = sums[h * N_BASIS + c] + radial
        place_kind = place_kind_ref[0, slots, :]
        rows = [jnp.concatenate([a, b], axis=1) for a, b in zip(*radials)]
        feat_ref[s, 0:64] = jnp.concatenate(rows, axis=0).astype(BF16)
        rows = [(place_kind == k).astype(F32) for k in range(N_KIND)]
        feat_ref[s, 80:128] = jnp.concatenate(rows, axis=0).astype(BF16)
        return tuple(sums)

    nothing = jnp.zeros((8, LANES), F32)
    sums = lax.fori_loop(0, GROUPS, geometry, (nothing,) * (2 * N_BASIS))
    rows = [jnp.sum(value, axis=0, keepdims=True) for value in sums]
    environ = jnp.concatenate(
        [jnp.concatenate(rows[:N_BASIS], axis=0), jnp.concatenate(rows[N_BASIS:], axis=0)], axis=1
    )
    shared = jnp.concatenate([environ, centre_hot], axis=0).astype(BF16)
    for s in range(GROUPS):
        feat_ref[s, 64:80] = shared

    atom_w = jnp.concatenate([atom_ref[...], atom_ref[...]], axis=1)
    half = nn_dot(first_ref[...], environ.astype(BF16))
    th = jnp.tanh(half)
    hidden_one = (half + half * th).astype(BF16)
    slope_one = 0.5 * (1.0 + th + half * (1.0 - th * th))
    half = nn_dot(second_ref[...], hidden_one)
    th = jnp.tanh(half)
    g_second = (atom_w * (1.0 + th + half * (1.0 - th * th))).astype(BF16)
    g_hidden = nn_dot(back_ref[...], g_second)
    g_first = (g_hidden * slope_one).astype(BF16)
    g_env = nn_dot(opening_ref[...], g_first)

    flat = jnp.concatenate([flat_ref[...], flat_ref[...]], axis=1)
    slot = lax.broadcasted_iota(jnp.int32, (16, HIDDEN), 0)
    quarter = lax.broadcasted_iota(jnp.int32, (16, HIDDEN), 1) // (HIDDEN // 4)
    members = [(slot == quarter + 4 * k).astype(F32).astype(BF16) for k in range(2)]

    def first_forward(s):
        ahead_ref[...] = nn_dot(up_ref[: AHEAD * HIDDEN, :], feat_ref[s])

    def group(s, g_env):
        feat = feat_ref[s]
        line = nn_dot(line_ref[...], feat)
        energy = line[0:8] + line[8:16]
        folded = []
        edge_w = sum_ref[...].astype(BF16)
        edge_w = jnp.concatenate([edge_w, edge_w], axis=1)

        def forward(k):
            many = nn_dot(up_ref[k * AHEAD * HIDDEN : (k + 1) * AHEAD * HIDDEN, :], feat)
            return [many[i * HIDDEN : (i + 1) * HIDDEN].astype(BF16) for i in range(AHEAD)]

        ahead = [ahead_ref[i * HIDDEN : (i + 1) * HIDDEN].astype(BF16) for i in range(AHEAD)]
        ahead += forward(1)
        for j in range(8):
            half = ahead.pop(0)
            if j == AHEAD:
                first_forward(jnp.minimum(s + 1, GROUPS - 1))
            th = jnp.tanh(half)
            rest = edge_w * (half * th)
            rest = rest[: HIDDEN // 2] + rest[HIDDEN // 2 :]
            folded.append(rest[: HIDDEN // 4] + rest[HIDDEN // 4 :])
            slope = th + half * (jnp.asarray(1.0, BF16) - th * th)
            g_in = nn_dot(down_ref[...], slope)
            cut = geo_ref[4, s, j : j + 1, :]
            g_in = (g_in[0:16] + g_in[16:32] + flat) * cut
            rows = pl.ds(s * 64 + j, 8, stride=8)
            gin0_ref[rows, :] = g_in[0:8, :LANES]
            gin1_ref[rows, :] = g_in[0:8, LANES:]
            g_env = g_env + g_in[8:16]
        for k in range(2):
            rest = jnp.concatenate(folded[k * 4 : k * 4 + 4], axis=0)
            energy = energy + nn_dot(members[k], rest)[0:8]
        energy_ref[s] = energy
        return g_env

    first_forward(0)
    g_env = lax.fori_loop(1, GROUPS, group, group(0, g_env))

    def backward(s, sums):
        sums = list(sums)
        slots = slice(s * 8, s * 8 + 8)
        for h in range(2):
            cols = slice(h * LANES, (h + 1) * LANES)
            dist_sq, cutoff, slope = (geo_ref[k, s, :, cols] for k in (3, 4, 5))
            g_cut = energy_ref[s, :, cols]
            g_gap = None
            gin = (gin0_ref, gin1_ref)[h]
            for c in range(N_BASIS):
                rows = slice(s * 64 + c * 8, s * 64 + c * 8 + 8)
                g_radial = gin[rows, :] + g_env[c : c + 1, cols]
                q = g_radial * gauss_ref[s, c * 8 : c * 8 + 8, cols]
                g_cut = g_cut + q
                moment = q * (dist_sq - CENTRES[c])
                g_gap = moment if g_gap is None else g_gap + moment
            g_dist = (-4.0 * SHARP) * (cutoff * g_gap) + 2.0 * (g_cut * slope)
            chunk = index_ref[0, slots, cols] // LANES
            target = scat[h][s]
            for comp in range(3):
                g_vec = g_dist * geo_ref[comp, s, :, cols]
                sums[h * 3 + comp] = sums[h * 3 + comp] + g_vec
                for part, value in enumerate(split_parts(g_vec, 2)):
                    for which in range(4):
                        row = part * 12 + which * 3 + comp
                        target[pl.ds(row, 8, stride=24), :] = jnp.where(chunk == which, value, 0.0)
        return tuple(sums)

    def scatter(s):
        lhs = []
        for j in range(8):
            rows = slice(j * 24, j * 24 + 24)
            lhs.append(jnp.concatenate([half[s][rows, :] for half in scat], axis=1).astype(BF16))
        return nt_dot(jnp.concatenate(lhs, axis=1), hot_ref[:, s * 16 * LANES : (s + 1) * 16 * LANES])

    sums, total = (nothing,) * 6, None
    for s in range(GROUPS):
        sums = backward(s, sums)
        part = scatter(s)
        total = part if total is None else total + part
    total = total[0:12] + total[12:24]
    centre = jnp.concatenate([jnp.sum(value, axis=0, keepdims=True) for value in sums], axis=0)
    pad = jnp.zeros((2, LANES), F32)
    out_ref[0:8] = jnp.concatenate([total[6:12], pad], axis=0)
    out_ref[8:16] = jnp.concatenate([total[0:6] - centre, pad], axis=0)


def returned_sum(returned, border0, border1):
    row = lax.broadcasted_iota(jnp.int32, (8, LANES), 0)
    place = lax.broadcasted_iota(jnp.int32, (LANES, LANES), 0)
    lhs, rhs = [], []
    for which, border in enumerate((border0, border1)):
        three = returned[which * 3 : which * 3 + 3]
        twice = jnp.concatenate([three, three, jnp.zeros((2, LANES), F32)], axis=0)
        meant = (border // LANES == 1) == (row >= 3)
        kept = jnp.where(meant, twice, 0.0)
        lhs.append(jnp.concatenate(split_parts(kept, 3), axis=0).astype(BF16))
        rhs.append((place == (border & (LANES - 1))).astype(F32).astype(BF16))
    total = nt_dot(jnp.concatenate(lhs, axis=1), jnp.concatenate(rhs, axis=1))
    return total[0:8] + total[8:16] + total[16:24]


def moved(state, own_grad, ghosts, domain):
    border0 = state[14:15].astype(jnp.int32)
    border1 = state[15:16].astype(jnp.int32)
    inverse = rows_of_two(state[6:7], state[7:8])
    returned = four_sets(*(ghosts[domain + offset] for offset in (1, -1, 2, -2)))
    grad = own_grad + returned_sum(returned, border0, border1)
    speed = state[8:16] - TIME_STEP * grad * inverse
    return state[0:8] + TIME_STEP * speed, speed, border0, border1


def step_kernel(home_ref, far_ref, near_ref, wide_ref, next_ref, around_ref):
    below, above = wide_ref.at[0, 0], wide_ref.at[1, 1]
    states = dict(zip((-2, -1, 2, 3), around(far_ref, STATE)))
    ghosts, owns = {}, {}
    for k in range(2):
        states[k] = home_ref[k, STATE]
        for domain, block in ((k, near_ref.at[k]), (k - 2, below.at[k]), (k + 2, above.at[k])):
            ghosts[domain], owns[domain] = block[GHOSTS], block[OWN]
        ghosts[k - 4], ghosts[k + 4] = below[k, 16:24], above[k, 16:24]
    for domain, state in states.items():
        place, speed, border0, border1 = moved(state, owns[domain], ghosts, domain)
        sent = border_positions(place, border0, border1)
        if domain in (0, 1):
            next_ref[domain, SENT] = sent
            next_ref[domain, 8:14] = place[0:6]
            next_ref[domain, 14:16] = state[6:8]
            next_ref[domain, 16:22] = speed[0:6]
            next_ref[domain, 22:24] = state[14:16]
        else:
            around_ref[domain + 2 if domain < 0 else domain] = sent


def last_kernel(where_ref, home_ref, near_ref, far_ref, next_ref):
    ghosts = dict(zip((-2, -1, 2, 3), around(far_ref, GHOSTS)))
    ghosts[0], ghosts[1] = near_ref[0, GHOSTS], near_ref[1, GHOSTS]
    for domain in range(2):
        place, speed, _, _ = moved(home_ref[domain, STATE], near_ref[domain, OWN], ghosts, domain)
        next_ref[domain, 0:6] = place[0:6]
        next_ref[domain, 6:8] = jnp.broadcast_to(where_ref[4:5], (2, LANES))
        next_ref[domain, 8:16] = speed


def swap_kernel(where_ref, own_ref, mate_ref, x_out, v_out, x_ref, v_ref, sems):
    core, swaps, side, position = (where_ref[k : k + 1] == 0 for k in range(4))

    def of_core(pair):
        return jnp.where(core, pair[0], pair[1])

    def of_side(s):
        return of_core(jnp.where(position, mate_ref[s, 0], mate_ref[s, 1]))

    mine = of_core(own_ref)
    chosen = jnp.where(swaps, mine, jnp.where(side, of_side(0), of_side(1)))
    scale = jnp.sqrt(mine[6:7] / chosen[6:7])
    put_flat(x_ref, chosen[0:6])
    put_flat(v_ref, chosen[8:14] * scale)
    bring((x_ref, v_ref), (x_out, v_out), sems)


def vmem():
    return pl.BlockSpec(memory_space=pltpu.VMEM)


def smem():
    return pl.BlockSpec(memory_space=pltpu.SMEM)


def tiles(*shape):
    return jax.ShapeDtypeStruct(shape + (LANES,), F32)


def call(kernel, scalars, arrays, out_shape, scratch=(), flops=10**6, inputs=None, outputs=None,
         limit=24 * 2**20):
    outputs = outputs or vmem
    out_specs = [outputs() for _ in out_shape] if isinstance(out_shape, list) else outputs()
    return pl.pallas_call(
        kernel,
        out_shape=out_shape,
        in_specs=[smem()] * len(scalars) + [(inputs or vmem)()] * len(arrays),
        out_specs=out_specs,
        scratch_shapes=list(scratch),
        cost_estimate=pl.CostEstimate(flops=flops, bytes_accessed=10**6, transcendentals=0),
        compiler_params=pltpu.CompilerParams(vmem_limit_bytes=limit),
    )(*scalars, *arrays)


def anywhere():
    return pl.BlockSpec(memory_space=pltpu.HBM)


def landing(arrays):
    return [pltpu.VMEM(a.shape, a.dtype) for a in arrays] + [pltpu.SemaphoreType.DMA((len(arrays),))]


def weight_shapes():
    return [
        jax.ShapeDtypeStruct((8 * HIDDEN, LANES), BF16),
        jax.ShapeDtypeStruct((32, HIDDEN), BF16),
        jax.ShapeDtypeStruct((16, LANES), BF16),
        tiles(16),
        tiles(HIDDEN),
        jax.ShapeDtypeStruct((LANES, SLOTS * 2 * LANES), BF16),
        tiles(HIDDEN),
        jax.ShapeDtypeStruct((HIDDEN, N_BASIS), BF16),
        jax.ShapeDtypeStruct((HIDDEN, HIDDEN), BF16),
        jax.ShapeDtypeStruct((HIDDEN, HIDDEN), BF16),
    ]


def begin_shapes(arrays):
    through = [jax.ShapeDtypeStruct(arrays[k].shape, arrays[k].dtype) for k in (5, 6, 7, 2, 10)]
    space = landing([arrays[k] for k in (0, 1, 3, 4, 8, 9, 11, 12)])
    space[3] = pltpu.SMEM(arrays[4].shape, F32)
    space[-1] = pltpu.SemaphoreType.DMA((len(arrays),))
    made = [tiles(24)] + weight_shapes() + through
    return made, space


def force_scratch():
    return [
        pltpu.VMEM((GROUPS, 128, 2 * LANES), BF16),
        pltpu.VMEM((GROUPS, 64, 2 * LANES), F32),
        pltpu.VMEM((6, GROUPS, 8, 2 * LANES), F32),
        pltpu.VMEM((GROUPS, 8, 2 * LANES), F32),
        pltpu.VMEM((GROUPS * 64, LANES), F32),
        pltpu.VMEM((GROUPS * 64, LANES), F32),
    ] + [pltpu.VMEM((8 * 24, LANES), F32)] * (2 * GROUPS) + [pltpu.VMEM((AHEAD * HIDDEN, 2 * LANES), F32)]


def on_chip(value, domains):
    groups = [[2 * i, 2 * i + 1] for i in range(domains // 2)]
    return lax.all_gather(value, "space", axis_index_groups=groups)


def across_chips(value, domains, chips=1):
    groups = [[(2 * (i - chips) + 1) % domains, 2 * i] for i in range(domains // 2)]
    return lax.all_gather(value, "space", axis_index_groups=groups)


def along_ladder(value, rungs, domains):
    groups = []
    for domain in range(domains):
        shift = domain % 2
        for low in range(shift, rungs - shift, 2):
            groups.append([low * domains + domain, (low + 1) * domains + domain])
        if shift and domain // 2 % 2 == 0:
            for end in (0, rungs - 1):
                groups.append([end * domains + domain, end * domains + domain + 2])
    return lax.all_gather(value, ("replica", "space"), axis_index_groups=groups)


def on_device(
    particle_coordinates,
    particle_motions,
    particle_kinds,
    filled_totals,
    adjacent_particles,
    adjacent_place_kinds,
    border_particle_numbers,
    reciprocal_kind_inertia,
    thermal_levels,
    swap_mates,
    bond_intake_coefficients,
    bond_output_coefficients,
    particle_opening_coefficients,
    particle_middle_coefficients,
    particle_output_coefficients,
):
    domains, rungs = lax.axis_size("space"), lax.axis_size("replica")
    core = lax.axis_index("space") % 2
    rank = lax.axis_index("replica")
    mate = swap_mates[0]
    odd = rank % 2
    side = jnp.where((mate > rank) == (odd == 0), 0, 1)
    position = jnp.where(side == 0, 1 - odd, odd)
    where_to = [value.astype(F32) for value in (core, mate != rank, side, position)]
    where_to = jnp.stack(where_to + [thermal_levels[0]])
    where_to = jnp.broadcast_to(where_to[:, None], (5, LANES))

    arrays = (
        particle_coordinates.reshape(1, -1),
        particle_motions.reshape(1, -1),
        particle_kinds,
        border_particle_numbers,
        reciprocal_kind_inertia,
        adjacent_particles,
        adjacent_place_kinds,
        filled_totals,
        bond_intake_coefficients.T,
        bond_output_coefficients[None],
        particle_opening_coefficients.T,
        particle_middle_coefficients,
        particle_output_coefficients[None],
    )
    arrays = tuple(pltpu.with_memory_space_constraint(a, pltpu.HBM) for a in arrays)
    made, space = begin_shapes(arrays)
    begin, *fixed = call(begin_kernel, (), arrays, made, space, inputs=anywhere)
    home = on_chip(begin, domains)
    far = on_chip(across_chips(home, domains), domains)
    for step in range(STEPS):
        partial = call(force_kernel, (), (where_to, home, far, *fixed), tiles(16), force_scratch())
        near = on_chip(partial, domains)
        if step < STEPS - 1:
            one = across_chips(near, domains)
            two = across_chips(near[:, GHOSTS], domains, 2)
            wide = on_chip(jnp.concatenate([one, two], axis=2), domains)
            shapes = [tiles(2, 24), tiles(4, 8)]
            home, far = call(step_kernel, (), (home, far, near, wide), shapes)
        else:
            far = on_chip(across_chips(near[:, GHOSTS], domains), domains)
            state = call(last_kernel, (), (where_to, home, near, far), tiles(2, 16))
    mates = on_chip(along_ladder(state, rungs, domains), domains)
    shape = particle_coordinates.shape
    out = jax.ShapeDtypeStruct((1, particle_coordinates.size), F32)
    scratch = landing((out, out))
    new_x, new_v = call(
        swap_kernel, (), (where_to, state, mates), [out, out], scratch, outputs=anywhere
    )
    return new_x.reshape(shape), new_v.reshape(shape)


def solution(mesh):
    return jax.shard_map(
        on_device,
        mesh=mesh,
        in_specs=(
            P("replica", None, "space"),
            P("replica", None, "space"),
            P("replica", "space"),
            P("replica", "space"),
            P("replica", None, "space"),
            P("replica", None, "space"),
            P("replica", None, "space"),
            P(),
            P("replica"),
            P("replica"),
            P(),
            P(),
            P(),
            P(),
            P(),
        ),
        out_specs=(P("replica", None, "space"), P("replica", None, "space")),
        check_vma=False,
    )
```

```python
import functools

import jax
import jax.numpy as jnp
from jax import lax
from jax.experimental import pallas as pl
from jax.experimental.pallas import tpu as pltpu
from jax.sharding import PartitionSpec as P

STEPS = 2
TIME_STEP = 0.05
CUT_SQ = 9.0
N_BASIS = 8
N_KIND = 6
LANES = 128
SLOTS = 32
GROUPS = SLOTS // 8
HIDDEN = 256
AHEAD = 4
SENT, STATE = slice(0, 8), slice(8, 24)
GHOSTS, OWN = slice(0, 8), slice(8, 16)
SHARP = (N_BASIS / CUT_SQ) ** 2
CENTRES = [CUT_SQ * c / (N_BASIS - 1) for c in range(N_BASIS)]
F32 = jnp.float32
BF16 = jnp.bfloat16


def nt_dot(a, b):
    return lax.dot_general(a, b, (((1,), (1,)), ((), ())), preferred_element_type=F32)


def tn_dot(a, b):
    return lax.dot_general(a, b, (((0,), (0,)), ((), ())), preferred_element_type=F32)


def nn_dot(a, b):
    return lax.dot_general(a, b, (((1,), (0,)), ((), ())), preferred_element_type=F32)


def tile_of(flat_ref):
    rows = [
        flat_ref[:, (comp * 2 + chunk) * LANES : (comp * 2 + chunk + 1) * LANES]
        for chunk in range(2)
        for comp in range(3)
    ]
    return jnp.concatenate(rows, axis=0)


def put_flat(flat_ref, tile):
    for chunk in range(2):
        for comp in range(3):
            start = (comp * 2 + chunk) * LANES
            row = chunk * 3 + comp
            flat_ref[:, start : start + LANES] = tile[row : row + 1]


def rows_of_two(first, second, pad_with=None):
    shape = (3, LANES)
    pad = jnp.zeros((2, LANES), first.dtype)
    return jnp.concatenate(
        [jnp.broadcast_to(first, shape), jnp.broadcast_to(second, shape), pad], axis=0
    )


def take_lanes(table, lane):
    return jnp.take_along_axis(table, lane, axis=1, mode="promise_in_bounds")


def border_positions(tile, border0, border1):
    index = rows_of_two(border0, border1)
    pad = jnp.zeros((2, LANES), F32)
    low = jnp.concatenate([tile[0:3], tile[0:3], pad], axis=0)
    high = jnp.concatenate([tile[3:6], tile[3:6], pad], axis=0)
    lane = index & (LANES - 1)
    return jnp.where(index < LANES, take_lanes(low, lane), take_lanes(high, lane))


def four_sets(set0, set1, set2, set3):
    row = lax.broadcasted_iota(jnp.int32, (8, LANES), 0)
    col = lax.broadcasted_iota(jnp.int32, (8, LANES), 1)
    left = col < LANES // 2
    return jnp.where(row < 3, jnp.where(left, set0, set1), jnp.where(left, set2, set3))


def split_parts(value, count):
    parts = []
    for _ in range(count):
        part = value.astype(BF16).astype(F32)
        parts.append(part)
        value = value - part
    return parts


def bring(sources, targets, sems):
    copies = [
        pltpu.make_async_copy(source, target, sems.at[k])
        for k, (source, target) in enumerate(zip(sources, targets))
    ]
    for copy in copies:
        copy.start()
    for copy in copies:
        copy.wait()


def fed_columns():
    feature = lax.broadcasted_iota(jnp.int32, (28, LANES), 0)
    col = lax.broadcasted_iota(jnp.int32, (28, LANES), 1)
    block, which = col // 8, col % 8
    radial = (block < 8) & (feature == block)
    environ = (block == 8) & (feature == 8 + which)
    centre = (block == 9) & (which < N_KIND) & (feature == 16 + which)
    neigh = (block >= 10) & (feature == 22 + block - 10)
    return (radial | environ | centre | neigh).astype(F32)


def own_columns(slot, rows):
    col = lax.broadcasted_iota(jnp.int32, (rows, LANES), 1)
    return ((col // 8 == 8) | (col // 8 == 9) | (col % 8 == slot)).astype(F32)


def two_parts(value):
    high, low = split_parts(value, 2)
    return jnp.concatenate([high, low], axis=0).astype(BF16)


def begin_kernel(*refs):
    inputs, refs = refs[:13], refs[13:]
    (out_ref, up_ref, down_ref, line_ref, flat_ref, sum_ref, hot_ref, atom_ref, first_ref,
     second_ref, back_ref, index_ref, place_ref, total_ref, kind_ref, opening_ref), refs = (
        refs[:16], refs[16:]
    )
    x_ref, v_ref, border_ref, inertia_ref, intake_ref, edge_out_ref, middle_ref, atom_out_ref = (
        refs[:8]
    )
    landed = (
        x_ref, v_ref, kind_ref, border_ref, inertia_ref, index_ref, place_ref, total_ref,
        intake_ref, edge_out_ref, opening_ref, middle_ref, atom_out_ref,
    )
    bring(inputs, landed, refs[8])

    x_tile = tile_of(x_ref)
    border = border_ref[0]
    border0 = jnp.concatenate([border[0:1], border[1:2]], axis=1)
    border1 = jnp.concatenate([border[2:3], border[3:4]], axis=1)
    kind = kind_ref[...]
    inverse = jnp.zeros(kind.shape, F32)
    for k in range(N_KIND):
        inverse = jnp.where(kind == k, inertia_ref[k], inverse)
    out_ref[0:8] = border_positions(x_tile, border0, border1)
    out_ref[8:14] = x_tile
    out_ref[14:15] = inverse[:, :LANES]
    out_ref[15:16] = inverse[:, LANES:]
    out_ref[16:22] = tile_of(v_ref)
    out_ref[22:23] = border0.astype(F32)
    out_ref[23:24] = border1.astype(F32)

    place = lax.broadcasted_iota(jnp.int32, (LANES, 2 * LANES), 0).astype(F32).astype(BF16)
    one, none = jnp.asarray(1.0, BF16), jnp.asarray(0.0, BF16)

    def group(s, carry):
        for j in range(8):
            lane = (index_ref[0, pl.ds(s * 8 + j, 1), :] & (LANES - 1)).astype(F32)
            lane = jnp.broadcast_to(lane, (16, 2 * LANES)).astype(BF16)
            lane = jnp.concatenate([lane] * (LANES // 16), axis=0)
            cols = pl.ds(pl.multiple_of((s * 8 + j) * 2 * LANES, 2 * LANES), 2 * LANES)
            hot_ref[:, cols] = jnp.where(place == lane, one, none)
        return carry

    lax.fori_loop(0, GROUPS, group, 0)
    intake = intake_ref[...]
    fed = fed_columns()
    for j in range(8):
        up = (0.5 * fed * own_columns(j, 1)).astype(BF16)
        up_ref[j * HIDDEN : (j + 1) * HIDDEN, :] = tn_dot(intake, up).astype(BF16)
    edge_w = edge_out_ref[...]
    weighted = intake.astype(F32) * (0.5 * edge_w)
    down_ref[...] = two_parts(weighted[0:16])
    line = jnp.sum(weighted, axis=1, keepdims=True)
    flat_ref[...] = jnp.broadcast_to(line[0:16], (16, LANES))
    line = jnp.sum(fed * line, axis=0, keepdims=True)
    slot = lax.broadcasted_iota(jnp.int32, (8, LANES), 0)
    line_ref[...] = two_parts(own_columns(slot, 8) * line)
    sum_ref[...] = jnp.transpose(jnp.broadcast_to(edge_w, (LANES, HIDDEN)))
    atom_ref[...] = jnp.transpose(jnp.broadcast_to(0.5 * atom_out_ref[...], (LANES, HIDDEN)))
    first_ref[...] = jnp.transpose((0.5 * opening_ref[...]).astype(F32)).astype(BF16)
    second_ref[...] = 0.5 * middle_ref[...]
    back_ref[...] = jnp.transpose(middle_ref[...].astype(F32)).astype(BF16)


def around(far_ref, rows):
    if len(far_ref.shape) == 3:
        return [far_ref[k, rows] for k in range(4)]
    return [far_ref[0, 0, 0, rows], far_ref[0, 0, 1, rows], far_ref[1, 1, 0, rows], far_ref[1, 1, 1, rows]]


def force_kernel(
    where_ref,
    home_ref,
    far_ref,
    up_ref,
    down_ref,
    line_ref,
    flat_ref,
    sum_ref,
    hot_ref,
    atom_ref,
    first_ref,
    second_ref,
    back_ref,
    index_ref,
    place_kind_ref,
    total_ref,
    kind_ref,
    opening_ref,
    out_ref,
    feat_ref,
    gauss_ref,
    geo_ref,
    energy_ref,
    gin0_ref,
    gin1_ref,
    *scratch,
):
    scat, ahead_ref = (scratch[:GROUPS], scratch[GROUPS : 2 * GROUPS]), scratch[2 * GROUPS]
    first_core = where_ref[0:1] == 0
    own = jnp.where(first_core, home_ref[0, STATE], home_ref[1, STATE])
    minus2, minus1, plus2, plus3 = around(far_ref, SENT)
    near0, near1 = home_ref[0, SENT], home_ref[1, SENT]

    def pick(a, b):
        return jnp.where(first_core, a, b)

    ghost = four_sets(
        pick(minus1, near0), pick(near1, plus2), pick(minus2, minus1), pick(plus2, plus3)
    )

    kind_rows = lax.broadcasted_iota(jnp.int32, (8, 2 * LANES), 0)
    centre_hot = (kind_rows == kind_ref[...]).astype(F32)
    slot_row = lax.broadcasted_iota(jnp.int32, (8, LANES), 0)
    tables = [
        [jnp.broadcast_to(t[r * 3 + c : r * 3 + c + 1], (8, LANES)) for c in range(3)]
        for t in (own, ghost)
        for r in range(2)
    ]

    def geometry(s, sums):
        sums = list(sums)
        slots = pl.ds(pl.multiple_of(s * 8, 8), 8)
        radials = [[], []]
        for h in range(2):
            cols = slice(h * LANES, (h + 1) * LANES)
            index = index_ref[0, slots, cols]
            lane = index & (LANES - 1)
            chunk = index // LANES
            dist_sq = None
            for comp in range(3):
                found = take_lanes(tables[0][comp], lane)
                for which in range(1, 4):
                    found = jnp.where(chunk == which, take_lanes(tables[which][comp], lane), found)
                vec = found - tables[h][comp]
                geo_ref[comp, s, :, cols] = vec
                dist_sq = vec * vec if comp == 0 else dist_sq + vec * vec
            live = slot_row + s * 8 < total_ref[:, cols]
            inside = 1.0 - dist_sq * (1.0 / CUT_SQ)
            used = live & (inside > 0.0)
            cutoff = jnp.where(used, inside * inside, 0.0)
            geo_ref[3, s, :, cols] = dist_sq
            geo_ref[4, s, :, cols] = cutoff
            geo_ref[5, s, :, cols] = jnp.where(used, inside * (-2.0 / CUT_SQ), 0.0)
            for c in range(N_BASIS):
                gap = dist_sq - CENTRES[c]
                gauss = jnp.exp(-SHARP * (gap * gap))
                gauss_ref[s, c * 8 : c * 8 + 8, cols] = gauss
                radial = gauss * cutoff
                radials[h].append(radial)
                sums[h * N_BASIS + c] = sums[h * N_BASIS + c] + radial
        place_kind = place_kind_ref[0, slots, :]
        rows = [jnp.concatenate([a, b], axis=1) for a, b in zip(*radials)]
        feat_ref[s, 0:64] = jnp.concatenate(rows, axis=0).astype(BF16)
        rows = [(place_kind == k).astype(F32) for k in range(N_KIND)]
        feat_ref[s, 80:128] = jnp.concatenate(rows, axis=0).astype(BF16)
        return tuple(sums)

    nothing = jnp.zeros((8, LANES), F32)
    sums = lax.fori_loop(0, GROUPS, geometry, (nothing,) * (2 * N_BASIS))
    rows = [jnp.sum(value, axis=0, keepdims=True) for value in sums]
    environ = jnp.concatenate(
        [jnp.concatenate(rows[:N_BASIS], axis=0), jnp.concatenate(rows[N_BASIS:], axis=0)], axis=1
    )
    shared = jnp.concatenate([environ, centre_hot], axis=0).astype(BF16)
    for s in range(GROUPS):
        feat_ref[s, 64:80] = shared

    atom_w = jnp.concatenate([atom_ref[...], atom_ref[...]], axis=1)
    half = nn_dot(first_ref[...], environ.astype(BF16))
    th = jnp.tanh(half)
    hidden_one = (half + half * th).astype(BF16)
    slope_one = 0.5 * (1.0 + th + half * (1.0 - th * th))
    half = nn_dot(second_ref[...], hidden_one)
    th = jnp.tanh(half)
    g_second = (atom_w * (1.0 + th + half * (1.0 - th * th))).astype(BF16)
    g_hidden = nn_dot(back_ref[...], g_second)
    g_first = (g_hidden * slope_one).astype(BF16)
    g_env = nn_dot(opening_ref[...], g_first)

    flat = jnp.concatenate([flat_ref[...], flat_ref[...]], axis=1)
    slot = lax.broadcasted_iota(jnp.int32, (16, HIDDEN), 0)
    quarter = lax.broadcasted_iota(jnp.int32, (16, HIDDEN), 1) // (HIDDEN // 4)
    members = [(slot == quarter + 4 * k).astype(F32).astype(BF16) for k in range(2)]

    def first_forward(s):
        ahead_ref[...] = nn_dot(up_ref[: AHEAD * HIDDEN, :], feat_ref[s])

    def group(s, g_env):
        feat = feat_ref[s]
        line = nn_dot(line_ref[...], feat)
        energy = line[0:8] + line[8:16]
        folded = []
        edge_w = sum_ref[...].astype(BF16)
        edge_w = jnp.concatenate([edge_w, edge_w], axis=1)

        def forward(k):
            many = nn_dot(up_ref[k * AHEAD * HIDDEN : (k + 1) * AHEAD * HIDDEN, :], feat)
            return [many[i * HIDDEN : (i + 1) * HIDDEN].astype(BF16) for i in range(AHEAD)]

        ahead = [ahead_ref[i * HIDDEN : (i + 1) * HIDDEN].astype(BF16) for i in range(AHEAD)]
        ahead += forward(1)
        for j in range(8):
            half = ahead.pop(0)
            if j == AHEAD:
                first_forward(jnp.minimum(s + 1, GROUPS - 1))
            th = jnp.tanh(half)
            rest = edge_w * (half * th)
            rest = rest[: HIDDEN // 2] + rest[HIDDEN // 2 :]
            folded.append(rest[: HIDDEN // 4] + rest[HIDDEN // 4 :])
            slope = th + half * (jnp.asarray(1.0, BF16) - th * th)
            g_in = nn_dot(down_ref[...], slope)
            cut = geo_ref[4, s, j : j + 1, :]
            g_in = (g_in[0:16] + g_in[16:32] + flat) * cut
            rows = pl.ds(s * 64 + j, 8, stride=8)
            gin0_ref[rows, :] = g_in[0:8, :LANES]
            gin1_ref[rows, :] = g_in[0:8, LANES:]
            g_env = g_env + g_in[8:16]
        for k in range(2):
            rest = jnp.concatenate(folded[k * 4 : k * 4 + 4], axis=0)
            energy = energy + nn_dot(members[k], rest)[0:8]
        energy_ref[s] = energy
        return g_env

    first_forward(0)
    g_env = lax.fori_loop(1, GROUPS, group, group(0, g_env))

    def backward(s, sums):
        sums = list(sums)
        slots = slice(s * 8, s * 8 + 8)
        for h in range(2):
            cols = slice(h * LANES, (h + 1) * LANES)
            dist_sq, cutoff, slope = (geo_ref[k, s, :, cols] for k in (3, 4, 5))
            g_cut = energy_ref[s, :, cols]
            g_gap = None
            gin = (gin0_ref, gin1_ref)[h]
            for c in range(N_BASIS):
                rows = slice(s * 64 + c * 8, s * 64 + c * 8 + 8)
                g_radial = gin[rows, :] + g_env[c : c + 1, cols]
                q = g_radial * gauss_ref[s, c * 8 : c * 8 + 8, cols]
                g_cut = g_cut + q
                moment = q * (dist_sq - CENTRES[c])
                g_gap = moment if g_gap is None else g_gap + moment
            g_dist = (-4.0 * SHARP) * (cutoff * g_gap) + 2.0 * (g_cut * slope)
            chunk = index_ref[0, slots, cols] // LANES
            target = scat[h][s]
            for comp in range(3):
                g_vec = g_dist * geo_ref[comp, s, :, cols]
                sums[h * 3 + comp] = sums[h * 3 + comp] + g_vec
                for part, value in enumerate(split_parts(g_vec, 2)):
                    for which in range(4):
                        row = part * 12 + which * 3 + comp
                        target[pl.ds(row, 8, stride=24), :] = jnp.where(chunk == which, value, 0.0)
        return tuple(sums)

    def scatter(s):
        lhs = []
        for j in range(8):
            rows = slice(j * 24, j * 24 + 24)
            lhs.append(jnp.concatenate([half[s][rows, :] for half in scat], axis=1).astype(BF16))
        return nt_dot(jnp.concatenate(lhs, axis=1), hot_ref[:, s * 16 * LANES : (s + 1) * 16 * LANES])

    sums, total = (nothing,) * 6, None
    for s in range(GROUPS):
        sums = backward(s, sums)
        part = scatter(s)
        total = part if total is None else total + part
    total = total[0:12] + total[12:24]
    centre = jnp.concatenate([jnp.sum(value, axis=0, keepdims=True) for value in sums], axis=0)
    pad = jnp.zeros((2, LANES), F32)
    out_ref[0:8] = jnp.concatenate([total[6:12], pad], axis=0)
    out_ref[8:16] = jnp.concatenate([total[0:6] - centre, pad], axis=0)


def returned_sum(returned, border0, border1):
    row = lax.broadcasted_iota(jnp.int32, (8, LANES), 0)
    place = lax.broadcasted_iota(jnp.int32, (LANES, LANES), 0)
    lhs, rhs = [], []
    for which, border in enumerate((border0, border1)):
        three = returned[which * 3 : which * 3 + 3]
        twice = jnp.concatenate([three, three, jnp.zeros((2, LANES), F32)], axis=0)
        meant = (border // LANES == 1) == (row >= 3)
        kept = jnp.where(meant, twice, 0.0)
        lhs.append(jnp.concatenate(split_parts(kept, 3), axis=0).astype(BF16))
        rhs.append((place == (border & (LANES - 1))).astype(F32).astype(BF16))
    total = nt_dot(jnp.concatenate(lhs, axis=1), jnp.concatenate(rhs, axis=1))
    return total[0:8] + total[8:16] + total[16:24]


def moved(state, own_grad, ghosts, domain):
    border0 = state[14:15].astype(jnp.int32)
    border1 = state[15:16].astype(jnp.int32)
    inverse = rows_of_two(state[6:7], state[7:8])
    returned = four_sets(*(ghosts[domain + offset] for offset in (1, -1, 2, -2)))
    grad = own_grad + returned_sum(returned, border0, border1)
    speed = state[8:16] - TIME_STEP * grad * inverse
    return state[0:8] + TIME_STEP * speed, speed, border0, border1


def step_kernel(where_ref, home_ref, far_ref, wide_ref, next_ref, around_ref):
    blocks = [wide_ref.at[0, 0], wide_ref.at[0, 1], wide_ref.at[1, 1]]
    first_chip = where_ref[5:6] == 0

    def forces(domain, rows):
        one, other = (blocks[k // 4][k % 4 // 2, k % 2, rows] for k in (domain + 4, domain + 6))
        return jnp.where(first_chip, one, other)

    states = dict(zip((-2, -1, 2, 3), around(far_ref, STATE)))
    states[0], states[1] = home_ref[0, STATE], home_ref[1, STATE]
    ghosts = {domain: forces(domain, GHOSTS) for domain in range(-4, 6)}
    for domain, state in states.items():
        place, speed, border0, border1 = moved(state, forces(domain, OWN), ghosts, domain)
        sent = border_positions(place, border0, border1)
        if domain in (0, 1):
            next_ref[domain, SENT] = sent
            next_ref[domain, 8:14] = place[0:6]
            next_ref[domain, 14:16] = state[6:8]
            next_ref[domain, 16:22] = speed[0:6]
            next_ref[domain, 22:24] = state[14:16]
        else:
            around_ref[domain + 2 if domain < 0 else domain] = sent


def last_kernel(where_ref, home_ref, near_ref, far_ref, next_ref):
    ghosts = dict(zip((-2, -1, 2, 3), around(far_ref, GHOSTS)))
    ghosts[0], ghosts[1] = near_ref[0, GHOSTS], near_ref[1, GHOSTS]
    for domain in range(2):
        place, speed, _, _ = moved(home_ref[domain, STATE], near_ref[domain, OWN], ghosts, domain)
        next_ref[domain, 0:6] = place[0:6]
        next_ref[domain, 6:8] = jnp.broadcast_to(where_ref[4:5], (2, LANES))
        next_ref[domain, 8:16] = speed


def swap_kernel(where_ref, own_ref, mate_ref, x_out, v_out, x_ref, v_ref, sems):
    core, swaps, side, position = (where_ref[k : k + 1] == 0 for k in range(4))

    def of_core(pair):
        return jnp.where(core, pair[0], pair[1])

    def of_side(s):
        return of_core(jnp.where(position, mate_ref[s, 0], mate_ref[s, 1]))

    mine = of_core(own_ref)
    chosen = jnp.where(swaps, mine, jnp.where(side, of_side(0), of_side(1)))
    scale = jnp.sqrt(mine[6:7] / chosen[6:7])
    put_flat(x_ref, chosen[0:6])
    put_flat(v_ref, chosen[8:14] * scale)
    bring((x_ref, v_ref), (x_out, v_out), sems)


def vmem():
    return pl.BlockSpec(memory_space=pltpu.VMEM)


def smem():
    return pl.BlockSpec(memory_space=pltpu.SMEM)


def tiles(*shape):
    return jax.ShapeDtypeStruct(shape + (LANES,), F32)


def call(kernel, scalars, arrays, out_shape, scratch=(), flops=10**6, inputs=None, outputs=None,
         limit=24 * 2**20):
    outputs = outputs or vmem
    out_specs = [outputs() for _ in out_shape] if isinstance(out_shape, list) else outputs()
    return pl.pallas_call(
        kernel,
        out_shape=out_shape,
        in_specs=[smem()] * len(scalars) + [(inputs or vmem)()] * len(arrays),
        out_specs=out_specs,
        scratch_shapes=list(scratch),
        cost_estimate=pl.CostEstimate(flops=flops, bytes_accessed=10**6, transcendentals=0),
        compiler_params=pltpu.CompilerParams(vmem_limit_bytes=limit),
    )(*scalars, *arrays)


def anywhere():
    return pl.BlockSpec(memory_space=pltpu.HBM)


def landing(arrays):
    return [pltpu.VMEM(a.shape, a.dtype) for a in arrays] + [pltpu.SemaphoreType.DMA((len(arrays),))]


def weight_shapes():
    return [
        jax.ShapeDtypeStruct((8 * HIDDEN, LANES), BF16),
        jax.ShapeDtypeStruct((32, HIDDEN), BF16),
        jax.ShapeDtypeStruct((16, LANES), BF16),
        tiles(16),
        tiles(HIDDEN),
        jax.ShapeDtypeStruct((LANES, SLOTS * 2 * LANES), BF16),
        tiles(HIDDEN),
        jax.ShapeDtypeStruct((HIDDEN, N_BASIS), BF16),
        jax.ShapeDtypeStruct((HIDDEN, HIDDEN), BF16),
        jax.ShapeDtypeStruct((HIDDEN, HIDDEN), BF16),
    ]


def begin_shapes(arrays):
    through = [jax.ShapeDtypeStruct(arrays[k].shape, arrays[k].dtype) for k in (5, 6, 7, 2, 10)]
    space = landing([arrays[k] for k in (0, 1, 3, 4, 8, 9, 11, 12)])
    space[3] = pltpu.SMEM(arrays[4].shape, F32)
    space[-1] = pltpu.SemaphoreType.DMA((len(arrays),))
    made = [tiles(24)] + weight_shapes() + through
    return made, space


def force_scratch():
    return [
        pltpu.VMEM((GROUPS, 128, 2 * LANES), BF16),
        pltpu.VMEM((GROUPS, 64, 2 * LANES), F32),
        pltpu.VMEM((6, GROUPS, 8, 2 * LANES), F32),
        pltpu.VMEM((GROUPS, 8, 2 * LANES), F32),
        pltpu.VMEM((GROUPS * 64, LANES), F32),
        pltpu.VMEM((GROUPS * 64, LANES), F32),
    ] + [pltpu.VMEM((8 * 24, LANES), F32)] * (2 * GROUPS) + [pltpu.VMEM((AHEAD * HIDDEN, 2 * LANES), F32)]


def on_chip(value, domains):
    groups = [[2 * i, 2 * i + 1] for i in range(domains // 2)]
    return lax.all_gather(value, "space", axis_index_groups=groups)


def across_chips(value, domains, chips=1):
    groups = [[(2 * (i - chips) + 1) % domains, 2 * i] for i in range(domains // 2)]
    return lax.all_gather(value, "space", axis_index_groups=groups)


def across_pair(value, domains):
    groups = [[4 * i + core, 4 * i + 2 + core] for i in range(domains // 4) for core in range(2)]
    return lax.all_gather(value, "space", axis_index_groups=groups)


def along_ladder(value, rungs, domains):
    groups = []
    for domain in range(domains):
        shift = domain % 2
        for low in range(shift, rungs - shift, 2):
            groups.append([low * domains + domain, (low + 1) * domains + domain])
        if shift and domain // 2 % 2 == 0:
            for end in (0, rungs - 1):
                groups.append([end * domains + domain, end * domains + domain + 2])
    return lax.all_gather(value, ("replica", "space"), axis_index_groups=groups)


def on_device(
    particle_coordinates,
    particle_motions,
    particle_kinds,
    filled_totals,
    adjacent_particles,
    adjacent_place_kinds,
    border_particle_numbers,
    reciprocal_kind_inertia,
    thermal_levels,
    swap_mates,
    bond_intake_coefficients,
    bond_output_coefficients,
    particle_opening_coefficients,
    particle_middle_coefficients,
    particle_output_coefficients,
):
    domains, rungs = lax.axis_size("space"), lax.axis_size("replica")
    core = lax.axis_index("space") % 2
    rank = lax.axis_index("replica")
    mate = swap_mates[0]
    odd = rank % 2
    side = jnp.where((mate > rank) == (odd == 0), 0, 1)
    position = jnp.where(side == 0, 1 - odd, odd)
    where_to = [value.astype(F32) for value in (core, mate != rank, side, position)]
    chip = lax.axis_index("space") // 2 % 2
    where_to = jnp.stack(where_to + [thermal_levels[0], chip.astype(F32)])
    where_to = jnp.broadcast_to(where_to[:, None], (6, LANES))

    arrays = (
        particle_coordinates.reshape(1, -1),
        particle_motions.reshape(1, -1),
        particle_kinds,
        border_particle_numbers,
        reciprocal_kind_inertia,
        adjacent_particles,
        adjacent_place_kinds,
        filled_totals,
        bond_intake_coefficients.T,
        bond_output_coefficients[None],
        particle_opening_coefficients.T,
        particle_middle_coefficients,
        particle_output_coefficients[None],
    )
    arrays = tuple(pltpu.with_memory_space_constraint(a, pltpu.HBM) for a in arrays)
    made, space = begin_shapes(arrays)
    begin, *fixed = call(begin_kernel, (), arrays, made, space, inputs=anywhere)
    home = on_chip(begin, domains)
    far = on_chip(across_chips(home, domains), domains)
    for step in range(STEPS):
        partial = call(force_kernel, (), (where_to, home, far, *fixed), tiles(16), force_scratch())
        near = on_chip(partial, domains)
        if step < STEPS - 1:
            pair = across_pair(near, domains)
            wide = on_chip(across_chips(pair, domains, 2), domains)
            shapes = [tiles(2, 24), tiles(4, 8)]
            home, far = call(step_kernel, (), (where_to, home, far, wide), shapes)
        else:
            far = on_chip(across_chips(near[:, GHOSTS], domains), domains)
            state = call(last_kernel, (), (where_to, home, near, far), tiles(2, 16))
    mates = on_chip(along_ladder(state, rungs, domains), domains)
    shape = particle_coordinates.shape
    out = jax.ShapeDtypeStruct((1, particle_coordinates.size), F32)
    scratch = landing((out, out))
    new_x, new_v = call(
        swap_kernel, (), (where_to, state, mates), [out, out], scratch, outputs=anywhere
    )
    return new_x.reshape(shape), new_v.reshape(shape)


def solution(mesh):
    return jax.shard_map(
        on_device,
        mesh=mesh,
        in_specs=(
            P("replica", None, "space"),
            P("replica", None, "space"),
            P("replica", "space"),
            P("replica", "space"),
            P("replica", None, "space"),
            P("replica", None, "space"),
            P("replica", None, "space"),
            P(),
            P("replica"),
            P("replica"),
            P(),
            P(),
            P(),
            P(),
            P(),
        ),
        out_specs=(P("replica", None, "space"), P("replica", None, "space")),
        check_vma=False,
    )
```

```python
import functools

import jax
import jax.numpy as jnp
from jax import lax
from jax.experimental import pallas as pl
from jax.experimental.pallas import tpu as pltpu
from jax.sharding import PartitionSpec as P

STEPS = 2
TIME_STEP = 0.05
CUT_SQ = 9.0
N_BASIS = 8
N_KIND = 6
LANES = 128
SLOTS = 32
GROUPS = SLOTS // 8
HIDDEN = 256
AHEAD = 4
SENT, STATE = slice(0, 8), slice(8, 24)
GHOSTS, OWN = slice(0, 8), slice(8, 16)
SHARP = (N_BASIS / CUT_SQ) ** 2
CENTRES = [CUT_SQ * c / (N_BASIS - 1) for c in range(N_BASIS)]
F32 = jnp.float32
BF16 = jnp.bfloat16


def nt_dot(a, b):
    return lax.dot_general(a, b, (((1,), (1,)), ((), ())), preferred_element_type=F32)


def tn_dot(a, b):
    return lax.dot_general(a, b, (((0,), (0,)), ((), ())), preferred_element_type=F32)


def nn_dot(a, b):
    return lax.dot_general(a, b, (((1,), (0,)), ((), ())), preferred_element_type=F32)


def tile_of(flat_ref):
    rows = [
        flat_ref[:, (comp * 2 + chunk) * LANES : (comp * 2 + chunk + 1) * LANES]
        for chunk in range(2)
        for comp in range(3)
    ]
    return jnp.concatenate(rows, axis=0)


def put_flat(flat_ref, tile):
    for chunk in range(2):
        for comp in range(3):
            start = (comp * 2 + chunk) * LANES
            row = chunk * 3 + comp
            flat_ref[:, start : start + LANES] = tile[row : row + 1]


def rows_of_two(first, second, pad_with=None):
    shape = (3, LANES)
    pad = jnp.zeros((2, LANES), first.dtype)
    return jnp.concatenate(
        [jnp.broadcast_to(first, shape), jnp.broadcast_to(second, shape), pad], axis=0
    )


def take_lanes(table, lane):
    return jnp.take_along_axis(table, lane, axis=1, mode="promise_in_bounds")


def border_positions(tile, border0, border1):
    index = rows_of_two(border0, border1)
    pad = jnp.zeros((2, LANES), F32)
    low = jnp.concatenate([tile[0:3], tile[0:3], pad], axis=0)
    high = jnp.concatenate([tile[3:6], tile[3:6], pad], axis=0)
    lane = index & (LANES - 1)
    return jnp.where(index < LANES, take_lanes(low, lane), take_lanes(high, lane))


def four_sets(set0, set1, set2, set3):
    row = lax.broadcasted_iota(jnp.int32, (8, LANES), 0)
    col = lax.broadcasted_iota(jnp.int32, (8, LANES), 1)
    left = col < LANES // 2
    return jnp.where(row < 3, jnp.where(left, set0, set1), jnp.where(left, set2, set3))


def split_parts(value, count):
    parts = []
    for _ in range(count):
        part = value.astype(BF16).astype(F32)
        parts.append(part)
        value = value - part
    return parts


def bring(sources, targets, sems):
    copies = [
        pltpu.make_async_copy(source, target, sems.at[k])
        for k, (source, target) in enumerate(zip(sources, targets))
    ]
    for copy in copies:
        copy.start()
    for copy in copies:
        copy.wait()


def fed_columns():
    feature = lax.broadcasted_iota(jnp.int32, (28, LANES), 0)
    col = lax.broadcasted_iota(jnp.int32, (28, LANES), 1)
    block, which = col // 8, col % 8
    radial = (block < 8) & (feature == block)
    environ = (block == 8) & (feature == 8 + which)
    centre = (block == 9) & (which < N_KIND) & (feature == 16 + which)
    neigh = (block >= 10) & (feature == 22 + block - 10)
    return (radial | environ | centre | neigh).astype(F32)


def own_columns(slot, rows):
    col = lax.broadcasted_iota(jnp.int32, (rows, LANES), 1)
    return ((col // 8 == 8) | (col // 8 == 9) | (col % 8 == slot)).astype(F32)


def two_parts(value):
    high, low = split_parts(value, 2)
    return jnp.concatenate([high, low], axis=0).astype(BF16)


def begin_kernel(*refs):
    inputs, refs = refs[:13], refs[13:]
    (out_ref, up_ref, down_ref, line_ref, flat_ref, sum_ref, hot_ref, atom_ref, first_ref,
     second_ref, back_ref, index_ref, place_ref, total_ref, kind_ref, opening_ref), refs = (
        refs[:16], refs[16:]
    )
    x_ref, v_ref, border_ref, inertia_ref, intake_ref, edge_out_ref, middle_ref, atom_out_ref = (
        refs[:8]
    )
    landed = (
        x_ref, v_ref, kind_ref, border_ref, inertia_ref, index_ref, place_ref, total_ref,
        intake_ref, edge_out_ref, opening_ref, middle_ref, atom_out_ref,
    )
    bring(inputs, landed, refs[8])

    x_tile = tile_of(x_ref)
    border = border_ref[0]
    border0 = jnp.concatenate([border[0:1], border[1:2]], axis=1)
    border1 = jnp.concatenate([border[2:3], border[3:4]], axis=1)
    kind = kind_ref[...]
    inverse = jnp.zeros(kind.shape, F32)
    for k in range(N_KIND):
        inverse = jnp.where(kind == k, inertia_ref[k], inverse)
    out_ref[0:8] = border_positions(x_tile, border0, border1)
    out_ref[8:14] = x_tile
    out_ref[14:15] = inverse[:, :LANES]
    out_ref[15:16] = inverse[:, LANES:]
    out_ref[16:22] = tile_of(v_ref)
    out_ref[22:23] = border0.astype(F32)
    out_ref[23:24] = border1.astype(F32)

    place = lax.broadcasted_iota(jnp.int32, (LANES, 2 * LANES), 0).astype(F32).astype(BF16)
    one, none = jnp.asarray(1.0, BF16), jnp.asarray(0.0, BF16)

    def group(s, carry):
        for j in range(8):
            lane = (index_ref[0, pl.ds(s * 8 + j, 1), :] & (LANES - 1)).astype(F32)
            lane = jnp.broadcast_to(lane, (16, 2 * LANES)).astype(BF16)
            lane = jnp.concatenate([lane] * (LANES // 16), axis=0)
            cols = pl.ds(pl.multiple_of((s * 8 + j) * 2 * LANES, 2 * LANES), 2 * LANES)
            hot_ref[:, cols] = jnp.where(place == lane, one, none)
        return carry

    lax.fori_loop(0, GROUPS, group, 0)
    intake = intake_ref[...]
    fed = fed_columns()
    for j in range(8):
        up = (0.5 * fed * own_columns(j, 1)).astype(BF16)
        up_ref[j * HIDDEN : (j + 1) * HIDDEN, :] = tn_dot(intake, up).astype(BF16)
    edge_w = edge_out_ref[...]
    weighted = intake.astype(F32) * (0.5 * edge_w)
    down_ref[...] = two_parts(weighted[0:16])
    line = jnp.sum(weighted, axis=1, keepdims=True)
    flat_ref[...] = jnp.broadcast_to(line[0:16], (16, LANES))
    line = jnp.sum(fed * line, axis=0, keepdims=True)
    slot = lax.broadcasted_iota(jnp.int32, (8, LANES), 0)
    line_ref[...] = two_parts(own_columns(slot, 8) * line)
    sum_ref[...] = jnp.transpose(jnp.broadcast_to(edge_w, (LANES, HIDDEN)))
    atom_ref[...] = jnp.transpose(jnp.broadcast_to(0.5 * atom_out_ref[...], (LANES, HIDDEN)))
    first_ref[...] = jnp.transpose((0.5 * opening_ref[...]).astype(F32)).astype(BF16)
    second_ref[...] = 0.5 * middle_ref[...]
    back_ref[...] = middle_ref[...]


def around(where_ref, far_ref, rows):
    if len(far_ref.shape) == 3:
        return [far_ref[k, rows] for k in range(4)]
    first_chip = where_ref[5:6] == 0
    before = [jnp.where(first_chip, far_ref[1, 0, k, rows], far_ref[0, 0, k, rows]) for k in range(2)]
    after = [jnp.where(first_chip, far_ref[0, 1, k, rows], far_ref[1, 1, k, rows]) for k in range(2)]
    return before + after


def force_kernel(
    where_ref,
    home_ref,
    far_ref,
    up_ref,
    down_ref,
    line_ref,
    flat_ref,
    sum_ref,
    hot_ref,
    atom_ref,
    first_ref,
    second_ref,
    back_ref,
    index_ref,
    place_kind_ref,
    total_ref,
    kind_ref,
    opening_ref,
    out_ref,
    feat_ref,
    gauss_ref,
    geo_ref,
    energy_ref,
    gin0_ref,
    gin1_ref,
    *scratch,
):
    scat, ahead_ref = (scratch[:GROUPS], scratch[GROUPS : 2 * GROUPS]), scratch[2 * GROUPS]
    first_core = where_ref[0:1] == 0
    own = jnp.where(first_core, home_ref[0, STATE], home_ref[1, STATE])
    minus2, minus1, plus2, plus3 = around(where_ref, far_ref, SENT)
    near0, near1 = home_ref[0, SENT], home_ref[1, SENT]

    def pick(a, b):
        return jnp.where(first_core, a, b)

    ghost = four_sets(
        pick(minus1, near0), pick(near1, plus2), pick(minus2, minus1), pick(plus2, plus3)
    )

    kind_rows = lax.broadcasted_iota(jnp.int32, (8, 2 * LANES), 0)
    centre_hot = (kind_rows == kind_ref[...]).astype(F32)
    slot_row = lax.broadcasted_iota(jnp.int32, (8, LANES), 0)
    tables = [
        [jnp.broadcast_to(t[r * 3 + c : r * 3 + c + 1], (8, LANES)) for c in range(3)]
        for t in (own, ghost)
        for r in range(2)
    ]

    def geometry(s, sums):
        sums = list(sums)
        slots = pl.ds(pl.multiple_of(s * 8, 8), 8)
        radials = [[], []]
        for h in range(2):
            cols = slice(h * LANES, (h + 1) * LANES)
            index = index_ref[0, slots, cols]
            lane = index & (LANES - 1)
            chunk = index // LANES
            dist_sq = None
            for comp in range(3):
                found = take_lanes(tables[0][comp], lane)
                for which in range(1, 4):
                    found = jnp.where(chunk == which, take_lanes(tables[which][comp], lane), found)
                vec = found - tables[h][comp]
                geo_ref[comp, s, :, cols] = vec
                dist_sq = vec * vec if comp == 0 else dist_sq + vec * vec
            live = slot_row + s * 8 < total_ref[:, cols]
            inside = 1.0 - dist_sq * (1.0 / CUT_SQ)
            used = live & (inside > 0.0)
            cutoff = jnp.where(used, inside * inside, 0.0)
            geo_ref[3, s, :, cols] = dist_sq
            geo_ref[4, s, :, cols] = cutoff
            geo_ref[5, s, :, cols] = jnp.where(used, inside * (-2.0 / CUT_SQ), 0.0)
            for c in range(N_BASIS):
                gap = dist_sq - CENTRES[c]
                gauss = jnp.exp(-SHARP * (gap * gap))
                gauss_ref[s, c * 8 : c * 8 + 8, cols] = gauss
                radial = gauss * cutoff
                radials[h].append(radial)
                sums[h * N_BASIS + c] = sums[h * N_BASIS + c] + radial
        place_kind = place_kind_ref[0, slots, :]
        rows = [jnp.concatenate([a, b], axis=1) for a, b in zip(*radials)]
        feat_ref[s, 0:64] = jnp.concatenate(rows, axis=0).astype(BF16)
        rows = [(place_kind == k).astype(F32) for k in range(N_KIND)]
        feat_ref[s, 80:128] = jnp.concatenate(rows, axis=0).astype(BF16)
        return tuple(sums)

    nothing = jnp.zeros((8, LANES), F32)
    sums = lax.fori_loop(0, GROUPS, geometry, (nothing,) * (2 * N_BASIS))
    rows = [jnp.sum(value, axis=0, keepdims=True) for value in sums]
    environ = jnp.concatenate(
        [jnp.concatenate(rows[:N_BASIS], axis=0), jnp.concatenate(rows[N_BASIS:], axis=0)], axis=1
    )
    shared = jnp.concatenate([environ, centre_hot], axis=0).astype(BF16)
    for s in range(GROUPS):
        feat_ref[s, 64:80] = shared

    atom_w = jnp.concatenate([atom_ref[...], atom_ref[...]], axis=1)
    half = nn_dot(first_ref[...], environ.astype(BF16))
    th = jnp.tanh(half)
    hidden_one = (half + half * th).astype(BF16)
    slope_one = 0.5 * (1.0 + th + half * (1.0 - th * th))
    half = nn_dot(second_ref[...], hidden_one)
    th = jnp.tanh(half)
    g_second = (atom_w * (1.0 + th + half * (1.0 - th * th))).astype(BF16)
    g_hidden = tn_dot(back_ref[...], g_second)
    g_first = (g_hidden * slope_one).astype(BF16)
    g_env = nn_dot(opening_ref[...], g_first)

    flat = jnp.concatenate([flat_ref[...], flat_ref[...]], axis=1)
    slot = lax.broadcasted_iota(jnp.int32, (16, HIDDEN), 0)
    quarter = lax.broadcasted_iota(jnp.int32, (16, HIDDEN), 1) // (HIDDEN // 4)
    members = [(slot == quarter + 4 * k).astype(F32).astype(BF16) for k in range(2)]

    def first_forward(s):
        ahead_ref[...] = nn_dot(up_ref[: AHEAD * HIDDEN, :], feat_ref[s])

    def group(s, g_env):
        feat = feat_ref[s]
        line = nn_dot(line_ref[...], feat)
        energy = line[0:8] + line[8:16]
        folded = []
        edge_w = sum_ref[...].astype(BF16)
        edge_w = jnp.concatenate([edge_w, edge_w], axis=1)

        def forward(k):
            many = nn_dot(up_ref[k * AHEAD * HIDDEN : (k + 1) * AHEAD * HIDDEN, :], feat)
            return [many[i * HIDDEN : (i + 1) * HIDDEN].astype(BF16) for i in range(AHEAD)]

        ahead = [ahead_ref[i * HIDDEN : (i + 1) * HIDDEN].astype(BF16) for i in range(AHEAD)]
        ahead += forward(1)
        for j in range(8):
            half = ahead.pop(0)
            if j == AHEAD:
                first_forward(jnp.minimum(s + 1, GROUPS - 1))
            th = jnp.tanh(half)
            rest = edge_w * (half * th)
            rest = rest[: HIDDEN // 2] + rest[HIDDEN // 2 :]
            folded.append(rest[: HIDDEN // 4] + rest[HIDDEN // 4 :])
            slope = th + half * (jnp.asarray(1.0, BF16) - th * th)
            g_in = nn_dot(down_ref[...], slope)
            cut = geo_ref[4, s, j : j + 1, :]
            g_in = (g_in[0:16] + g_in[16:32] + flat) * cut
            rows = pl.ds(s * 64 + j, 8, stride=8)
            gin0_ref[rows, :] = g_in[0:8, :LANES]
            gin1_ref[rows, :] = g_in[0:8, LANES:]
            g_env = g_env + g_in[8:16]
        for k in range(2):
            rest = jnp.concatenate(folded[k * 4 : k * 4 + 4], axis=0)
            energy = energy + nn_dot(members[k], rest)[0:8]
        energy_ref[s] = energy
        return g_env

    first_forward(0)
    g_env = lax.fori_loop(1, GROUPS, group, group(0, g_env))

    def backward(s, sums):
        sums = list(sums)
        slots = slice(s * 8, s * 8 + 8)
        for h in range(2):
            cols = slice(h * LANES, (h + 1) * LANES)
            dist_sq, cutoff, slope = (geo_ref[k, s, :, cols] for k in (3, 4, 5))
            g_cut = energy_ref[s, :, cols]
            g_gap = None
            gin = (gin0_ref, gin1_ref)[h]
            for c in range(N_BASIS):
                rows = slice(s * 64 + c * 8, s * 64 + c * 8 + 8)
                g_radial = gin[rows, :] + g_env[c : c + 1, cols]
                q = g_radial * gauss_ref[s, c * 8 : c * 8 + 8, cols]
                g_cut = g_cut + q
                moment = q * (dist_sq - CENTRES[c])
                g_gap = moment if g_gap is None else g_gap + moment
            g_dist = (-4.0 * SHARP) * (cutoff * g_gap) + 2.0 * (g_cut * slope)
            chunk = index_ref[0, slots, cols] // LANES
            target = scat[h][s]
            for comp in range(3):
                g_vec = g_dist * geo_ref[comp, s, :, cols]
                sums[h * 3 + comp] = sums[h * 3 + comp] + g_vec
                for part, value in enumerate(split_parts(g_vec, 2)):
                    for which in range(4):
                        row = part * 12 + which * 3 + comp
                        target[pl.ds(row, 8, stride=24), :] = jnp.where(chunk == which, value, 0.0)
        return tuple(sums)

    def scatter(s):
        lhs = []
        for j in range(8):
            rows = slice(j * 24, j * 24 + 24)
            lhs.append(jnp.concatenate([half[s][rows, :] for half in scat], axis=1).astype(BF16))
        return nt_dot(jnp.concatenate(lhs, axis=1), hot_ref[:, s * 16 * LANES : (s + 1) * 16 * LANES])

    sums, total = (nothing,) * 6, None
    for s in range(GROUPS):
        sums = backward(s, sums)
        part = scatter(s)
        total = part if total is None else total + part
    total = total[0:12] + total[12:24]
    centre = jnp.concatenate([jnp.sum(value, axis=0, keepdims=True) for value in sums], axis=0)
    pad = jnp.zeros((2, LANES), F32)
    out_ref[0:8] = jnp.concatenate([total[6:12], pad], axis=0)
    out_ref[8:16] = jnp.concatenate([total[0:6] - centre, pad], axis=0)


def returned_sum(returned, border0, border1):
    row = lax.broadcasted_iota(jnp.int32, (8, LANES), 0)
    place = lax.broadcasted_iota(jnp.int32, (LANES, LANES), 0)
    lhs, rhs = [], []
    for which, border in enumerate((border0, border1)):
        three = returned[which * 3 : which * 3 + 3]
        twice = jnp.concatenate([three, three, jnp.zeros((2, LANES), F32)], axis=0)
        meant = (border // LANES == 1) == (row >= 3)
        kept = jnp.where(meant, twice, 0.0)
        lhs.append(jnp.concatenate(split_parts(kept, 3), axis=0).astype(BF16))
        rhs.append((place == (border & (LANES - 1))).astype(F32).astype(BF16))
    total = nt_dot(jnp.concatenate(lhs, axis=1), jnp.concatenate(rhs, axis=1))
    return total[0:8] + total[8:16] + total[16:24]


def moved(state, own_grad, ghosts, domain):
    border0 = state[14:15].astype(jnp.int32)
    border1 = state[15:16].astype(jnp.int32)
    inverse = rows_of_two(state[6:7], state[7:8])
    returned = four_sets(*(ghosts[domain + offset] for offset in (1, -1, 2, -2)))
    grad = own_grad + returned_sum(returned, border0, border1)
    speed = state[8:16] - TIME_STEP * grad * inverse
    return state[0:8] + TIME_STEP * speed, speed, border0, border1


def step_kernel(where_ref, home_ref, far_ref, wide_ref, next_ref, around_ref):
    first_chip, even_pair = where_ref[5:6] == 0, where_ref[6:7] == 0
    blocks = (
        (wide_ref.at[1, 0], wide_ref.at[0, 0]),
        (wide_ref.at[0, 0], wide_ref.at[0, 1]),
        (wide_ref.at[0, 1], wide_ref.at[1, 1]),
    )

    def on_line(k, rows):
        even, odd = (block[k % 4 // 2, k % 2, rows] for block in blocks[k // 4])
        return jnp.where(even_pair, even, odd)

    def forces(domain, rows):
        return jnp.where(first_chip, on_line(domain + 4, rows), on_line(domain + 6, rows))

    states = dict(zip((-2, -1, 2, 3), around(where_ref, far_ref, STATE)))
    states[0], states[1] = home_ref[0, STATE], home_ref[1, STATE]
    ghosts = {domain: forces(domain, GHOSTS) for domain in range(-4, 6)}
    for domain, state in states.items():
        place, speed, border0, border1 = moved(state, forces(domain, OWN), ghosts, domain)
        sent = border_positions(place, border0, border1)
        if domain in (0, 1):
            next_ref[domain, SENT] = sent
            next_ref[domain, 8:14] = place[0:6]
            next_ref[domain, 14:16] = state[6:8]
            next_ref[domain, 16:22] = speed[0:6]
            next_ref[domain, 22:24] = state[14:16]
        else:
            around_ref[domain + 2 if domain < 0 else domain] = sent


def last_kernel(where_ref, home_ref, near_ref, far_ref, next_ref):
    ghosts = dict(zip((-2, -1, 2, 3), around(where_ref, far_ref, GHOSTS)))
    ghosts[0], ghosts[1] = near_ref[0, GHOSTS], near_ref[1, GHOSTS]
    for domain in range(2):
        place, speed, _, _ = moved(home_ref[domain, STATE], near_ref[domain, OWN], ghosts, domain)
        next_ref[domain, 0:6] = place[0:6]
        next_ref[domain, 6:8] = jnp.broadcast_to(where_ref[4:5], (2, LANES))
        next_ref[domain, 8:16] = speed


def swap_kernel(where_ref, own_ref, mate_ref, x_out, v_out, x_ref, v_ref, sems):
    core, swaps, side, position = (where_ref[k : k + 1] == 0 for k in range(4))

    def of_core(pair):
        return jnp.where(core, pair[0], pair[1])

    def of_side(s):
        return of_core(jnp.where(position, mate_ref[s, 0], mate_ref[s, 1]))

    mine = of_core(own_ref)
    chosen = jnp.where(swaps, mine, jnp.where(side, of_side(0), of_side(1)))
    scale = jnp.sqrt(mine[6:7] / chosen[6:7])
    put_flat(x_ref, chosen[0:6])
    put_flat(v_ref, chosen[8:14] * scale)
    bring((x_ref, v_ref), (x_out, v_out), sems)


def vmem():
    return pl.BlockSpec(memory_space=pltpu.VMEM)


def smem():
    return pl.BlockSpec(memory_space=pltpu.SMEM)


def tiles(*shape):
    return jax.ShapeDtypeStruct(shape + (LANES,), F32)


def call(kernel, scalars, arrays, out_shape, scratch=(), flops=10**6, inputs=None, outputs=None,
         limit=24 * 2**20):
    outputs = outputs or vmem
    out_specs = [outputs() for _ in out_shape] if isinstance(out_shape, list) else outputs()
    return pl.pallas_call(
        kernel,
        out_shape=out_shape,
        in_specs=[smem()] * len(scalars) + [(inputs or vmem)()] * len(arrays),
        out_specs=out_specs,
        scratch_shapes=list(scratch),
        cost_estimate=pl.CostEstimate(flops=flops, bytes_accessed=10**6, transcendentals=0),
        compiler_params=pltpu.CompilerParams(vmem_limit_bytes=limit),
    )(*scalars, *arrays)


def anywhere():
    return pl.BlockSpec(memory_space=pltpu.HBM)


def landing(arrays):
    return [pltpu.VMEM(a.shape, a.dtype) for a in arrays] + [pltpu.SemaphoreType.DMA((len(arrays),))]


def weight_shapes():
    return [
        jax.ShapeDtypeStruct((8 * HIDDEN, LANES), BF16),
        jax.ShapeDtypeStruct((32, HIDDEN), BF16),
        jax.ShapeDtypeStruct((16, LANES), BF16),
        tiles(16),
        tiles(HIDDEN),
        jax.ShapeDtypeStruct((LANES, SLOTS * 2 * LANES), BF16),
        tiles(HIDDEN),
        jax.ShapeDtypeStruct((HIDDEN, N_BASIS), BF16),
        jax.ShapeDtypeStruct((HIDDEN, HIDDEN), BF16),
        jax.ShapeDtypeStruct((HIDDEN, HIDDEN), BF16),
    ]


def begin_shapes(arrays):
    through = [jax.ShapeDtypeStruct(arrays[k].shape, arrays[k].dtype) for k in (5, 6, 7, 2, 10)]
    space = landing([arrays[k] for k in (0, 1, 3, 4, 8, 9, 11, 12)])
    space[3] = pltpu.SMEM(arrays[4].shape, F32)
    space[-1] = pltpu.SemaphoreType.DMA((len(arrays),))
    made = [tiles(24)] + weight_shapes() + through
    return made, space


def force_scratch():
    return [
        pltpu.VMEM((GROUPS, 128, 2 * LANES), BF16),
        pltpu.VMEM((GROUPS, 64, 2 * LANES), F32),
        pltpu.VMEM((6, GROUPS, 8, 2 * LANES), F32),
        pltpu.VMEM((GROUPS, 8, 2 * LANES), F32),
        pltpu.VMEM((GROUPS * 64, LANES), F32),
        pltpu.VMEM((GROUPS * 64, LANES), F32),
    ] + [pltpu.VMEM((8 * 24, LANES), F32)] * (2 * GROUPS) + [pltpu.VMEM((AHEAD * HIDDEN, 2 * LANES), F32)]


def on_chip(value, domains):
    groups = [[2 * i, 2 * i + 1] for i in range(domains // 2)]
    return lax.all_gather(value, "space", axis_index_groups=groups)


def across_chips(value, domains):
    groups = []
    for i in range(domains // 4):
        groups += [[4 * i, 4 * i + 2], [4 * i + 3, (4 * i + 5) % domains]]
    return lax.all_gather(value, "space", axis_index_groups=groups)


def across_pair(value, domains):
    groups = []
    for i in range(domains // 4):
        groups += [[4 * i, 4 * i + 3], [4 * i + 1, 4 * i + 2]]
    return lax.all_gather(value, "space", axis_index_groups=groups)


def between_pairs(value, domains):
    groups = []
    for i in range(0, domains // 4, 2):
        for chip in range(2):
            first = 4 * i + 2 * chip
            groups += [[first, first + 4], [first + 5, (first + 9) % domains]]
    return lax.all_gather(value, "space", axis_index_groups=groups)


def even_odd_core(rank, rungs):
    far = (rank % 4 == 0) | (rank % 4 == 3)
    return 1 - (far & (rank > 0) & (rank < rungs - 1))


def along_ladder(value, rungs, domains):
    groups = []
    for chip in range(0, domains, 2):
        for low in range(rungs - 1):
            pair = []
            for rank in (low, low + 1):
                core = even_odd_core(rank, rungs)
                pair.append(rank * domains + chip + (core if low % 2 == 0 else 1 - core))
            groups.append(pair)
        if chip % 4 == 0:
            for end in (0, rungs - 1):
                groups.append([end * domains + chip, end * domains + chip + 2])
    return lax.all_gather(value, ("replica", "space"), axis_index_groups=groups)


def on_device(
    particle_coordinates,
    particle_motions,
    particle_kinds,
    filled_totals,
    adjacent_particles,
    adjacent_place_kinds,
    border_particle_numbers,
    reciprocal_kind_inertia,
    thermal_levels,
    swap_mates,
    bond_intake_coefficients,
    bond_output_coefficients,
    particle_opening_coefficients,
    particle_middle_coefficients,
    particle_output_coefficients,
):
    domains, rungs = lax.axis_size("space"), lax.axis_size("replica")
    core = lax.axis_index("space") % 2
    rank = lax.axis_index("replica")
    mate = swap_mates[0]
    odd = rank % 2
    even_odd = (mate > rank) == (odd == 0)
    side = even_odd_core(rank, rungs)
    side = jnp.where(even_odd, side, 1 - side)
    position = jnp.where(even_odd, 1 - odd, odd)
    where_to = [value.astype(F32) for value in (core, mate != rank, side, position)]
    here = lax.axis_index("space")
    chip, pair = (here // 2 % 2).astype(F32), (here // 4 % 2).astype(F32)
    where_to = jnp.stack(where_to + [thermal_levels[0], chip, pair])
    where_to = jnp.broadcast_to(where_to[:, None], (7, LANES))

    arrays = (
        particle_coordinates.reshape(1, -1),
        particle_motions.reshape(1, -1),
        particle_kinds,
        border_particle_numbers,
        reciprocal_kind_inertia,
        adjacent_particles,
        adjacent_place_kinds,
        filled_totals,
        bond_intake_coefficients.T,
        bond_output_coefficients[None],
        particle_opening_coefficients.T,
        particle_middle_coefficients,
        particle_output_coefficients[None],
    )
    arrays = tuple(pltpu.with_memory_space_constraint(a, pltpu.HBM) for a in arrays)
    made, space = begin_shapes(arrays)
    begin, *fixed = call(begin_kernel, (), arrays, made, space, inputs=anywhere)
    home = on_chip(begin, domains)
    far = on_chip(across_chips(home, domains), domains)
    for step in range(STEPS):
        partial = call(force_kernel, (), (where_to, home, far, *fixed), tiles(16), force_scratch())
        near = on_chip(partial, domains)
        if step < STEPS - 1:
            pair = across_pair(near, domains)
            wide = on_chip(between_pairs(pair, domains), domains)
            shapes = [tiles(2, 24), tiles(4, 8)]
            home, far = call(step_kernel, (), (where_to, home, far, wide), shapes)
        else:
            far = on_chip(across_chips(near[:, GHOSTS], domains), domains)
            state = call(last_kernel, (), (where_to, home, near, far), tiles(2, 16))
    mates = on_chip(along_ladder(state, rungs, domains), domains)
    shape = particle_coordinates.shape
    out = jax.ShapeDtypeStruct((1, particle_coordinates.size), F32)
    scratch = landing((out, out))
    new_x, new_v = call(
        swap_kernel, (), (where_to, state, mates), [out, out], scratch, outputs=anywhere
    )
    return new_x.reshape(shape), new_v.reshape(shape)


def solution(mesh):
    return jax.shard_map(
        on_device,
        mesh=mesh,
        in_specs=(
            P("replica", None, "space"),
            P("replica", None, "space"),
            P("replica", "space"),
            P("replica", "space"),
            P("replica", None, "space"),
            P("replica", None, "space"),
            P("replica", None, "space"),
            P(),
            P("replica"),
            P("replica"),
            P(),
            P(),
            P(),
            P(),
            P(),
        ),
        out_specs=(P("replica", None, "space"), P("replica", None, "space")),
        check_vma=False,
    )
```

```python
import functools

import jax
import jax.numpy as jnp
from jax import lax
from jax.experimental import pallas as pl
from jax.experimental.pallas import tpu as pltpu
from jax.sharding import PartitionSpec as P

STEPS = 2
TIME_STEP = 0.05
CUT_SQ = 9.0
N_BASIS = 8
N_KIND = 6
LANES = 128
SLOTS = 32
GROUPS = SLOTS // 8
HIDDEN = 256
AHEAD = 4
SENT, STATE = slice(0, 8), slice(8, 24)
GHOSTS, OWN = slice(0, 8), slice(8, 16)
SHARP = (N_BASIS / CUT_SQ) ** 2
CENTRES = [CUT_SQ * c / (N_BASIS - 1) for c in range(N_BASIS)]
F32 = jnp.float32
BF16 = jnp.bfloat16


def nt_dot(a, b):
    return lax.dot_general(a, b, (((1,), (1,)), ((), ())), preferred_element_type=F32)


def tn_dot(a, b):
    return lax.dot_general(a, b, (((0,), (0,)), ((), ())), preferred_element_type=F32)


def nn_dot(a, b):
    return lax.dot_general(a, b, (((1,), (0,)), ((), ())), preferred_element_type=F32)


def tile_of(flat_ref):
    rows = [
        flat_ref[:, (comp * 2 + chunk) * LANES : (comp * 2 + chunk + 1) * LANES]
        for chunk in range(2)
        for comp in range(3)
    ]
    return jnp.concatenate(rows, axis=0)


def put_flat(flat_ref, tile):
    for chunk in range(2):
        for comp in range(3):
            start = (comp * 2 + chunk) * LANES
            row = chunk * 3 + comp
            flat_ref[:, start : start + LANES] = tile[row : row + 1]


def rows_of_two(first, second, pad_with=None):
    shape = (3, LANES)
    pad = jnp.zeros((2, LANES), first.dtype)
    return jnp.concatenate(
        [jnp.broadcast_to(first, shape), jnp.broadcast_to(second, shape), pad], axis=0
    )


def take_lanes(table, lane):
    return jnp.take_along_axis(table, lane, axis=1, mode="promise_in_bounds")


def border_positions(tile, border0, border1):
    index = rows_of_two(border0, border1)
    pad = jnp.zeros((2, LANES), F32)
    low = jnp.concatenate([tile[0:3], tile[0:3], pad], axis=0)
    high = jnp.concatenate([tile[3:6], tile[3:6], pad], axis=0)
    lane = index & (LANES - 1)
    return jnp.where(index < LANES, take_lanes(low, lane), take_lanes(high, lane))


def four_sets(set0, set1, set2, set3):
    row = lax.broadcasted_iota(jnp.int32, (8, LANES), 0)
    col = lax.broadcasted_iota(jnp.int32, (8, LANES), 1)
    left = col < LANES // 2
    return jnp.where(row < 3, jnp.where(left, set0, set1), jnp.where(left, set2, set3))


def split_parts(value, count):
    parts = []
    for _ in range(count):
        part = value.astype(BF16).astype(F32)
        parts.append(part)
        value = value - part
    return parts


def bring(sources, targets, sems):
    copies = [
        pltpu.make_async_copy(source, target, sems.at[k])
        for k, (source, target) in enumerate(zip(sources, targets))
    ]
    for copy in copies:
        copy.start()
    for copy in copies:
        copy.wait()


def fed_columns():
    feature = lax.broadcasted_iota(jnp.int32, (28, LANES), 0)
    col = lax.broadcasted_iota(jnp.int32, (28, LANES), 1)
    block, which = col // 8, col % 8
    radial = (block < 8) & (feature == block)
    environ = (block == 8) & (feature == 8 + which)
    centre = (block == 9) & (which < N_KIND) & (feature == 16 + which)
    neigh = (block >= 10) & (feature == 22 + block - 10)
    return (radial | environ | centre | neigh).astype(F32)


def own_columns(slot, rows):
    col = lax.broadcasted_iota(jnp.int32, (rows, LANES), 1)
    return ((col // 8 == 8) | (col // 8 == 9) | (col % 8 == slot)).astype(F32)


def two_parts(value):
    high, low = split_parts(value, 2)
    return jnp.concatenate([high, low], axis=0).astype(BF16)


def begin_kernel(*refs):
    inputs, refs = refs[:13], refs[13:]
    (out_ref, up_ref, down_ref, line_ref, flat_ref, sum_ref, hot_ref, atom_ref, first_ref,
     second_ref, back_ref, index_ref, place_ref, total_ref, kind_ref, opening_ref), refs = (
        refs[:16], refs[16:]
    )
    x_ref, v_ref, border_ref, inertia_ref, intake_ref, edge_out_ref, middle_ref, atom_out_ref = (
        refs[:8]
    )
    landed = (
        x_ref, v_ref, kind_ref, border_ref, inertia_ref, index_ref, place_ref, total_ref,
        intake_ref, edge_out_ref, opening_ref, middle_ref, atom_out_ref,
    )
    bring(inputs, landed, refs[8])

    x_tile = tile_of(x_ref)
    border = border_ref[0]
    border0 = jnp.concatenate([border[0:1], border[1:2]], axis=1)
    border1 = jnp.concatenate([border[2:3], border[3:4]], axis=1)
    kind = kind_ref[...]
    inverse = jnp.zeros(kind.shape, F32)
    for k in range(N_KIND):
        inverse = jnp.where(kind == k, inertia_ref[k], inverse)
    out_ref[0:8] = border_positions(x_tile, border0, border1)
    out_ref[8:14] = x_tile
    out_ref[14:15] = inverse[:, :LANES]
    out_ref[15:16] = inverse[:, LANES:]
    out_ref[16:22] = tile_of(v_ref)
    out_ref[22:23] = border0.astype(F32)
    out_ref[23:24] = border1.astype(F32)

    place = lax.broadcasted_iota(jnp.int32, (LANES, 2 * LANES), 0).astype(F32).astype(BF16)
    one, none = jnp.asarray(1.0, BF16), jnp.asarray(0.0, BF16)

    def group(s, carry):
        for j in range(8):
            lane = (index_ref[0, pl.ds(s * 8 + j, 1), :] & (LANES - 1)).astype(F32)
            lane = jnp.broadcast_to(lane, (16, 2 * LANES)).astype(BF16)
            lane = jnp.concatenate([lane] * (LANES // 16), axis=0)
            cols = pl.ds(pl.multiple_of((s * 8 + j) * 2 * LANES, 2 * LANES), 2 * LANES)
            hot_ref[:, cols] = jnp.where(place == lane, one, none)
        return carry

    lax.fori_loop(0, GROUPS, group, 0)
    intake = intake_ref[...]
    fed = fed_columns()
    for j in range(8):
        up = (0.5 * fed * own_columns(j, 1)).astype(BF16)
        up_ref[j * HIDDEN : (j + 1) * HIDDEN, :] = tn_dot(intake, up).astype(BF16)
    edge_w = edge_out_ref[...]
    weighted = intake.astype(F32) * (0.5 * edge_w)
    down_ref[...] = two_parts(weighted[0:16])
    line = jnp.sum(weighted, axis=1, keepdims=True)
    flat_ref[...] = jnp.broadcast_to(line[0:16], (16, LANES))
    line = jnp.sum(fed * line, axis=0, keepdims=True)
    slot = lax.broadcasted_iota(jnp.int32, (8, LANES), 0)
    line_ref[...] = two_parts(own_columns(slot, 8) * line)
    sum_ref[...] = jnp.transpose(jnp.broadcast_to(edge_w, (LANES, HIDDEN)))
    atom_ref[...] = jnp.transpose(jnp.broadcast_to(0.5 * atom_out_ref[...], (LANES, HIDDEN)))
    first_ref[...] = jnp.transpose((0.5 * opening_ref[...]).astype(F32)).astype(BF16)
    second_ref[...] = 0.5 * middle_ref[...]
    back_ref[...] = middle_ref[...]


def around(where_ref, far_ref, rows):
    if len(far_ref.shape) == 3:
        return [far_ref[k, rows] for k in range(4)]
    first_chip = where_ref[5:6] == 0
    before = [jnp.where(first_chip, far_ref[1, 0, k, rows], far_ref[0, 0, k, rows]) for k in range(2)]
    after = [jnp.where(first_chip, far_ref[0, 1, k, rows], far_ref[1, 1, k, rows]) for k in range(2)]
    return before + after


def force_kernel(
    where_ref,
    home_ref,
    far_ref,
    up_ref,
    down_ref,
    line_ref,
    flat_ref,
    sum_ref,
    hot_ref,
    atom_ref,
    first_ref,
    second_ref,
    back_ref,
    index_ref,
    place_kind_ref,
    total_ref,
    kind_ref,
    opening_ref,
    out_ref,
    feat_ref,
    gauss_ref,
    geo_ref,
    energy_ref,
    gin0_ref,
    gin1_ref,
    *scratch,
):
    scat, ahead_ref = (scratch[:GROUPS], scratch[GROUPS : 2 * GROUPS]), scratch[2 * GROUPS]
    first_core = where_ref[0:1] == 0
    own = jnp.where(first_core, home_ref[0, STATE], home_ref[1, STATE])
    minus2, minus1, plus2, plus3 = around(where_ref, far_ref, SENT)
    near0, near1 = home_ref[0, SENT], home_ref[1, SENT]

    def pick(a, b):
        return jnp.where(first_core, a, b)

    ghost = four_sets(
        pick(minus1, near0), pick(near1, plus2), pick(minus2, minus1), pick(plus2, plus3)
    )

    kind_rows = lax.broadcasted_iota(jnp.int32, (8, 2 * LANES), 0)
    centre_hot = (kind_rows == kind_ref[...]).astype(F32)
    slot_row = lax.broadcasted_iota(jnp.int32, (8, LANES), 0)
    tables = [
        [jnp.broadcast_to(t[r * 3 + c : r * 3 + c + 1], (8, LANES)) for c in range(3)]
        for t in (own, ghost)
        for r in range(2)
    ]

    def geometry(s, sums):
        sums = list(sums)
        slots = pl.ds(pl.multiple_of(s * 8, 8), 8)
        radials = [[], []]
        for h in range(2):
            cols = slice(h * LANES, (h + 1) * LANES)
            index = index_ref[0, slots, cols]
            lane = index & (LANES - 1)
            chunk = index // LANES
            dist_sq = None
            for comp in range(3):
                found = take_lanes(tables[0][comp], lane)
                for which in range(1, 4):
                    found = jnp.where(chunk == which, take_lanes(tables[which][comp], lane), found)
                vec = found - tables[h][comp]
                geo_ref[comp, s, :, cols] = vec
                dist_sq = vec * vec if comp == 0 else dist_sq + vec * vec
            live = slot_row + s * 8 < total_ref[:, cols]
            inside = 1.0 - dist_sq * (1.0 / CUT_SQ)
            used = live & (inside > 0.0)
            cutoff = jnp.where(used, inside * inside, 0.0)
            geo_ref[3, s, :, cols] = dist_sq
            geo_ref[4, s, :, cols] = cutoff
            geo_ref[5, s, :, cols] = jnp.where(used, inside * (-2.0 / CUT_SQ), 0.0)
            for c in range(N_BASIS):
                gap = dist_sq - CENTRES[c]
                gauss = jnp.exp(-SHARP * (gap * gap))
                gauss_ref[s, c * 8 : c * 8 + 8, cols] = gauss
                radial = gauss * cutoff
                radials[h].append(radial)
                sums[h * N_BASIS + c] = sums[h * N_BASIS + c] + radial
        place_kind = place_kind_ref[0, slots, :]
        rows = [jnp.concatenate([a, b], axis=1) for a, b in zip(*radials)]
        feat_ref[s, 0:64] = jnp.concatenate(rows, axis=0).astype(BF16)
        rows = [(place_kind == k).astype(F32) for k in range(N_KIND)]
        feat_ref[s, 80:128] = jnp.concatenate(rows, axis=0).astype(BF16)
        return tuple(sums)

    nothing = jnp.zeros((8, LANES), F32)
    sums = lax.fori_loop(0, GROUPS, geometry, (nothing,) * (2 * N_BASIS))
    rows = [jnp.sum(value, axis=0, keepdims=True) for value in sums]
    environ = jnp.concatenate(
        [jnp.concatenate(rows[:N_BASIS], axis=0), jnp.concatenate(rows[N_BASIS:], axis=0)], axis=1
    )
    shared = jnp.concatenate([environ, centre_hot], axis=0).astype(BF16)
    for s in range(GROUPS):
        feat_ref[s, 64:80] = shared

    atom_w = jnp.concatenate([atom_ref[...], atom_ref[...]], axis=1)
    half = nn_dot(first_ref[...], environ.astype(BF16))
    th = jnp.tanh(half)
    hidden_one = (half + half * th).astype(BF16)
    slope_one = 0.5 * (1.0 + th + half * (1.0 - th * th))
    half = nn_dot(second_ref[...], hidden_one)
    th = jnp.tanh(half)
    g_second = (atom_w * (1.0 + th + half * (1.0 - th * th))).astype(BF16)
    g_hidden = tn_dot(back_ref[...], g_second)
    g_first = (g_hidden * slope_one).astype(BF16)
    g_env = nn_dot(opening_ref[...], g_first)

    flat = jnp.concatenate([flat_ref[...], flat_ref[...]], axis=1)
    slot = lax.broadcasted_iota(jnp.int32, (16, HIDDEN), 0)
    quarter = lax.broadcasted_iota(jnp.int32, (16, HIDDEN), 1) // (HIDDEN // 4)
    members = [(slot == quarter + 4 * k).astype(F32).astype(BF16) for k in range(2)]

    def first_forward(s):
        ahead_ref[...] = nn_dot(up_ref[: AHEAD * HIDDEN, :], feat_ref[s])

    def group(s, g_env):
        feat = feat_ref[s]
        line = nn_dot(line_ref[...], feat)
        energy = line[0:8] + line[8:16]
        folded = []
        edge_w = sum_ref[...].astype(BF16)
        edge_w = jnp.concatenate([edge_w, edge_w], axis=1)

        def forward(k):
            many = nn_dot(up_ref[k * AHEAD * HIDDEN : (k + 1) * AHEAD * HIDDEN, :], feat)
            return [many[i * HIDDEN : (i + 1) * HIDDEN].astype(BF16) for i in range(AHEAD)]

        ahead = [ahead_ref[i * HIDDEN : (i + 1) * HIDDEN].astype(BF16) for i in range(AHEAD)]
        ahead += forward(1)
        for j in range(8):
            half = ahead.pop(0)
            if j == AHEAD:
                first_forward(jnp.minimum(s + 1, GROUPS - 1))
            th = jnp.tanh(half)
            rest = edge_w * (half * th)
            rest = rest[: HIDDEN // 2] + rest[HIDDEN // 2 :]
            folded.append(rest[: HIDDEN // 4] + rest[HIDDEN // 4 :])
            slope = th + half * (jnp.asarray(1.0, BF16) - th * th)
            g_in = nn_dot(down_ref[...], slope)
            cut = geo_ref[4, s, j : j + 1, :]
            g_in = (g_in[0:16] + g_in[16:32] + flat) * cut
            rows = pl.ds(s * 64 + j, 8, stride=8)
            gin0_ref[rows, :] = g_in[0:8, :LANES]
            gin1_ref[rows, :] = g_in[0:8, LANES:]
            g_env = g_env + g_in[8:16]
        for k in range(2):
            rest = jnp.concatenate(folded[k * 4 : k * 4 + 4], axis=0)
            energy = energy + nn_dot(members[k], rest)[0:8]
        energy_ref[s] = energy
        return g_env

    first_forward(0)
    g_env = lax.fori_loop(1, GROUPS, group, group(0, g_env))

    def backward(s, sums):
        sums = list(sums)
        slots = slice(s * 8, s * 8 + 8)
        for h in range(2):
            cols = slice(h * LANES, (h + 1) * LANES)
            dist_sq, cutoff, slope = (geo_ref[k, s, :, cols] for k in (3, 4, 5))
            g_cut = energy_ref[s, :, cols]
            g_gap = None
            gin = (gin0_ref, gin1_ref)[h]
            for c in range(N_BASIS):
                rows = slice(s * 64 + c * 8, s * 64 + c * 8 + 8)
                g_radial = gin[rows, :] + g_env[c : c + 1, cols]
                q = g_radial * gauss_ref[s, c * 8 : c * 8 + 8, cols]
                g_cut = g_cut + q
                moment = q * (dist_sq - CENTRES[c])
                g_gap = moment if g_gap is None else g_gap + moment
            g_dist = (-4.0 * SHARP) * (cutoff * g_gap) + 2.0 * (g_cut * slope)
            chunk = index_ref[0, slots, cols] // LANES
            target = scat[h][s]
            for comp in range(3):
                g_vec = g_dist * geo_ref[comp, s, :, cols]
                sums[h * 3 + comp] = sums[h * 3 + comp] + g_vec
                for part, value in enumerate(split_parts(g_vec, 2)):
                    for which in range(4):
                        row = part * 12 + which * 3 + comp
                        target[pl.ds(row, 8, stride=24), :] = jnp.where(chunk == which, value, 0.0)
        return tuple(sums)

    def scatter(s):
        lhs = []
        for j in range(8):
            rows = slice(j * 24, j * 24 + 24)
            lhs.append(jnp.concatenate([half[s][rows, :] for half in scat], axis=1).astype(BF16))
        return nt_dot(jnp.concatenate(lhs, axis=1), hot_ref[:, s * 16 * LANES : (s + 1) * 16 * LANES])

    sums, total = (nothing,) * 6, None
    for s in range(GROUPS):
        sums = backward(s, sums)
        part = scatter(s)
        total = part if total is None else total + part
    total = total[0:12] + total[12:24]
    centre = jnp.concatenate([jnp.sum(value, axis=0, keepdims=True) for value in sums], axis=0)
    pad = jnp.zeros((2, LANES), F32)
    out_ref[0:8] = jnp.concatenate([total[6:12], pad], axis=0)
    out_ref[8:16] = jnp.concatenate([total[0:6] - centre, pad], axis=0)


def returned_sum(returned, border0, border1):
    row = lax.broadcasted_iota(jnp.int32, (8, LANES), 0)
    place = lax.broadcasted_iota(jnp.int32, (LANES, LANES), 0)
    lhs, rhs = [], []
    for which, border in enumerate((border0, border1)):
        three = returned[which * 3 : which * 3 + 3]
        twice = jnp.concatenate([three, three, jnp.zeros((2, LANES), F32)], axis=0)
        meant = (border // LANES == 1) == (row >= 3)
        kept = jnp.where(meant, twice, 0.0)
        lhs.append(jnp.concatenate(split_parts(kept, 3), axis=0).astype(BF16))
        rhs.append((place == (border & (LANES - 1))).astype(F32).astype(BF16))
    total = nt_dot(jnp.concatenate(lhs, axis=1), jnp.concatenate(rhs, axis=1))
    return total[0:8] + total[8:16] + total[16:24]


def moved(state, own_grad, ghosts, domain):
    border0 = state[14:15].astype(jnp.int32)
    border1 = state[15:16].astype(jnp.int32)
    inverse = rows_of_two(state[6:7], state[7:8])
    returned = four_sets(*(ghosts[domain + offset] for offset in (1, -1, 2, -2)))
    grad = own_grad + returned_sum(returned, border0, border1)
    speed = state[8:16] - TIME_STEP * grad * inverse
    return state[0:8] + TIME_STEP * speed, speed, border0, border1


def step_kernel(where_ref, home_ref, far_ref, wide_ref, next_ref, around_ref):
    first_chip, even_pair = where_ref[5:6] == 0, where_ref[6:7] == 0
    blocks = (
        (wide_ref.at[1, 0], wide_ref.at[0, 0]),
        (wide_ref.at[0, 0], wide_ref.at[0, 1]),
        (wide_ref.at[0, 1], wide_ref.at[1, 1]),
    )

    def on_line(k, rows):
        even, odd = (block[k % 4 // 2, k % 2, rows] for block in blocks[k // 4])
        return jnp.where(even_pair, even, odd)

    def forces(domain, rows):
        return jnp.where(first_chip, on_line(domain + 4, rows), on_line(domain + 6, rows))

    states = dict(zip((-2, -1, 2, 3), around(where_ref, far_ref, STATE)))
    states[0], states[1] = home_ref[0, STATE], home_ref[1, STATE]
    ghosts = {domain: forces(domain, GHOSTS) for domain in range(-4, 6)}
    for domain, state in states.items():
        place, speed, border0, border1 = moved(state, forces(domain, OWN), ghosts, domain)
        sent = border_positions(place, border0, border1)
        if domain in (0, 1):
            next_ref[domain, SENT] = sent
            next_ref[domain, 8:14] = place[0:6]
            next_ref[domain, 14:16] = state[6:8]
            next_ref[domain, 16:22] = speed[0:6]
            next_ref[domain, 22:24] = state[14:16]
        else:
            around_ref[domain + 2 if domain < 0 else domain] = sent


def last_kernel(where_ref, home_ref, near_ref, far_ref, next_ref):
    ghosts = dict(zip((-2, -1, 2, 3), around(where_ref, far_ref, GHOSTS)))
    ghosts[0], ghosts[1] = near_ref[0, GHOSTS], near_ref[1, GHOSTS]
    for domain in range(2):
        place, speed, _, _ = moved(home_ref[domain, STATE], near_ref[domain, OWN], ghosts, domain)
        next_ref[domain, 0:6] = place[0:6]
        next_ref[domain, 6:8] = jnp.broadcast_to(where_ref[4:5], (2, LANES))
        next_ref[domain, 8:16] = speed


def swap_kernel(where_ref, own_ref, mate_ref, x_out, v_out, x_ref, v_ref, sems):
    core, swaps, side, position = (where_ref[k : k + 1] == 0 for k in range(4))

    def of_core(pair):
        return jnp.where(core, pair[0], pair[1])

    def of_side(s):
        return of_core(jnp.where(position, mate_ref[s, 0], mate_ref[s, 1]))

    mine = of_core(own_ref)
    chosen = jnp.where(swaps, mine, jnp.where(side, of_side(0), of_side(1)))
    scale = jnp.sqrt(mine[6:7] / chosen[6:7])
    put_flat(x_ref, chosen[0:6])
    put_flat(v_ref, chosen[8:14] * scale)
    bring((x_ref, v_ref), (x_out, v_out), sems)


def vmem():
    return pl.BlockSpec(memory_space=pltpu.VMEM)


def smem():
    return pl.BlockSpec(memory_space=pltpu.SMEM)


def tiles(*shape):
    return jax.ShapeDtypeStruct(shape + (LANES,), F32)


def call(kernel, scalars, arrays, out_shape, scratch=(), flops=10**6, inputs=None, outputs=None,
         limit=24 * 2**20):
    outputs = outputs or vmem
    out_specs = [outputs() for _ in out_shape] if isinstance(out_shape, list) else outputs()
    return pl.pallas_call(
        kernel,
        out_shape=out_shape,
        in_specs=[smem()] * len(scalars) + [(inputs or vmem)()] * len(arrays),
        out_specs=out_specs,
        scratch_shapes=list(scratch),
        cost_estimate=pl.CostEstimate(flops=flops, bytes_accessed=10**6, transcendentals=0),
        compiler_params=pltpu.CompilerParams(vmem_limit_bytes=limit),
    )(*scalars, *arrays)


def anywhere():
    return pl.BlockSpec(memory_space=pltpu.HBM)


def landing(arrays):
    return [pltpu.VMEM(a.shape, a.dtype) for a in arrays] + [pltpu.SemaphoreType.DMA((len(arrays),))]


def weight_shapes():
    return [
        jax.ShapeDtypeStruct((8 * HIDDEN, LANES), BF16),
        jax.ShapeDtypeStruct((32, HIDDEN), BF16),
        jax.ShapeDtypeStruct((16, LANES), BF16),
        tiles(16),
        tiles(HIDDEN),
        jax.ShapeDtypeStruct((LANES, SLOTS * 2 * LANES), BF16),
        tiles(HIDDEN),
        jax.ShapeDtypeStruct((HIDDEN, N_BASIS), BF16),
        jax.ShapeDtypeStruct((HIDDEN, HIDDEN), BF16),
        jax.ShapeDtypeStruct((HIDDEN, HIDDEN), BF16),
    ]


def begin_shapes(arrays):
    through = [jax.ShapeDtypeStruct(arrays[k].shape, arrays[k].dtype) for k in (5, 6, 7, 2, 10)]
    space = landing([arrays[k] for k in (0, 1, 3, 4, 8, 9, 11, 12)])
    space[3] = pltpu.SMEM(arrays[4].shape, F32)
    space[-1] = pltpu.SemaphoreType.DMA((len(arrays),))
    made = [tiles(24)] + weight_shapes() + through
    return made, space


def force_scratch():
    return [
        pltpu.VMEM((GROUPS, 128, 2 * LANES), BF16),
        pltpu.VMEM((GROUPS, 64, 2 * LANES), F32),
        pltpu.VMEM((6, GROUPS, 8, 2 * LANES), F32),
        pltpu.VMEM((GROUPS, 8, 2 * LANES), F32),
        pltpu.VMEM((GROUPS * 64, LANES), F32),
        pltpu.VMEM((GROUPS * 64, LANES), F32),
    ] + [pltpu.VMEM((8 * 24, LANES), F32)] * (2 * GROUPS) + [pltpu.VMEM((AHEAD * HIDDEN, 2 * LANES), F32)]


def on_chip(value, domains):
    groups = [[2 * i, 2 * i + 1] for i in range(domains // 2)]
    return lax.all_gather(value, "space", axis_index_groups=groups)


def across_chips(value, domains):
    groups = []
    for i in range(domains // 4):
        groups += [[4 * i, 4 * i + 2], [4 * i + 3, (4 * i + 5) % domains]]
    return lax.all_gather(value, "space", axis_index_groups=groups)


def in_pair(value, domains):
    groups = [[4 * i + k for k in range(4)] for i in range(domains // 4)]
    whole = lax.all_gather(value, "space", axis_index_groups=groups)
    return whole.reshape((2, 2) + value.shape)


def between_pairs(value, domains):
    groups = []
    for i in range(0, domains // 4, 2):
        for chip in range(2):
            first = 4 * i + 2 * chip
            groups += [[first, first + 4], [first + 5, (first + 9) % domains]]
    return lax.all_gather(value, "space", axis_index_groups=groups)


def even_odd_core(rank, rungs):
    far = (rank % 4 == 0) | (rank % 4 == 3)
    return 1 - (far & (rank > 0) & (rank < rungs - 1))


def along_ladder(value, rungs, domains):
    groups = []
    for chip in range(0, domains, 2):
        for low in range(rungs - 1):
            pair = []
            for rank in (low, low + 1):
                core = even_odd_core(rank, rungs)
                pair.append(rank * domains + chip + (core if low % 2 == 0 else 1 - core))
            groups.append(pair)
        if chip % 4 == 0:
            for end in (0, rungs - 1):
                groups.append([end * domains + chip, end * domains + chip + 2])
    return lax.all_gather(value, ("replica", "space"), axis_index_groups=groups)


def on_device(
    particle_coordinates,
    particle_motions,
    particle_kinds,
    filled_totals,
    adjacent_particles,
    adjacent_place_kinds,
    border_particle_numbers,
    reciprocal_kind_inertia,
    thermal_levels,
    swap_mates,
    bond_intake_coefficients,
    bond_output_coefficients,
    particle_opening_coefficients,
    particle_middle_coefficients,
    particle_output_coefficients,
):
    domains, rungs = lax.axis_size("space"), lax.axis_size("replica")
    core = lax.axis_index("space") % 2
    rank = lax.axis_index("replica")
    mate = swap_mates[0]
    odd = rank % 2
    even_odd = (mate > rank) == (odd == 0)
    side = even_odd_core(rank, rungs)
    side = jnp.where(even_odd, side, 1 - side)
    position = jnp.where(even_odd, 1 - odd, odd)
    where_to = [value.astype(F32) for value in (core, mate != rank, side, position)]
    here = lax.axis_index("space")
    chip, pair = (here // 2 % 2).astype(F32), (here // 4 % 2).astype(F32)
    where_to = jnp.stack(where_to + [thermal_levels[0], chip, pair])
    where_to = jnp.broadcast_to(where_to[:, None], (7, LANES))

    arrays = (
        particle_coordinates.reshape(1, -1),
        particle_motions.reshape(1, -1),
        particle_kinds,
        border_particle_numbers,
        reciprocal_kind_inertia,
        adjacent_particles,
        adjacent_place_kinds,
        filled_totals,
        bond_intake_coefficients.T,
        bond_output_coefficients[None],
        particle_opening_coefficients.T,
        particle_middle_coefficients,
        particle_output_coefficients[None],
    )
    arrays = tuple(pltpu.with_memory_space_constraint(a, pltpu.HBM) for a in arrays)
    made, space = begin_shapes(arrays)
    begin, *fixed = call(begin_kernel, (), arrays, made, space, inputs=anywhere)
    home = on_chip(begin, domains)
    far = on_chip(across_chips(home, domains), domains)
    for step in range(STEPS):
        partial = call(force_kernel, (), (where_to, home, far, *fixed), tiles(16), force_scratch())
        if step < STEPS - 1:
            pair = in_pair(partial, domains)
            wide = on_chip(between_pairs(pair, domains), domains)
            shapes = [tiles(2, 24), tiles(4, 8)]
            home, far = call(step_kernel, (), (where_to, home, far, wide), shapes)
        else:
            near = on_chip(partial, domains)
            far = on_chip(across_chips(near[:, GHOSTS], domains), domains)
            state = call(last_kernel, (), (where_to, home, near, far), tiles(2, 16))
    mates = on_chip(along_ladder(state, rungs, domains), domains)
    shape = particle_coordinates.shape
    out = jax.ShapeDtypeStruct((1, particle_coordinates.size), F32)
    scratch = landing((out, out))
    new_x, new_v = call(
        swap_kernel, (), (where_to, state, mates), [out, out], scratch, outputs=anywhere
    )
    return new_x.reshape(shape), new_v.reshape(shape)


def solution(mesh):
    return jax.shard_map(
        on_device,
        mesh=mesh,
        in_specs=(
            P("replica", None, "space"),
            P("replica", None, "space"),
            P("replica", "space"),
            P("replica", "space"),
            P("replica", None, "space"),
            P("replica", None, "space"),
            P("replica", None, "space"),
            P(),
            P("replica"),
            P("replica"),
            P(),
            P(),
            P(),
            P(),
            P(),
        ),
        out_specs=(P("replica", None, "space"), P("replica", None, "space")),
        check_vma=False,
    )
```

```python
import functools

import jax
import jax.numpy as jnp
from jax import lax
from jax.experimental import pallas as pl
from jax.experimental.pallas import tpu as pltpu
from jax.sharding import PartitionSpec as P

STEPS = 2
TIME_STEP = 0.05
CUT_SQ = 9.0
N_BASIS = 8
N_KIND = 6
LANES = 128
SLOTS = 32
GROUPS = SLOTS // 8
HIDDEN = 256
AHEAD = 4
SENT, STATE = slice(0, 8), slice(8, 24)
GHOSTS, OWN = slice(0, 8), slice(8, 16)
SHARP = (N_BASIS / CUT_SQ) ** 2
CENTRES = [CUT_SQ * c / (N_BASIS - 1) for c in range(N_BASIS)]
F32 = jnp.float32
BF16 = jnp.bfloat16


def nt_dot(a, b):
    return lax.dot_general(a, b, (((1,), (1,)), ((), ())), preferred_element_type=F32)


def tn_dot(a, b):
    return lax.dot_general(a, b, (((0,), (0,)), ((), ())), preferred_element_type=F32)


def nn_dot(a, b):
    return lax.dot_general(a, b, (((1,), (0,)), ((), ())), preferred_element_type=F32)


def tile_of(flat_ref):
    rows = [
        flat_ref[:, (comp * 2 + chunk) * LANES : (comp * 2 + chunk + 1) * LANES]
        for chunk in range(2)
        for comp in range(3)
    ]
    return jnp.concatenate(rows, axis=0)


def put_flat(flat_ref, tile):
    for chunk in range(2):
        for comp in range(3):
            start = (comp * 2 + chunk) * LANES
            row = chunk * 3 + comp
            flat_ref[:, start : start + LANES] = tile[row : row + 1]


def rows_of_two(first, second, pad_with=None):
    shape = (3, LANES)
    pad = jnp.zeros((2, LANES), first.dtype)
    return jnp.concatenate(
        [jnp.broadcast_to(first, shape), jnp.broadcast_to(second, shape), pad], axis=0
    )


def take_lanes(table, lane):
    return jnp.take_along_axis(table, lane, axis=1, mode="promise_in_bounds")


def border_positions(tile, border0, border1):
    index = rows_of_two(border0, border1)
    pad = jnp.zeros((2, LANES), F32)
    low = jnp.concatenate([tile[0:3], tile[0:3], pad], axis=0)
    high = jnp.concatenate([tile[3:6], tile[3:6], pad], axis=0)
    lane = index & (LANES - 1)
    return jnp.where(index < LANES, take_lanes(low, lane), take_lanes(high, lane))


def four_sets(set0, set1, set2, set3):
    row = lax.broadcasted_iota(jnp.int32, (8, LANES), 0)
    col = lax.broadcasted_iota(jnp.int32, (8, LANES), 1)
    left = col < LANES // 2
    return jnp.where(row < 3, jnp.where(left, set0, set1), jnp.where(left, set2, set3))


def split_parts(value, count):
    parts = []
    for _ in range(count):
        part = value.astype(BF16).astype(F32)
        parts.append(part)
        value = value - part
    return parts


def fed_columns():
    feature = lax.broadcasted_iota(jnp.int32, (28, LANES), 0)
    col = lax.broadcasted_iota(jnp.int32, (28, LANES), 1)
    block, which = col // 8, col % 8
    radial = (block < 8) & (feature == block)
    environ = (block == 8) & (feature == 8 + which)
    centre = (block == 9) & (which < N_KIND) & (feature == 16 + which)
    neigh = (block >= 10) & (feature == 22 + block - 10)
    return (radial | environ | centre | neigh).astype(F32)


def own_columns(slot, rows):
    col = lax.broadcasted_iota(jnp.int32, (rows, LANES), 1)
    return ((col // 8 == 8) | (col // 8 == 9) | (col % 8 == slot)).astype(F32)


def two_parts(value):
    high, low = split_parts(value, 2)
    return jnp.concatenate([high, low], axis=0).astype(BF16)


def begin_kernel(*refs):
    inputs, refs = refs[:13], refs[13:]
    (out_ref, up_ref, down_ref, line_ref, flat_ref, sum_ref, hot_ref, atom_ref, first_ref,
     second_ref, back_ref, index_ref, place_ref, total_ref, kind_ref, opening_ref), refs = (
        refs[:16], refs[16:]
    )
    x_ref, v_ref, border_ref, inertia_ref, intake_ref, edge_out_ref, middle_ref, atom_out_ref = (
        refs[:8]
    )
    landed = (
        x_ref, v_ref, kind_ref, border_ref, inertia_ref, index_ref, place_ref, total_ref,
        intake_ref, edge_out_ref, opening_ref, middle_ref, atom_out_ref,
    )
    copies = [
        pltpu.make_async_copy(source, target, refs[8].at[k])
        for k, (source, target) in enumerate(zip(inputs, landed))
    ]
    indices = copies.pop(5)
    indices.start()
    for copy in copies:
        copy.start()
    indices.wait()
    place = lax.broadcasted_iota(jnp.int32, (LANES, 2 * LANES), 0).astype(F32).astype(BF16)
    one, none = jnp.asarray(1.0, BF16), jnp.asarray(0.0, BF16)

    def group(s, carry):
        for j in range(8):
            lane = (index_ref[0, pl.ds(s * 8 + j, 1), :] & (LANES - 1)).astype(F32)
            lane = jnp.broadcast_to(lane, (16, 2 * LANES)).astype(BF16)
            lane = jnp.concatenate([lane] * (LANES // 16), axis=0)
            cols = pl.ds(pl.multiple_of((s * 8 + j) * 2 * LANES, 2 * LANES), 2 * LANES)
            hot_ref[:, cols] = jnp.where(place == lane, one, none)
        return carry

    lax.fori_loop(0, GROUPS, group, 0)
    for copy in copies:
        copy.wait()

    x_tile = tile_of(x_ref)
    border = border_ref[0]
    border0 = jnp.concatenate([border[0:1], border[1:2]], axis=1)
    border1 = jnp.concatenate([border[2:3], border[3:4]], axis=1)
    kind = kind_ref[...]
    inverse = jnp.zeros(kind.shape, F32)
    for k in range(N_KIND):
        inverse = jnp.where(kind == k, inertia_ref[k], inverse)
    out_ref[0:8] = border_positions(x_tile, border0, border1)
    out_ref[8:14] = x_tile
    out_ref[14:15] = inverse[:, :LANES]
    out_ref[15:16] = inverse[:, LANES:]
    out_ref[16:22] = tile_of(v_ref)
    out_ref[22:23] = border0.astype(F32)
    out_ref[23:24] = border1.astype(F32)

    intake = intake_ref[...]
    fed = fed_columns()
    for j in range(8):
        up = (0.5 * fed * own_columns(j, 1)).astype(BF16)
        up_ref[j * HIDDEN : (j + 1) * HIDDEN, :] = tn_dot(intake, up).astype(BF16)
    edge_w = edge_out_ref[...]
    weighted = intake.astype(F32) * (0.5 * edge_w)
    down_ref[...] = two_parts(weighted[0:16])
    line = jnp.sum(weighted, axis=1, keepdims=True)
    flat_ref[...] = jnp.broadcast_to(line[0:16], (16, LANES))
    line = jnp.sum(fed * line, axis=0, keepdims=True)
    slot = lax.broadcasted_iota(jnp.int32, (8, LANES), 0)
    line_ref[...] = two_parts(own_columns(slot, 8) * line)
    sum_ref[...] = jnp.transpose(jnp.broadcast_to(edge_w, (LANES, HIDDEN)))
    atom_ref[...] = jnp.transpose(jnp.broadcast_to(0.5 * atom_out_ref[...], (LANES, HIDDEN)))
    first_ref[...] = jnp.transpose((0.5 * opening_ref[...]).astype(F32)).astype(BF16)
    second_ref[...] = 0.5 * middle_ref[...]
    back_ref[...] = middle_ref[...]


def around(where_ref, far_ref, rows):
    if len(far_ref.shape) == 3:
        return [far_ref[k, rows] for k in range(4)]
    first_chip = where_ref[5:6] == 0
    before = [jnp.where(first_chip, far_ref[1, 0, k, rows], far_ref[0, 0, k, rows]) for k in range(2)]
    after = [jnp.where(first_chip, far_ref[0, 1, k, rows], far_ref[1, 1, k, rows]) for k in range(2)]
    return before + after


def force_kernel(
    where_ref,
    home_ref,
    far_ref,
    up_ref,
    down_ref,
    line_ref,
    flat_ref,
    sum_ref,
    hot_ref,
    atom_ref,
    first_ref,
    second_ref,
    back_ref,
    index_ref,
    place_kind_ref,
    total_ref,
    kind_ref,
    opening_ref,
    out_ref,
    feat_ref,
    gauss_ref,
    geo_ref,
    energy_ref,
    gin0_ref,
    gin1_ref,
    *scratch,
):
    scat, ahead_ref = (scratch[:GROUPS], scratch[GROUPS : 2 * GROUPS]), scratch[2 * GROUPS]
    first_core = where_ref[0:1] == 0
    own = jnp.where(first_core, home_ref[0, STATE], home_ref[1, STATE])
    minus2, minus1, plus2, plus3 = around(where_ref, far_ref, SENT)
    near0, near1 = home_ref[0, SENT], home_ref[1, SENT]

    def pick(a, b):
        return jnp.where(first_core, a, b)

    ghost = four_sets(
        pick(minus1, near0), pick(near1, plus2), pick(minus2, minus1), pick(plus2, plus3)
    )

    kind_rows = lax.broadcasted_iota(jnp.int32, (8, 2 * LANES), 0)
    centre_hot = (kind_rows == kind_ref[...]).astype(F32)
    slot_row = lax.broadcasted_iota(jnp.int32, (8, LANES), 0)
    tables = [
        [jnp.broadcast_to(t[r * 3 + c : r * 3 + c + 1], (8, LANES)) for c in range(3)]
        for t in (own, ghost)
        for r in range(2)
    ]

    def geometry(s, sums):
        sums = list(sums)
        slots = pl.ds(pl.multiple_of(s * 8, 8), 8)
        radials = [[], []]
        for h in range(2):
            cols = slice(h * LANES, (h + 1) * LANES)
            index = index_ref[0, slots, cols]
            lane = index & (LANES - 1)
            chunk = index // LANES
            dist_sq = None
            for comp in range(3):
                found = take_lanes(tables[0][comp], lane)
                for which in range(1, 4):
                    found = jnp.where(chunk == which, take_lanes(tables[which][comp], lane), found)
                vec = found - tables[h][comp]
                geo_ref[comp, s, :, cols] = vec
                dist_sq = vec * vec if comp == 0 else dist_sq + vec * vec
            live = slot_row + s * 8 < total_ref[:, cols]
            inside = 1.0 - dist_sq * (1.0 / CUT_SQ)
            used = live & (inside > 0.0)
            cutoff = jnp.where(used, inside * inside, 0.0)
            geo_ref[3, s, :, cols] = dist_sq
            geo_ref[4, s, :, cols] = cutoff
            geo_ref[5, s, :, cols] = jnp.where(used, inside * (-2.0 / CUT_SQ), 0.0)
            for c in range(N_BASIS):
                gap = dist_sq - CENTRES[c]
                gauss = jnp.exp(-SHARP * (gap * gap))
                gauss_ref[s, c * 8 : c * 8 + 8, cols] = gauss
                radial = gauss * cutoff
                radials[h].append(radial)
                sums[h * N_BASIS + c] = sums[h * N_BASIS + c] + radial
        place_kind = place_kind_ref[0, slots, :]
        rows = [jnp.concatenate([a, b], axis=1) for a, b in zip(*radials)]
        feat_ref[s, 0:64] = jnp.concatenate(rows, axis=0).astype(BF16)
        rows = [(place_kind == k).astype(F32) for k in range(N_KIND)]
        feat_ref[s, 80:128] = jnp.concatenate(rows, axis=0).astype(BF16)
        return tuple(sums)

    nothing = jnp.zeros((8, LANES), F32)
    sums = lax.fori_loop(0, GROUPS, geometry, (nothing,) * (2 * N_BASIS))
    rows = [jnp.sum(value, axis=0, keepdims=True) for value in sums]
    environ = jnp.concatenate(
        [jnp.concatenate(rows[:N_BASIS], axis=0), jnp.concatenate(rows[N_BASIS:], axis=0)], axis=1
    )
    shared = jnp.concatenate([environ, centre_hot], axis=0).astype(BF16)
    for s in range(GROUPS):
        feat_ref[s, 64:80] = shared

    atom_w = jnp.concatenate([atom_ref[...], atom_ref[...]], axis=1)
    half = nn_dot(first_ref[...], environ.astype(BF16))
    th = jnp.tanh(half)
    hidden_one = (half + half * th).astype(BF16)
    slope_one = 0.5 * (1.0 + th + half * (1.0 - th * th))
    half = nn_dot(second_ref[...], hidden_one)
    th = jnp.tanh(half)
    g_second = (atom_w * (1.0 + th + half * (1.0 - th * th))).astype(BF16)
    g_hidden = tn_dot(back_ref[...], g_second)
    g_first = (g_hidden * slope_one).astype(BF16)
    g_env = nn_dot(opening_ref[...], g_first)

    flat = jnp.concatenate([flat_ref[...], flat_ref[...]], axis=1)
    slot = lax.broadcasted_iota(jnp.int32, (16, HIDDEN), 0)
    quarter = lax.broadcasted_iota(jnp.int32, (16, HIDDEN), 1) // (HIDDEN // 4)
    members = [(slot == quarter + 4 * k).astype(F32).astype(BF16) for k in range(2)]

    def first_forward(s):
        ahead_ref[...] = nn_dot(up_ref[: AHEAD * HIDDEN, :], feat_ref[s])

    def group(s, g_env):
        feat = feat_ref[s]
        line = nn_dot(line_ref[...], feat)
        energy = line[0:8] + line[8:16]
        folded = []
        edge_w = sum_ref[...].astype(BF16)
        edge_w = jnp.concatenate([edge_w, edge_w], axis=1)

        def forward(k):
            many = nn_dot(up_ref[k * AHEAD * HIDDEN : (k + 1) * AHEAD * HIDDEN, :], feat)
            return [many[i * HIDDEN : (i + 1) * HIDDEN].astype(BF16) for i in range(AHEAD)]

        ahead = [ahead_ref[i * HIDDEN : (i + 1) * HIDDEN].astype(BF16) for i in range(AHEAD)]
        ahead += forward(1)
        for j in range(8):
            half = ahead.pop(0)
            if j == AHEAD:
                first_forward(jnp.minimum(s + 1, GROUPS - 1))
            th = jnp.tanh(half)
            rest = edge_w * (half * th)
            rest = rest[: HIDDEN // 2] + rest[HIDDEN // 2 :]
            folded.append(rest[: HIDDEN // 4] + rest[HIDDEN // 4 :])
            slope = th + half * (jnp.asarray(1.0, BF16) - th * th)
            g_in = nn_dot(down_ref[...], slope)
            cut = geo_ref[4, s, j : j + 1, :]
            g_in = (g_in[0:16] + g_in[16:32] + flat) * cut
            rows = pl.ds(s * 64 + j, 8, stride=8)
            gin0_ref[rows, :] = g_in[0:8, :LANES]
            gin1_ref[rows, :] = g_in[0:8, LANES:]
            g_env = g_env + g_in[8:16]
        for k in range(2):
            rest = jnp.concatenate(folded[k * 4 : k * 4 + 4], axis=0)
            energy = energy + nn_dot(members[k], rest)[0:8]
        energy_ref[s] = energy
        return g_env

    first_forward(0)
    g_env = lax.fori_loop(1, GROUPS, group, group(0, g_env))

    def backward(s, sums):
        sums = list(sums)
        slots = slice(s * 8, s * 8 + 8)
        for h in range(2):
            cols = slice(h * LANES, (h + 1) * LANES)
            dist_sq, cutoff, slope = (geo_ref[k, s, :, cols] for k in (3, 4, 5))
            g_cut = energy_ref[s, :, cols]
            g_gap = None
            gin = (gin0_ref, gin1_ref)[h]
            for c in range(N_BASIS):
                rows = slice(s * 64 + c * 8, s * 64 + c * 8 + 8)
                g_radial = gin[rows, :] + g_env[c : c + 1, cols]
                q = g_radial * gauss_ref[s, c * 8 : c * 8 + 8, cols]
                g_cut = g_cut + q
                moment = q * (dist_sq - CENTRES[c])
                g_gap = moment if g_gap is None else g_gap + moment
            g_dist = (-4.0 * SHARP) * (cutoff * g_gap) + 2.0 * (g_cut * slope)
            chunk = index_ref[0, slots, cols] // LANES
            target = scat[h][s]
            for comp in range(3):
                g_vec = g_dist * geo_ref[comp, s, :, cols]
                sums[h * 3 + comp] = sums[h * 3 + comp] + g_vec
                for part, value in enumerate(split_parts(g_vec, 2)):
                    for which in range(4):
                        row = part * 12 + which * 3 + comp
                        target[pl.ds(row, 8, stride=24), :] = jnp.where(chunk == which, value, 0.0)
        return tuple(sums)

    def scatter(s):
        lhs = []
        for j in range(8):
            rows = slice(j * 24, j * 24 + 24)
            lhs.append(jnp.concatenate([half[s][rows, :] for half in scat], axis=1).astype(BF16))
        return nt_dot(jnp.concatenate(lhs, axis=1), hot_ref[:, s * 16 * LANES : (s + 1) * 16 * LANES])

    sums, total = (nothing,) * 6, None
    for s in range(GROUPS):
        sums = backward(s, sums)
        part = scatter(s)
        total = part if total is None else total + part
    total = total[0:12] + total[12:24]
    centre = jnp.concatenate([jnp.sum(value, axis=0, keepdims=True) for value in sums], axis=0)
    pad = jnp.zeros((2, LANES), F32)
    out_ref[0:8] = jnp.concatenate([total[6:12], pad], axis=0)
    out_ref[8:16] = jnp.concatenate([total[0:6] - centre, pad], axis=0)


def returned_sum(returned, border0, border1):
    row = lax.broadcasted_iota(jnp.int32, (8, LANES), 0)
    place = lax.broadcasted_iota(jnp.int32, (LANES, LANES), 0)
    lhs, rhs = [], []
    for which, border in enumerate((border0, border1)):
        three = returned[which * 3 : which * 3 + 3]
        twice = jnp.concatenate([three, three, jnp.zeros((2, LANES), F32)], axis=0)
        meant = (border // LANES == 1) == (row >= 3)
        kept = jnp.where(meant, twice, 0.0)
        lhs.append(jnp.concatenate(split_parts(kept, 3), axis=0).astype(BF16))
        rhs.append((place == (border & (LANES - 1))).astype(F32).astype(BF16))
    total = nt_dot(jnp.concatenate(lhs, axis=1), jnp.concatenate(rhs, axis=1))
    return total[0:8] + total[8:16] + total[16:24]


def moved(state, own_grad, ghosts, domain):
    border0 = state[14:15].astype(jnp.int32)
    border1 = state[15:16].astype(jnp.int32)
    inverse = rows_of_two(state[6:7], state[7:8])
    returned = four_sets(*(ghosts[domain + offset] for offset in (1, -1, 2, -2)))
    grad = own_grad + returned_sum(returned, border0, border1)
    speed = state[8:16] - TIME_STEP * grad * inverse
    return state[0:8] + TIME_STEP * speed, speed, border0, border1


def step_kernel(where_ref, home_ref, far_ref, wide_ref, next_ref, around_ref):
    first_chip, even_pair = where_ref[5:6] == 0, where_ref[6:7] == 0
    blocks = (
        (wide_ref.at[1, 0], wide_ref.at[0, 0]),
        (wide_ref.at[0, 0], wide_ref.at[0, 1]),
        (wide_ref.at[0, 1], wide_ref.at[1, 1]),
    )

    def on_line(k, rows):
        even, odd = (block[k % 4 // 2, k % 2, rows] for block in blocks[k // 4])
        return jnp.where(even_pair, even, odd)

    def forces(domain, rows):
        return jnp.where(first_chip, on_line(domain + 4, rows), on_line(domain + 6, rows))

    states = dict(zip((-2, -1, 2, 3), around(where_ref, far_ref, STATE)))
    states[0], states[1] = home_ref[0, STATE], home_ref[1, STATE]
    ghosts = {domain: forces(domain, GHOSTS) for domain in range(-4, 6)}
    for domain, state in states.items():
        place, speed, border0, border1 = moved(state, forces(domain, OWN), ghosts, domain)
        sent = border_positions(place, border0, border1)
        if domain in (0, 1):
            next_ref[domain, SENT] = sent
            next_ref[domain, 8:14] = place[0:6]
            next_ref[domain, 14:16] = state[6:8]
            next_ref[domain, 16:22] = speed[0:6]
            next_ref[domain, 22:24] = state[14:16]
        else:
            around_ref[domain + 2 if domain < 0 else domain] = sent


def last_kernel(where_ref, home_ref, near_ref, far_ref, next_ref):
    ghosts = dict(zip((-2, -1, 2, 3), around(where_ref, far_ref, GHOSTS)))
    ghosts[0], ghosts[1] = near_ref[0, GHOSTS], near_ref[1, GHOSTS]
    for domain in range(2):
        place, speed, _, _ = moved(home_ref[domain, STATE], near_ref[domain, OWN], ghosts, domain)
        next_ref[domain, 0:6] = place[0:6]
        next_ref[domain, 6:8] = jnp.broadcast_to(where_ref[4:5], (2, LANES))
        next_ref[domain, 8:16] = speed


def swap_kernel(where_ref, own_ref, mate_ref, x_out, v_out, x_ref, v_ref, sems):
    core, swaps, side, position = (where_ref[k : k + 1] == 0 for k in range(4))

    def of_core(pair):
        return jnp.where(core, pair[0], pair[1])

    def of_side(s):
        return of_core(jnp.where(position, mate_ref[s, 0], mate_ref[s, 1]))

    mine = of_core(own_ref)
    chosen = jnp.where(swaps, mine, jnp.where(side, of_side(0), of_side(1)))
    put_flat(x_ref, chosen[0:6])
    x_copy = pltpu.make_async_copy(x_ref, x_out, sems.at[0])
    x_copy.start()
    scale = jnp.sqrt(mine[6:7] / chosen[6:7])
    put_flat(v_ref, chosen[8:14] * scale)
    v_copy = pltpu.make_async_copy(v_ref, v_out, sems.at[1])
    v_copy.start()
    x_copy.wait()
    v_copy.wait()


def vmem():
    return pl.BlockSpec(memory_space=pltpu.VMEM)


def smem():
    return pl.BlockSpec(memory_space=pltpu.SMEM)


def tiles(*shape):
    return jax.ShapeDtypeStruct(shape + (LANES,), F32)


def call(kernel, scalars, arrays, out_shape, scratch=(), flops=10**6, inputs=None, outputs=None,
         limit=24 * 2**20):
    outputs = outputs or vmem
    out_specs = [outputs() for _ in out_shape] if isinstance(out_shape, list) else outputs()
    return pl.pallas_call(
        kernel,
        out_shape=out_shape,
        in_specs=[smem()] * len(scalars) + [(inputs or vmem)()] * len(arrays),
        out_specs=out_specs,
        scratch_shapes=list(scratch),
        cost_estimate=pl.CostEstimate(flops=flops, bytes_accessed=10**6, transcendentals=0),
        compiler_params=pltpu.CompilerParams(vmem_limit_bytes=limit),
    )(*scalars, *arrays)


def anywhere():
    return pl.BlockSpec(memory_space=pltpu.HBM)


def landing(arrays):
    return [pltpu.VMEM(a.shape, a.dtype) for a in arrays] + [pltpu.SemaphoreType.DMA((len(arrays),))]


def weight_shapes():
    return [
        jax.ShapeDtypeStruct((8 * HIDDEN, LANES), BF16),
        jax.ShapeDtypeStruct((32, HIDDEN), BF16),
        jax.ShapeDtypeStruct((16, LANES), BF16),
        tiles(16),
        tiles(HIDDEN),
        jax.ShapeDtypeStruct((LANES, SLOTS * 2 * LANES), BF16),
        tiles(HIDDEN),
        jax.ShapeDtypeStruct((HIDDEN, N_BASIS), BF16),
        jax.ShapeDtypeStruct((HIDDEN, HIDDEN), BF16),
        jax.ShapeDtypeStruct((HIDDEN, HIDDEN), BF16),
    ]


def begin_shapes(arrays):
    through = [jax.ShapeDtypeStruct(arrays[k].shape, arrays[k].dtype) for k in (5, 6, 7, 2, 10)]
    space = landing([arrays[k] for k in (0, 1, 3, 4, 8, 9, 11, 12)])
    space[3] = pltpu.SMEM(arrays[4].shape, F32)
    space[-1] = pltpu.SemaphoreType.DMA((len(arrays),))
    made = [tiles(24)] + weight_shapes() + through
    return made, space


def force_scratch():
    return [
        pltpu.VMEM((GROUPS, 128, 2 * LANES), BF16),
        pltpu.VMEM((GROUPS, 64, 2 * LANES), F32),
        pltpu.VMEM((6, GROUPS, 8, 2 * LANES), F32),
        pltpu.VMEM((GROUPS, 8, 2 * LANES), F32),
        pltpu.VMEM((GROUPS * 64, LANES), F32),
        pltpu.VMEM((GROUPS * 64, LANES), F32),
    ] + [pltpu.VMEM((8 * 24, LANES), F32)] * (2 * GROUPS) + [pltpu.VMEM((AHEAD * HIDDEN, 2 * LANES), F32)]


def on_chip(value, domains):
    groups = [[2 * i, 2 * i + 1] for i in range(domains // 2)]
    return lax.all_gather(value, "space", axis_index_groups=groups)


def across_chips(value, domains):
    groups = []
    for i in range(domains // 4):
        groups += [[4 * i, 4 * i + 2], [4 * i + 3, (4 * i + 5) % domains]]
    return lax.all_gather(value, "space", axis_index_groups=groups)


def in_pair(value, domains):
    groups = [[4 * i + k for k in range(4)] for i in range(domains // 4)]
    whole = lax.all_gather(value, "space", axis_index_groups=groups)
    return whole.reshape((2, 2) + value.shape)


def between_pairs(value, domains):
    groups = []
    for i in range(0, domains // 4, 2):
        for chip in range(2):
            first = 4 * i + 2 * chip
            groups += [[first, first + 4], [first + 5, (first + 9) % domains]]
    return lax.all_gather(value, "space", axis_index_groups=groups)


def even_odd_core(rank, rungs):
    far = (rank % 4 == 0) | (rank % 4 == 3)
    return 1 - (far & (rank > 0) & (rank < rungs - 1))


def along_ladder(value, rungs, domains):
    groups = []
    for chip in range(0, domains, 2):
        for low in range(rungs - 1):
            pair = []
            for rank in (low, low + 1):
                core = even_odd_core(rank, rungs)
                pair.append(rank * domains + chip + (core if low % 2 == 0 else 1 - core))
            groups.append(pair)
        if chip % 4 == 0:
            for end in (0, rungs - 1):
                groups.append([end * domains + chip, end * domains + chip + 2])
    return lax.all_gather(value, ("replica", "space"), axis_index_groups=groups)


def on_device(
    particle_coordinates,
    particle_motions,
    particle_kinds,
    filled_totals,
    adjacent_particles,
    adjacent_place_kinds,
    border_particle_numbers,
    reciprocal_kind_inertia,
    thermal_levels,
    swap_mates,
    bond_intake_coefficients,
    bond_output_coefficients,
    particle_opening_coefficients,
    particle_middle_coefficients,
    particle_output_coefficients,
):
    domains, rungs = lax.axis_size("space"), lax.axis_size("replica")
    core = lax.axis_index("space") % 2
    rank = lax.axis_index("replica")
    mate = swap_mates[0]
    odd = rank % 2
    even_odd = (mate > rank) == (odd == 0)
    side = even_odd_core(rank, rungs)
    side = jnp.where(even_odd, side, 1 - side)
    position = jnp.where(even_odd, 1 - odd, odd)
    where_to = [value.astype(F32) for value in (core, mate != rank, side, position)]
    here = lax.axis_index("space")
    chip, pair = (here // 2 % 2).astype(F32), (here // 4 % 2).astype(F32)
    where_to = jnp.stack(where_to + [thermal_levels[0], chip, pair])
    where_to = jnp.broadcast_to(where_to[:, None], (7, LANES))

    arrays = (
        particle_coordinates.reshape(1, -1),
        particle_motions.reshape(1, -1),
        particle_kinds,
        border_particle_numbers,
        reciprocal_kind_inertia,
        adjacent_particles,
        adjacent_place_kinds,
        filled_totals,
        bond_intake_coefficients.T,
        bond_output_coefficients[None],
        particle_opening_coefficients.T,
        particle_middle_coefficients,
        particle_output_coefficients[None],
    )
    arrays = tuple(pltpu.with_memory_space_constraint(a, pltpu.HBM) for a in arrays)
    made, space = begin_shapes(arrays)
    begin, *fixed = call(begin_kernel, (), arrays, made, space, inputs=anywhere)
    home = on_chip(begin, domains)
    far = on_chip(across_chips(home, domains), domains)
    for step in range(STEPS):
        partial = call(force_kernel, (), (where_to, home, far, *fixed), tiles(16), force_scratch())
        if step < STEPS - 1:
            pair = in_pair(partial, domains)
            wide = on_chip(between_pairs(pair, domains), domains)
            shapes = [tiles(2, 24), tiles(4, 8)]
            home, far = call(step_kernel, (), (where_to, home, far, wide), shapes)
        else:
            near = on_chip(partial, domains)
            far = on_chip(across_chips(near[:, GHOSTS], domains), domains)
            state = call(last_kernel, (), (where_to, home, near, far), tiles(2, 16))
    mates = on_chip(along_ladder(state, rungs, domains), domains)
    shape = particle_coordinates.shape
    out = jax.ShapeDtypeStruct((1, particle_coordinates.size), F32)
    scratch = landing((out, out))
    new_x, new_v = call(
        swap_kernel, (), (where_to, state, mates), [out, out], scratch, outputs=anywhere
    )
    return new_x.reshape(shape), new_v.reshape(shape)


def solution(mesh):
    return jax.shard_map(
        on_device,
        mesh=mesh,
        in_specs=(
            P("replica", None, "space"),
            P("replica", None, "space"),
            P("replica", "space"),
            P("replica", "space"),
            P("replica", None, "space"),
            P("replica", None, "space"),
            P("replica", None, "space"),
            P(),
            P("replica"),
            P("replica"),
            P(),
            P(),
            P(),
            P(),
            P(),
        ),
        out_specs=(P("replica", None, "space"), P("replica", None, "space")),
        check_vma=False,
    )
```
